32 devices in a mesh: group: 2 (over x), seq: 16 (over z, y, core).
Axes of the slice: x: 2, y: 2, z: 4, core: 2. Of those that a mesh axis runs over, the one named last changes fastest.
Arguments:
- x_rows: bfloat16 [32, 8192], P('group', 'seq'), parts along dimension 0, may hold values from -0.59765625 to 0.59765625
- attn_gain: bfloat16 [8192], replicated, may hold values from 0.5 to 1.5
- q_weight: bfloat16 [8192, 8192], P(None, 'seq'), may hold values from -0.0625 to 0.0625
- o_weight: bfloat16 [8192, 8192], P('seq'), may hold values from -0.0625 to 0.0625
- mlp_gain: bfloat16 [8192], replicated, may hold values from 0.5 to 1.5
- gate_weight: bfloat16 [8192, 14336], P(None, 'seq'), may hold values from -0.0625 to 0.0625
- up_weight: bfloat16 [8192, 14336], P(None, 'seq'), may hold values from -0.0625 to 0.0625
- down_weight: bfloat16 [14336, 8192], P('seq'), may hold values from -0.046875 to 0.046875
- kv_cache: bfloat16 [2, 4096, 1024], P(None, ('group', 'seq')), parts along dimension 1, may hold values from -250 to 250, as said below
- block_mask: int32 [32, 8, 16], P('group', None, 'seq'), parts along dimension 0, may hold values from 0 to 1, as said below
Outputs:
- y_rows: bfloat16 [32, 8192], P('group', 'seq'), parts along dimension 0
The draws below stay inside these ranges and needn't reach their ends.
There are 2 independent parts, one for each index of `group`. The reference program is written for one: setup_inputs(seed, part) draws one part's arguments, and reference() takes and returns one part's arrays. A program takes and returns all parts, laid end to end along the dimension named above; an argument that names none is the same for every part. Nothing has to cross between parts.
Inputs may be any that keep to these rules, and one draw needn't show every extreme that they name: `kv_cache`: document keys and values; they differ from document to document. `block_mask`: 1 where the row may attend to that block of 128 document tokens for that key-value head, else 0; the document's last block is 1 for every row and key-value head.
All inputs are finite; a program needn't handle non-finite values.
Results may differ from the reference program's by a relative error of at most 0.013.
The reference program's roundings to bfloat16 on the way (of `normed`, `queries`, `attended`, `stream`, `normed_two` and `hidden`) count: a program that leaves them out, or rounds other values in their place, can miss the bound.
Values may be sent and summed in bfloat16 or wider, within the bound.
No kernel may reach another device: no remote copies, remote signals or barrier semaphores. Data moves between devices by JAX's collectives and lax.ppermute only.
A program may use at most 192 MiB of HBM per device.

```python
import jax
import jax.numpy as jnp
from jax import lax

D = 8192
HEADS = 64
KV_HEADS = 8
HEAD_DIM = 128
FF_WIN = 14336
BLOCK = 128
ROWS = 16
KV_DEV = 128
DOC = 2048
NBLK = 16
N_SEQ = 16


def draw_kv_cache(key, part):
    width = KV_HEADS * HEAD_DIM
    keys = 1.5 * jnp.clip(jax.random.normal(jax.random.fold_in(key, 21), (DOC, width), jnp.float32), -4.0, 4.0)
    values = 4.0 * jnp.clip(jax.random.normal(jax.random.fold_in(key, 22), (DOC, width), jnp.float32), -4.0, 4.0)
    return jnp.stack([keys, values]).astype(jnp.bfloat16)


def draw_block_mask(key, part):
    position = jnp.arange(NBLK, dtype=jnp.int32)
    limit = 150 + 800 * position * position // (NBLK * NBLK)
    rolled = jax.random.randint(jax.random.fold_in(key, 31), (ROWS, KV_HEADS, NBLK), 0, 1000, jnp.int32)
    drawn = (rolled < limit[None, None, :]).astype(jnp.int32)
    last = (position == NBLK - 1)[None, None, :]
    return jnp.where(last, 1, drawn).astype(jnp.int32)


def levels(rng, extent, shards, low, high):
    loudness, own = 1.0, jax.random.fold_in(rng, 6)
    for axis_at, parts in shards:
        draws = jnp.exp(jax.random.uniform(jax.random.fold_in(own, axis_at), (parts,), jnp.float32, low / len(shards), high / len(shards)))
        loudness = loudness * jnp.repeat(draws, extent[axis_at] // parts).reshape([-1 if axis == axis_at else 1 for axis in range(len(extent))])
    return loudness


def gaussian(rng, dims, deviation, bound, split=(), kind=jnp.bfloat16):
    level = levels(rng, dims, split, -0.22, 0.18) if split else 1.0
    result = jax.random.normal(rng, dims, jnp.float32) * deviation * level
    return jnp.minimum(jnp.maximum(result, -bound), bound).astype(kind)


def setup_inputs(seed: int = 0, part: int = 0) -> dict:
    key_of = jax.random.split(jax.random.key(seed), 11)
    part_splits = jax.random.split(jax.random.fold_in(key_of[10], part), 11)
    return {
        "x_rows": gaussian(part_splits[0], (ROWS, D), 0.1, 0.59765625, ((1, 16),)),
        "attn_gain": jnp.clip(1.0 + 0.1 * jax.random.normal(key_of[1], (D,), jnp.float32), 0.5, 1.5).astype(jnp.bfloat16),
        "q_weight": gaussian(key_of[2], (D, HEADS * HEAD_DIM), D ** -0.5, 0.0625, ((1, 16),)),
        "o_weight": gaussian(key_of[3], (HEADS * HEAD_DIM, D), (HEADS * HEAD_DIM) ** -0.5, 0.0625, ((0, 16),)),
        "mlp_gain": jnp.clip(1.0 + 0.1 * jax.random.normal(key_of[4], (D,), jnp.float32), 0.5, 1.5).astype(jnp.bfloat16),
        "gate_weight": gaussian(key_of[5], (D, FF_WIN), D ** -0.5, 0.0625, ((1, 16),)),
        "up_weight": gaussian(key_of[6], (D, FF_WIN), D ** -0.5, 0.0625, ((1, 16),)),
        "down_weight": gaussian(key_of[7], (FF_WIN, D), FF_WIN ** -0.5, 0.046875, ((0, 16),)),
        "kv_cache": draw_kv_cache(jax.random.fold_in(jax.random.fold_in(key_of[10], part), 71), part),
        "block_mask": draw_block_mask(jax.random.fold_in(jax.random.fold_in(key_of[10], part), 71), part),
    }


eps = 1e-05
floor_score = -1e+30

def rms_norm(values, gain):
    wide = values.astype(jnp.float32)
    inverse = lax.rsqrt(lax.optimization_barrier(jnp.mean(wide * wide, axis=-1, keepdims=True)) + eps)
    return (wide * inverse * gain.astype(jnp.float32)).astype(jnp.bfloat16)

def reference(x_rows, attn_gain, q_weight, o_weight, mlp_gain, gate_weight, up_weight, down_weight, kv_cache, block_mask):
    rows = x_rows.shape[0]
    group = HEADS // KV_HEADS
    spans = KV_DEV // BLOCK
    scale = 1.0 / HEAD_DIM ** 0.5
    normed = rms_norm(x_rows, attn_gain)
    queries = jnp.dot(normed, q_weight, preferred_element_type=jnp.float32).astype(jnp.bfloat16)
    query_wide = queries.reshape(rows, KV_HEADS, group, HEAD_DIM).astype(jnp.float32)
    doc_keys = kv_cache[0]
    doc_values = kv_cache[1]

    def one_span(carry, index):
        top, total, accum = carry
        start = (index * KV_DEV).astype(jnp.int32)
        span_keys = lax.dynamic_slice_in_dim(doc_keys, start, KV_DEV, 0).reshape(KV_DEV, KV_HEADS, HEAD_DIM).astype(jnp.float32)
        span_values = lax.dynamic_slice_in_dim(doc_values, start, KV_DEV, 0).reshape(KV_DEV, KV_HEADS, HEAD_DIM).astype(jnp.float32)
        span_mask = lax.dynamic_slice_in_dim(block_mask, (index * spans).astype(jnp.int32), spans, 2)
        scores = jnp.einsum('rghd,kgd->rghk', query_wide, span_keys) * scale
        scores = scores.reshape(rows, KV_HEADS, group, spans, BLOCK)
        live = (span_mask == 1)[:, :, None, :, None]
        masked = jnp.where(live, scores, floor_score)
        local_top = lax.optimization_barrier(jnp.max(masked, axis=(3, 4)))
        weights = jnp.where(live, jnp.exp(masked - local_top[..., None, None]), 0.0)
        local_total = lax.optimization_barrier(jnp.sum(weights, axis=(3, 4)))
        rounded = lax.optimization_barrier(weights.astype(jnp.bfloat16)).astype(jnp.float32)
        rounded = rounded.reshape(rows, KV_HEADS, group, KV_DEV)
        local_accum = jnp.einsum('rghk,kgd->rghd', rounded, span_values)
        new_top = jnp.maximum(top, local_top)
        old_factor = jnp.exp(top - new_top)
        new_factor = jnp.exp(local_top - new_top)
        total = total * old_factor + local_total * new_factor
        accum = accum * old_factor[..., None] + local_accum * new_factor[..., None]
        return ((new_top, total, accum), None)
    init = (jnp.full((rows, KV_HEADS, group), floor_score, jnp.float32), jnp.zeros((rows, KV_HEADS, group), jnp.float32), jnp.zeros((rows, KV_HEADS, group, HEAD_DIM), jnp.float32))
    (top, total, accum), _ = lax.scan(one_span, init, jnp.arange(N_SEQ, dtype=jnp.int32))
    attended = accum / total[..., None]
    attended = attended.reshape(rows, HEADS * HEAD_DIM).astype(jnp.bfloat16)
    stream = (x_rows.astype(jnp.float32) + jnp.dot(attended, o_weight, preferred_element_type=jnp.float32)).astype(jnp.bfloat16)
    normed_two = rms_norm(stream, mlp_gain)
    gate = jnp.dot(normed_two, gate_weight, preferred_element_type=jnp.float32)
    upward = jnp.dot(normed_two, up_weight, preferred_element_type=jnp.float32)
    hidden = (jax.nn.silu(gate) * upward).astype(jnp.bfloat16)
    return (stream.astype(jnp.float32) + jnp.dot(hidden, down_weight, preferred_element_type=jnp.float32)).astype(jnp.bfloat16)
```

```python
import functools

import jax
import jax.numpy as jnp
from jax import lax
from jax.experimental import pallas as pl
from jax.experimental.pallas import tpu as pltpu
from jax.sharding import PartitionSpec as P

HEADS = 64
KV_HEADS = 8
HEAD_DIM = 128
BLOCK = 128
QUAD = 4

eps = 1e-05
floor_score = -1e30

bf16 = jnp.bfloat16
f32 = jnp.float32
VMEM = pl.BlockSpec(memory_space=pltpu.VMEM)


def call(body, outs, ins, scratch=(), limit=16 * 2**20, cost=None):
    return pl.pallas_call(
        body,
        out_shape=outs,
        in_specs=[VMEM] * len(ins),
        out_specs=jax.tree.map(lambda _: VMEM, outs),
        scratch_shapes=list(scratch),
        compiler_params=pltpu.CompilerParams(vmem_limit_bytes=limit),
        cost_estimate=cost,
    )(*ins)


def like(shape, dtype):
    return jax.ShapeDtypeStruct(shape, dtype)


def swap(x, distance):
    size = lax.axis_size("seq")
    return lax.ppermute(x, "seq", [(i, i ^ distance) for i in range(size)])


def pack_kernel(outer, kv_ref, mask_ref, *out_refs):
    quad = lax.axis_index("seq") // QUAD
    keys = kv_ref.shape[1]
    rows = mask_ref.shape[0]
    wide = kv_ref.shape[2] // outer
    mask = mask_ref[...]
    lane = lax.broadcasted_iota(jnp.int32, mask.shape, 1)
    for k in range(outer):
        peer = jnp.bitwise_xor(quad, k)
        cols = pl.ds(pl.multiple_of(peer * wide, wide), wide)
        out = out_refs[k]
        out[0:keys, :] = kv_ref[0, :, cols]
        out[keys : 2 * keys, :] = kv_ref[1, :, cols]
        for h in range(wide // HEAD_DIM):
            head = peer * (wide // HEAD_DIM) + h
            live = jnp.sum(
                jnp.where((lane == head) & (mask == 1), 1.0, 0.0).astype(f32), axis=1, keepdims=True
            )
            out[2 * keys : 2 * keys + rows, h * HEAD_DIM : (h + 1) * HEAD_DIM] = jnp.broadcast_to(
                live, (rows, HEAD_DIM)
            ).astype(bf16)


def split_kernel(outer, *refs):
    ins, (mine, other) = refs[:outer], refs[outer:]
    high = (lax.axis_index("seq") // 2) % 2
    size = ins[0].shape[0]
    for k in range(outer):
        span = pl.ds(k * size, size)
        mine[span, :] = ins[k][:, pl.ds(pl.multiple_of(high * HEAD_DIM, HEAD_DIM), HEAD_DIM)]
        other[span, :] = ins[k][:, pl.ds(pl.multiple_of((1 - high) * HEAD_DIM, HEAD_DIM), HEAD_DIM)]


def normed_chunks(outer, wide, part_refs, gain_ref):
    me = lax.axis_index("seq")
    width = QUAD * outer * wide
    squares = None
    for ref in part_refs:
        v = ref[...].astype(f32)
        s = jnp.sum(v * v, axis=1, keepdims=True)
        squares = s if squares is None else squares + s
    inverse = lax.rsqrt(squares / width + eps)
    for j in range(QUAD):
        for k in range(outer):
            source = jnp.bitwise_xor(me, QUAD * k + j)
            at = pl.ds(pl.multiple_of(source * wide, wide), wide)
            v = part_refs[j][:, k * wide : (k + 1) * wide].astype(f32)
            yield at, (v * inverse * gain_ref[:, at].astype(f32)).astype(bf16)


def query_kernel(outer, wide, *refs):
    parts, gain_ref, w_ref, out_ref = refs[:QUAD], refs[QUAD], refs[QUAD + 1], refs[QUAD + 2]
    total = None
    for at, chunk in normed_chunks(outer, wide, parts, gain_ref):
        term = jnp.dot(chunk, w_ref[at, :], preferred_element_type=f32)
        total = term if total is None else total + term
    out_ref[...] = total.astype(bf16)


def scatter_dot(outer, wide, left, w_ref, out_refs):
    me = lax.axis_index("seq")
    for j in (3, 2, 1, 0):
        for k in range(outer):
            target = jnp.bitwise_xor(me, QUAD * k + j)
            at = pl.ds(pl.multiple_of(target * wide, wide), wide)
            term = jnp.dot(left, w_ref[:, at], preferred_element_type=f32)
            out_refs[j][:, k * wide : (k + 1) * wide] = term.astype(out_refs[j].dtype)


def attend_kernel(outer, wide, q_ref, *refs):
    cache, w_ref, outs = refs[:QUAD], refs[QUAD], refs[QUAD + 1 :]
    rows = q_ref.shape[0]
    heads = q_ref.shape[1] // HEAD_DIM
    scale = 1.0 / HEAD_DIM**0.5
    size = cache[0].shape[0] // outer
    keys = (size - rows) // 2
    queries = jnp.concatenate(
        [q_ref[:, h * HEAD_DIM : (h + 1) * HEAD_DIM] for h in range(heads)], axis=0
    )
    states = []
    for ref in cache:
        for k in range(outer):
            at = k * size
            live = ref[at + 2 * keys : at + size, :].astype(f32) > 0.5
            live = jnp.concatenate([live.astype(f32)] * heads, axis=0) > 0.5
            score = (
                lax.dot_general(
                    queries,
                    ref[at : at + keys, :],
                    (((1,), (1,)), ((), ())),
                    preferred_element_type=f32,
                )
                * scale
            )
            masked = jnp.where(live, score, floor_score)
            top = jnp.max(masked, axis=1, keepdims=True)
            weight = jnp.where(live, jnp.exp(masked - top), 0.0)
            total = jnp.sum(weight, axis=1, keepdims=True)
            accum = jnp.dot(
                weight.astype(bf16), ref[at + keys : at + 2 * keys, :], preferred_element_type=f32
            )
            states.append((top, total, accum))
    top = functools.reduce(jnp.maximum, [s[0] for s in states])
    total = accum = None
    for t, s, a in states:
        factor = jnp.exp(t - top)
        total = s * factor if total is None else total + s * factor
        accum = a * factor if accum is None else accum + a * factor
    attended = (accum / total).astype(bf16)
    attended = jnp.concatenate([attended[h * rows : (h + 1) * rows] for h in range(heads)], axis=1)
    scatter_dot(outer, wide, attended, w_ref, outs)


def hidden_kernel(outer, wide, *refs):
    parts, gain_ref = refs[:QUAD], refs[QUAD]
    gate_ref, up_ref, down_ref = refs[QUAD + 1 : QUAD + 4]
    outs = refs[QUAD + 4 :]
    gate = up = None
    for at, chunk in normed_chunks(outer, wide, parts, gain_ref):
        g = jnp.dot(chunk, gate_ref[at, :], preferred_element_type=f32)
        u = jnp.dot(chunk, up_ref[at, :], preferred_element_type=f32)
        gate = g if gate is None else gate + g
        up = u if up is None else up + u
    hidden = (gate / (1.0 + jnp.exp(-gate)) * up).astype(bf16)
    scatter_dot(outer, wide, hidden, down_ref, outs)


def fold_kernel(outer, wide, own_ref, *refs):
    recv, keep_ref, sends = refs[: QUAD - 1], refs[QUAD - 1], refs[QUAD:]
    for k in range(outer):
        at = slice(k * wide, (k + 1) * wide)
        total = own_ref[:, at]
        for r in recv:
            total = total + r[:, at].astype(f32)
        if k == 0:
            keep_ref[...] = total
        else:
            sends[k - 1][...] = total.astype(bf16)


def final_kernel(base_ref, keep_ref, *refs):
    total = keep_ref[...]
    for r in refs[:-1]:
        total = total + r[...].astype(f32)
    refs[-1][...] = (base_ref[...].astype(f32) + total).astype(bf16)


def gathered(x, outer):
    line = jnp.concatenate([x] + [swap(x, QUAD * k) for k in range(1, outer)], axis=1)
    return [line] + [swap(line, j) for j in range(1, QUAD)]


def scattered(base, partials, outer, wide):
    rows = base.shape[0]
    recv = [swap(partials[j], j) for j in range(1, QUAD)]
    outs = [like((rows, wide), f32)] + [like((rows, wide), bf16)] * (outer - 1)
    keep, *sends = call(
        functools.partial(fold_kernel, outer, wide), outs, [partials[0], *recv]
    )
    arrived = [swap(s, QUAD * (k + 1)) for k, s in enumerate(sends)]
    return call(final_kernel, like((rows, wide), bf16), [base, keep, *arrived])


def local_pairs(
    x_rows, attn_gain, q_weight, o_weight, mlp_gain, gate_weight, up_weight, down_weight, kv_cache, block_mask
):
    rows, wide = x_rows.shape
    outer = lax.axis_size("seq") // QUAD
    columns = q_weight.shape[1]
    attn_gain = attn_gain.reshape(1, -1)
    mlp_gain = mlp_gain.reshape(1, -1)
    x_parts = gathered(x_rows, outer)

    size = 2 * kv_cache.shape[1] + rows
    across = kv_cache.shape[2] // outer
    packed = call(
        functools.partial(pack_kernel, outer),
        [like((size, across), bf16)] * outer,
        [kv_cache, block_mask[:, :, 0]],
    )
    line = [packed[0]] + [swap(packed[k], QUAD * k) for k in range(1, outer)]
    mine, other = call(
        functools.partial(split_kernel, outer), [like((size * outer, HEAD_DIM), bf16)] * 2, line
    )
    across_y = swap(other, 2)
    cache = [mine, across_y, swap(mine, 1), swap(across_y, 1)]

    queries = call(
        functools.partial(query_kernel, outer, wide),
        like((rows, columns), bf16),
        [*x_parts, attn_gain, q_weight],
    )
    partial_outs = [like((rows, outer * wide), f32)] + [like((rows, outer * wide), bf16)] * (QUAD - 1)
    partials = call(
        functools.partial(attend_kernel, outer, wide), partial_outs, [queries, *cache, o_weight]
    )
    stream = scattered(x_rows, partials, outer, wide)
    stream_parts = gathered(stream, outer)
    partials = call(
        functools.partial(hidden_kernel, outer, wide),
        partial_outs,
        [*stream_parts, mlp_gain, gate_weight, up_weight, down_weight],
    )
    return scattered(stream, partials, outer, wide)


def rms_norm(values, gain):
    wide = values.astype(f32)
    inverse = lax.rsqrt(jnp.mean(wide * wide, axis=-1, keepdims=True) + eps)
    return (wide * inverse * gain.astype(f32)).astype(bf16)


def combine_states(first, second):
    top_a, total_a, accum_a = first
    top_b, total_b, accum_b = second
    top = jnp.maximum(top_a, top_b)
    factor_a = jnp.exp(top_a - top)
    factor_b = jnp.exp(top_b - top)
    return (
        top,
        total_a * factor_a + total_b * factor_b,
        accum_a * factor_a[..., None] + accum_b * factor_b[..., None],
    )


def combined_all(x, axis, combine):
    everything = jax.tree.map(lambda part: lax.all_gather(part, axis), x)
    initial = jax.tree.map(lambda part: part[0], everything)

    def turn(k, so_far):
        return combine(so_far, jax.tree.map(lambda part: part[k], everything))

    return lax.fori_loop(1, lax.axis_size(axis), turn, initial)


def summed(weight, left):
    product = lax.dot_general(weight, left, (((0,), (1,)), ((), ())), preferred_element_type=f32)
    return lax.psum_scatter(product, "seq", scatter_dimension=0, tiled=True).T


def local_tokens(
    x_rows, attn_gain, q_weight, o_weight, mlp_gain, gate_weight, up_weight, down_weight, kv_cache, block_mask
):
    rows = x_rows.shape[0]
    group = HEADS // KV_HEADS
    key_len = kv_cache.shape[1]
    spans = key_len // BLOCK
    scale = 1.0 / HEAD_DIM**0.5
    normed = rms_norm(lax.all_gather(x_rows, "seq", axis=1, tiled=True), attn_gain)
    query_part = jnp.dot(normed, q_weight, preferred_element_type=f32).astype(bf16)
    queries = lax.all_gather(query_part, "seq", axis=1, tiled=True)

    def one_group(index):
        def cut(array, width):
            return lax.dynamic_slice_in_dim(array, index * width, width, 1)

        query_group = cut(queries, group * HEAD_DIM).reshape(rows, group, HEAD_DIM)
        scores = (
            jnp.einsum("rhd,kd->rhk", query_group, cut(kv_cache[0], HEAD_DIM), preferred_element_type=f32)
            * scale
        )
        scores = scores.reshape(rows, group, spans, BLOCK)
        live = (cut(block_mask, 1)[:, 0, :] == 1)[:, None, :, None]
        masked = jnp.where(live, scores, floor_score)
        top = jnp.max(masked, axis=(2, 3))
        weights = jnp.where(live, jnp.exp(masked - top[..., None, None]), 0.0)
        rounded = weights.astype(bf16).reshape(rows, group, key_len)
        accum = jnp.einsum("rhk,kd->rhd", rounded, cut(kv_cache[1], HEAD_DIM), preferred_element_type=f32)
        return (top, jnp.sum(weights, axis=(2, 3)), accum)

    states = lax.map(one_group, jnp.arange(KV_HEADS, dtype=jnp.int32))
    states = jax.tree.map(lambda part: jnp.moveaxis(part, 0, 1), states)
    columns = q_weight.shape[1]
    top, total, accum = combined_all(states, "seq", combine_states)
    attended = (accum / total[..., None]).reshape(rows, HEADS * HEAD_DIM).astype(bf16)
    attn_cols = lax.dynamic_slice_in_dim(attended, lax.axis_index("seq") * columns, columns, 1)
    stream = (x_rows.astype(f32) + summed(o_weight, attn_cols)).astype(bf16)
    normed_two = rms_norm(lax.all_gather(stream, "seq", axis=1, tiled=True), mlp_gain)
    gate = jnp.dot(normed_two, gate_weight, preferred_element_type=f32)
    upward = jnp.dot(normed_two, up_weight, preferred_element_type=f32)
    hidden = (jax.nn.silu(gate) * upward).astype(bf16)
    return (stream.astype(f32) + summed(down_weight, hidden)).astype(bf16)


def solution(mesh):
    pairs = mesh.shape["seq"] == 2 * KV_HEADS
    return jax.shard_map(
        local_pairs if pairs else local_tokens,
        mesh=mesh,
        in_specs=(
            P("group", "seq"),
            P(),
            P(None, "seq"),
            P("seq", None),
            P(),
            P(None, "seq"),
            P(None, "seq"),
            P("seq", None),
            P(None, ("group", "seq"), None),
            P("group", None, "seq"),
        ),
        out_specs=P("group", "seq"),
        check_vma=False,
    )
```

```python
import functools

import jax
import jax.numpy as jnp
from jax import lax
from jax.experimental import pallas as pl
from jax.experimental.pallas import tpu as pltpu
from jax.sharding import PartitionSpec as P

HEADS = 64
KV_HEADS = 8
HEAD_DIM = 128
BLOCK = 128
QUAD = 4

eps = 1e-05
floor_score = -1e30

bf16 = jnp.bfloat16
f32 = jnp.float32
VMEM = pl.BlockSpec(memory_space=pltpu.VMEM)


def call(body, outs, ins, beside=(), limit=4 * 2**20):
    count, extra = len(ins), len(beside)

    def kernel(*refs):
        body(*refs[:count], *refs[count + extra :])

    return pl.pallas_call(
        kernel,
        out_shape=outs,
        in_specs=[VMEM] * count + [pl.BlockSpec(memory_space=pl.ANY)] * extra,
        out_specs=jax.tree.map(lambda _: VMEM, outs),
        compiler_params=pltpu.CompilerParams(vmem_limit_bytes=limit),
    )(*ins, *beside)


def room(size):
    return pl.pallas_call(
        lambda out: None,
        out_shape=like((size, 1024), f32),
        out_specs=pl.BlockSpec(memory_space=pl.ANY),
    )()


def like(shape, dtype):
    return jax.ShapeDtypeStruct(shape, dtype)


def swap(x, distance):
    size = lax.axis_size("seq")
    return lax.ppermute(x, "seq", [(i, i ^ distance) for i in range(size)])


def live_lanes(mask, head, rows):
    lane = lax.broadcasted_iota(jnp.int32, mask.shape, 1)
    live = jnp.where((lane == head) & (mask == 1), 1.0, 0.0).astype(f32)
    return jnp.broadcast_to(jnp.sum(live, axis=1, keepdims=True), (rows, HEAD_DIM)).astype(bf16)


def pack_kernel(outer, kv_ref, mask_ref, own_ref, send_ref):
    y = (lax.axis_index("seq") // 2) % 2
    keys = kv_ref.shape[1]
    rows = mask_ref.shape[0]
    mask = mask_ref[...]
    for out, parity in ((send_ref, 1 - y), (own_ref, y)):
        for z in range(outer):
            head = 2 * z + parity
            cols = pl.ds(pl.multiple_of(head * HEAD_DIM, HEAD_DIM), HEAD_DIM)
            at = slice(z * HEAD_DIM, (z + 1) * HEAD_DIM)
            out[0:keys, at] = kv_ref[0, :, cols]
            out[keys : 2 * keys, at] = kv_ref[1, :, cols]
            out[2 * keys : 2 * keys + rows, at] = live_lanes(mask, head, rows)


def route_kernel(outer, own_ref, other_ref, order_ref, *outs):
    z = lax.axis_index("seq") // QUAD
    size = own_ref.shape[0]
    for k in range(outer):
        peer = jnp.bitwise_xor(z, k)
        cols = pl.ds(pl.multiple_of(peer * HEAD_DIM, HEAD_DIM), HEAD_DIM)
        outs[k][0:size, :] = own_ref[:, cols]
        outs[k][size : 2 * size, :] = other_ref[:, cols]


def stack_kernel(axis, *refs):
    at = 0
    for ref in refs[:-1]:
        size = ref.shape[axis]
        if axis == 0:
            refs[-1][at : at + size, :] = ref[...]
        else:
            refs[-1][:, at : at + size] = ref[...]
        at += size


def stacked(parts, axis, beside=()):
    shape = list(parts[0].shape)
    shape[axis] = sum(p.shape[axis] for p in parts)
    return call(functools.partial(stack_kernel, axis), like(tuple(shape), parts[0].dtype), parts, beside)


def normed_chunks(outer, wide, part_refs, gain_ref):
    me = lax.axis_index("seq")
    width = QUAD * outer * wide
    squares = None
    for ref, _ in part_refs:
        v = ref[...].astype(f32)
        s = jnp.sum(v * v, axis=1, keepdims=True)
        squares = s if squares is None else squares + s
    inverse = lax.rsqrt(squares / width + eps)
    for ref, distances in part_refs:
        for i, distance in enumerate(distances):
            source = jnp.bitwise_xor(me, distance)
            at = pl.ds(pl.multiple_of(source * wide, wide), wide)
            v = ref[:, i * wide : (i + 1) * wide].astype(f32)
            yield at, (v * inverse * gain_ref[:, at].astype(f32)).astype(bf16)


def line_of(outer, *nears):
    return [QUAD * k + j for j in nears for k in range(outer)]


def part_list(outer, refs):
    return list(zip(refs, (line_of(outer, 0), line_of(outer, 2), line_of(outer, 1, 3))))


def query_kernel(outer, wide, *refs):
    gain_ref, w_ref, out_ref = refs[3:]
    total = None
    for at, chunk in normed_chunks(outer, wide, part_list(outer, refs[:3]), gain_ref):
        term = jnp.dot(chunk, w_ref[at, :], preferred_element_type=f32)
        total = term if total is None else total + term
    out_ref[...] = total.astype(bf16)


def scatter_dot(wide, left, w_ref, out_ref, distances):
    me = lax.axis_index("seq")
    for i, distance in enumerate(distances):
        target = jnp.bitwise_xor(me, distance)
        at = pl.ds(pl.multiple_of(target * wide, wide), wide)
        out_ref[:, i * wide : (i + 1) * wide] = jnp.dot(left, w_ref[:, at], preferred_element_type=f32)


def scatter_kernel(wide, distances, left_ref, w_ref, out_ref):
    scatter_dot(wide, left_ref[...], w_ref, out_ref, distances)


def attend_kernel(wide, distances, spans, q_ref, *refs):
    cache, w_ref, left_ref, send_ref = refs[:-3], *refs[-3:]
    rows = q_ref.shape[0]
    heads = q_ref.shape[1] // HEAD_DIM
    scale = 1.0 / HEAD_DIM**0.5
    queries = jnp.concatenate(
        [q_ref[:, h * HEAD_DIM : (h + 1) * HEAD_DIM] for h in range(heads)], axis=0
    )
    states = []
    for ref, count in zip(cache, spans):
        size = ref.shape[0] // count
        keys = (size - rows) // 2
        for k in range(count):
            at = k * size
            live = ref[at + 2 * keys : at + size, :].astype(f32)
            live = jnp.concatenate([live] * heads, axis=0) > 0.5
            score = (
                lax.dot_general(
                    queries,
                    ref[at : at + keys, :],
                    (((1,), (1,)), ((), ())),
                    preferred_element_type=f32,
                )
                * scale
            )
            masked = jnp.where(live, score, floor_score)
            top = jnp.max(masked, axis=1, keepdims=True)
            weight = jnp.where(live, jnp.exp(masked - top), 0.0)
            total = jnp.sum(weight, axis=1, keepdims=True)
            accum = jnp.dot(
                weight.astype(bf16), ref[at + keys : at + 2 * keys, :], preferred_element_type=f32
            )
            states.append((top, total, accum))
    top = functools.reduce(jnp.maximum, [s[0] for s in states])
    total = accum = None
    for t, s, a in states:
        factor = jnp.exp(t - top)
        total = s * factor if total is None else total + s * factor
        accum = a * factor if accum is None else accum + a * factor
    attended = (accum / total).astype(bf16)
    attended = jnp.concatenate([attended[h * rows : (h + 1) * rows] for h in range(heads)], axis=1)
    left_ref[...] = attended
    scatter_dot(wide, attended, w_ref, send_ref, distances)


def hidden_kernel(outer, wide, distances, *refs):
    gain_ref, gate_ref, up_ref, down_ref, left_ref, send_ref = refs[3:]
    gate = up = None
    for at, chunk in normed_chunks(outer, wide, part_list(outer, refs[:3]), gain_ref):
        g = jnp.dot(chunk, gate_ref[at, :], preferred_element_type=f32)
        u = jnp.dot(chunk, up_ref[at, :], preferred_element_type=f32)
        gate = g if gate is None else gate + g
        up = u if up is None else up + u
    hidden = (gate / (1.0 + jnp.exp(-gate)) * up).astype(bf16)
    left_ref[...] = hidden
    scatter_dot(wide, hidden, down_ref, send_ref, distances)


def half_kernel(own_ref, recv_ref, keep_ref, send_ref):
    half = own_ref.shape[1] // 2
    keep_ref[...] = own_ref[:, :half] + recv_ref[:, :half]
    send_ref[...] = (own_ref[:, half:] + recv_ref[:, half:]).astype(send_ref.dtype)


def fold_kernel(wide, own_ref, recv_ref, keep_ref, *sends):
    for k, out in enumerate((keep_ref, *sends)):
        at = slice(k * wide, (k + 1) * wide)
        out[...] = (own_ref[:, at] + recv_ref[:, at].astype(f32)).astype(out.dtype)


def final_kernel(base_ref, keep_ref, *refs):
    total = keep_ref[...]
    for r in refs[:-1]:
        total = total + r[...].astype(f32)
    refs[-1][...] = (base_ref[...].astype(f32) + total).astype(bf16)


def z_gathered(x, outer):
    return stacked([x] + [swap(x, QUAD * k) for k in range(1, outer)], 1)


def near_gathered(line):
    other = swap(line, 2)
    return [line, other, swap(stacked([line, other], 1), 1)]


def scattered(base, send, left, weight, outer, wide, y_type, z_type, beside=()):
    rows = base.shape[0]
    far = swap(send, 1)
    keep = call(
        functools.partial(scatter_kernel, wide, line_of(outer, 0, 2)),
        like((rows, 2 * outer * wide), f32),
        [left, weight],
    )
    keep, send = call(
        half_kernel, [like((rows, outer * wide), f32), like((rows, outer * wide), y_type)], [keep, far], beside
    )
    outs = [like((rows, wide), f32)] + [like((rows, wide), z_type)] * (outer - 1)
    keep, *sends = call(functools.partial(fold_kernel, wide), outs, [keep, swap(send, 2)], beside)
    arrived = [swap(s, QUAD * (k + 1)) for k, s in enumerate(sends)]
    return call(final_kernel, like((rows, wide), bf16), [base, keep, *arrived])


def local_pairs(
    x_rows, attn_gain, q_weight, o_weight, mlp_gain, gate_weight, up_weight, down_weight, kv_cache, block_mask
):
    rows, wide = x_rows.shape
    outer = lax.axis_size("seq") // QUAD
    columns = q_weight.shape[1]
    beside = [room(18432)]
    attn_gain = attn_gain.reshape(1, -1)
    mlp_gain = mlp_gain.reshape(1, -1)
    near = line_of(outer, 1, 3)

    size = 2 * kv_cache.shape[1] + rows
    own, send = call(
        functools.partial(pack_kernel, outer),
        [like((size, outer * HEAD_DIM), bf16)] * 2,
        [kv_cache, block_mask[:, :, 0]],
        beside,
    )
    other = swap(send, 2)
    line = z_gathered(x_rows, outer)
    routed = call(
        functools.partial(route_kernel, outer),
        [like((2 * size, HEAD_DIM), bf16)] * outer,
        [own, other, line],
        beside,
    )
    x_parts = near_gathered(line)
    queries = call(
        functools.partial(query_kernel, outer, wide),
        like((rows, columns), bf16),
        [*x_parts, attn_gain, q_weight],
    )
    arrived = [swap(routed[k], QUAD * k) for k in range(1, outer)]
    mine = stacked([routed[0], *arrived], 0, [queries])
    cache = [mine, swap(mine, 1)]
    left, send = call(
        functools.partial(attend_kernel, wide, near, [2 * outer] * 2),
        [like((rows, columns), bf16), like((rows, 2 * outer * wide), f32)],
        [queries, *cache, o_weight],
    )
    stream = scattered(x_rows, send, left, o_weight, outer, wide, f32, f32, beside)
    parts = near_gathered(z_gathered(stream, outer))
    left, send = call(
        functools.partial(hidden_kernel, outer, wide, near),
        [like((rows, gate_weight.shape[1]), bf16), like((rows, 2 * outer * wide), f32)],
        [*parts, mlp_gain, gate_weight, up_weight, down_weight],
    )
    return scattered(stream, send, left, down_weight, outer, wide, bf16, f32)


def rms_norm(values, gain):
    wide = values.astype(f32)
    inverse = lax.rsqrt(jnp.mean(wide * wide, axis=-1, keepdims=True) + eps)
    return (wide * inverse * gain.astype(f32)).astype(bf16)


def combine_states(first, second):
    top_a, total_a, accum_a = first
    top_b, total_b, accum_b = second
    top = jnp.maximum(top_a, top_b)
    factor_a = jnp.exp(top_a - top)
    factor_b = jnp.exp(top_b - top)
    return (
        top,
        total_a * factor_a + total_b * factor_b,
        accum_a * factor_a[..., None] + accum_b * factor_b[..., None],
    )


def combined_all(x, axis, combine):
    everything = jax.tree.map(lambda part: lax.all_gather(part, axis), x)
    initial = jax.tree.map(lambda part: part[0], everything)

    def turn(k, so_far):
        return combine(so_far, jax.tree.map(lambda part: part[k], everything))

    return lax.fori_loop(1, lax.axis_size(axis), turn, initial)


def summed(weight, left):
    product = lax.dot_general(weight, left, (((0,), (1,)), ((), ())), preferred_element_type=f32)
    return lax.psum_scatter(product, "seq", scatter_dimension=0, tiled=True).T


def local_tokens(
    x_rows, attn_gain, q_weight, o_weight, mlp_gain, gate_weight, up_weight, down_weight, kv_cache, block_mask
):
    rows = x_rows.shape[0]
    group = HEADS // KV_HEADS
    key_len = kv_cache.shape[1]
    spans = key_len // BLOCK
    scale = 1.0 / HEAD_DIM**0.5
    normed = rms_norm(lax.all_gather(x_rows, "seq", axis=1, tiled=True), attn_gain)
    query_part = jnp.dot(normed, q_weight, preferred_element_type=f32).astype(bf16)
    queries = lax.all_gather(query_part, "seq", axis=1, tiled=True)

    def one_group(index):
        def cut(array, width):
            return lax.dynamic_slice_in_dim(array, index * width, width, 1)

        query_group = cut(queries, group * HEAD_DIM).reshape(rows, group, HEAD_DIM)
        scores = (
            jnp.einsum("rhd,kd->rhk", query_group, cut(kv_cache[0], HEAD_DIM), preferred_element_type=f32)
            * scale
        )
        scores = scores.reshape(rows, group, spans, BLOCK)
        live = (cut(block_mask, 1)[:, 0, :] == 1)[:, None, :, None]
        masked = jnp.where(live, scores, floor_score)
        top = jnp.max(masked, axis=(2, 3))
        weights = jnp.where(live, jnp.exp(masked - top[..., None, None]), 0.0)
        rounded = weights.astype(bf16).reshape(rows, group, key_len)
        accum = jnp.einsum("rhk,kd->rhd", rounded, cut(kv_cache[1], HEAD_DIM), preferred_element_type=f32)
        return (top, jnp.sum(weights, axis=(2, 3)), accum)

    states = lax.map(one_group, jnp.arange(KV_HEADS, dtype=jnp.int32))
    states = jax.tree.map(lambda part: jnp.moveaxis(part, 0, 1), states)
    columns = q_weight.shape[1]
    top, total, accum = combined_all(states, "seq", combine_states)
    attended = (accum / total[..., None]).reshape(rows, HEADS * HEAD_DIM).astype(bf16)
    attn_cols = lax.dynamic_slice_in_dim(attended, lax.axis_index("seq") * columns, columns, 1)
    stream = (x_rows.astype(f32) + summed(o_weight, attn_cols)).astype(bf16)
    normed_two = rms_norm(lax.all_gather(stream, "seq", axis=1, tiled=True), mlp_gain)
    gate = jnp.dot(normed_two, gate_weight, preferred_element_type=f32)
    upward = jnp.dot(normed_two, up_weight, preferred_element_type=f32)
    hidden = (jax.nn.silu(gate) * upward).astype(bf16)
    return (stream.astype(f32) + summed(down_weight, hidden)).astype(bf16)


def solution(mesh):
    pairs = mesh.shape["seq"] == 2 * KV_HEADS
    return jax.shard_map(
        local_pairs if pairs else local_tokens,
        mesh=mesh,
        in_specs=(
            P("group", "seq"),
            P(),
            P(None, "seq"),
            P("seq", None),
            P(),
            P(None, "seq"),
            P(None, "seq"),
            P("seq", None),
            P(None, ("group", "seq"), None),
            P("group", None, "seq"),
        ),
        out_specs=P("group", "seq"),
        check_vma=False,
    )
```

```python
import functools

import jax
import jax.numpy as jnp
from jax import lax
from jax.experimental import pallas as pl
from jax.experimental.pallas import tpu as pltpu
from jax.sharding import PartitionSpec as P

HEADS = 64
KV_HEADS = 8
HEAD_DIM = 128
BLOCK = 128
QUAD = 4

eps = 1e-05
floor_score = -1e30

bf16 = jnp.bfloat16
f32 = jnp.float32
VMEM = pl.BlockSpec(memory_space=pltpu.VMEM)


def call(body, outs, ins, beside=(), limit=4 * 2**20):
    count, extra = len(ins), len(beside)

    def kernel(*refs):
        body(*refs[:count], *refs[count + extra :])

    return pl.pallas_call(
        kernel,
        out_shape=outs,
        in_specs=[VMEM] * count + [pl.BlockSpec(memory_space=pl.ANY)] * extra,
        out_specs=jax.tree.map(lambda _: VMEM, outs),
        compiler_params=pltpu.CompilerParams(vmem_limit_bytes=limit),
    )(*ins, *beside)


def room(size):
    return pl.pallas_call(
        lambda out: None,
        out_shape=like((size, 1024), f32),
        out_specs=pl.BlockSpec(memory_space=pl.ANY),
    )()


def like(shape, dtype):
    return jax.ShapeDtypeStruct(shape, dtype)


def swap(x, distance):
    size = lax.axis_size("seq")
    return lax.ppermute(x, "seq", [(i, i ^ distance) for i in range(size)])


def live_lanes(mask, head, rows):
    lane = lax.broadcasted_iota(jnp.int32, mask.shape, 1)
    live = jnp.where((lane == head) & (mask == 1), 1.0, 0.0).astype(f32)
    return jnp.broadcast_to(jnp.sum(live, axis=1, keepdims=True), (rows, HEAD_DIM)).astype(bf16)


def pack_kernel(outer, kv_ref, mask_ref, own_ref, send_ref):
    y = (lax.axis_index("seq") // 2) % 2
    keys = kv_ref.shape[1]
    rows = mask_ref.shape[0]
    mask = mask_ref[...]
    for out, parity in ((send_ref, 1 - y), (own_ref, y)):
        for z in range(outer):
            head = 2 * z + parity
            cols = pl.ds(pl.multiple_of(head * HEAD_DIM, HEAD_DIM), HEAD_DIM)
            at = slice(z * HEAD_DIM, (z + 1) * HEAD_DIM)
            out[0:keys, at] = kv_ref[0, :, cols]
            out[keys : 2 * keys, at] = kv_ref[1, :, cols]
            out[2 * keys : 2 * keys + rows, at] = live_lanes(mask, head, rows)


def route_kernel(outer, own_ref, other_ref, *outs):
    z = lax.axis_index("seq") // QUAD
    size = own_ref.shape[0]
    for k in range(outer):
        peer = jnp.bitwise_xor(z, k)
        cols = pl.ds(pl.multiple_of(peer * HEAD_DIM, HEAD_DIM), HEAD_DIM)
        outs[k][0:size, :] = own_ref[:, cols]
        outs[k][size : 2 * size, :] = other_ref[:, cols]


def stack_kernel(axis, *refs):
    at = 0
    for ref in refs[:-1]:
        size = ref.shape[axis]
        if axis == 0:
            refs[-1][at : at + size, :] = ref[...]
        else:
            refs[-1][:, at : at + size] = ref[...]
        at += size


def stacked(parts, axis, beside=()):
    shape = list(parts[0].shape)
    shape[axis] = sum(p.shape[axis] for p in parts)
    return call(functools.partial(stack_kernel, axis), like(tuple(shape), parts[0].dtype), parts, beside)


def normed_chunks(outer, wide, part_refs, gain_ref):
    me = lax.axis_index("seq")
    width = QUAD * outer * wide
    squares = None
    for ref, _ in part_refs:
        v = ref[...].astype(f32)
        s = jnp.sum(v * v, axis=1, keepdims=True)
        squares = s if squares is None else squares + s
    inverse = lax.rsqrt(squares / width + eps)
    for ref, distances in part_refs:
        for i, distance in enumerate(distances):
            source = jnp.bitwise_xor(me, distance)
            at = pl.ds(pl.multiple_of(source * wide, wide), wide)
            v = ref[:, i * wide : (i + 1) * wide].astype(f32)
            yield at, (v * inverse * gain_ref[:, at].astype(f32)).astype(bf16)


def line_of(outer, *nears):
    return [QUAD * k + j for j in nears for k in range(outer)]


def part_list(outer, refs):
    return list(zip(refs, (line_of(outer, 0), line_of(outer, 2), line_of(outer, 1, 3))))


def query_kernel(outer, wide, *refs):
    gain_ref, w_ref, out_ref = refs[3:]
    total = None
    for at, chunk in normed_chunks(outer, wide, part_list(outer, refs[:3]), gain_ref):
        term = jnp.dot(chunk, w_ref[at, :], preferred_element_type=f32)
        total = term if total is None else total + term
    out_ref[...] = total.astype(bf16)


def scatter_dot(wide, left, w_ref, out_ref, distances):
    me = lax.axis_index("seq")
    for i, distance in enumerate(distances):
        target = jnp.bitwise_xor(me, distance)
        at = pl.ds(pl.multiple_of(target * wide, wide), wide)
        out_ref[:, i * wide : (i + 1) * wide] = jnp.dot(left, w_ref[:, at], preferred_element_type=f32)


def scatter_kernel(wide, distances, left_ref, w_ref, out_ref):
    scatter_dot(wide, left_ref[...], w_ref, out_ref, distances)


def span_states(spans, q_ref, cache):
    rows = q_ref.shape[0]
    heads = q_ref.shape[1] // HEAD_DIM
    scale = 1.0 / HEAD_DIM**0.5
    queries = jnp.concatenate(
        [q_ref[:, h * HEAD_DIM : (h + 1) * HEAD_DIM] for h in range(heads)], axis=0
    )
    states = []
    for ref in cache:
        size = ref.shape[0] // spans
        keys = (size - rows) // 2
        for k in range(spans):
            at = k * size
            live = ref[at + 2 * keys : at + size, :].astype(f32)
            live = jnp.concatenate([live] * heads, axis=0) > 0.5
            score = (
                lax.dot_general(
                    queries,
                    ref[at : at + keys, :],
                    (((1,), (1,)), ((), ())),
                    preferred_element_type=f32,
                )
                * scale
            )
            masked = jnp.where(live, score, floor_score)
            top = jnp.max(masked, axis=1, keepdims=True)
            weight = jnp.where(live, jnp.exp(masked - top), 0.0)
            total = jnp.sum(weight, axis=1, keepdims=True)
            accum = jnp.dot(
                weight.astype(bf16), ref[at + keys : at + 2 * keys, :], preferred_element_type=f32
            )
            states.append((top, total, accum))
    return states


def combined(states):
    top = functools.reduce(jnp.maximum, [s[0] for s in states])
    total = accum = None
    for t, s, a in states:
        factor = jnp.exp(t - top)
        total = s * factor if total is None else total + s * factor
        accum = a * factor if accum is None else accum + a * factor
    return top, total, accum


def early_kernel(spans, q_ref, *refs):
    cache, (top_ref, total_ref, accum_ref) = refs[:-3], refs[-3:]
    top, total, accum_ref[...] = combined(span_states(spans, q_ref, cache))
    top_ref[...] = jnp.broadcast_to(top, top_ref.shape)
    total_ref[...] = jnp.broadcast_to(total, total_ref.shape)


def attend_kernel(wide, distances, spans, q_ref, top_ref, total_ref, accum_ref, *refs):
    cache, w_ref, left_ref, send_ref = refs[:-3], *refs[-3:]
    rows = q_ref.shape[0]
    heads = q_ref.shape[1] // HEAD_DIM
    states = span_states(spans, q_ref, cache)
    states.append((top_ref[:, 0:1], total_ref[:, 0:1], accum_ref[...]))
    _, total, accum = combined(states)
    attended = (accum / total).astype(bf16)
    attended = jnp.concatenate([attended[h * rows : (h + 1) * rows] for h in range(heads)], axis=1)
    left_ref[...] = attended
    scatter_dot(wide, attended, w_ref, send_ref, distances)


def hidden_kernel(outer, wide, distances, *refs):
    gain_ref, gate_ref, up_ref, down_ref, left_ref, send_ref = refs[3:]
    gate = up = None
    for at, chunk in normed_chunks(outer, wide, part_list(outer, refs[:3]), gain_ref):
        g = jnp.dot(chunk, gate_ref[at, :], preferred_element_type=f32)
        u = jnp.dot(chunk, up_ref[at, :], preferred_element_type=f32)
        gate = g if gate is None else gate + g
        up = u if up is None else up + u
    hidden = (gate / (1.0 + jnp.exp(-gate)) * up).astype(bf16)
    left_ref[...] = hidden
    scatter_dot(wide, hidden, down_ref, send_ref, distances)


def half_kernel(own_ref, recv_ref, keep_ref, send_ref):
    half = own_ref.shape[1] // 2
    keep_ref[...] = own_ref[:, :half] + recv_ref[:, :half]
    send_ref[...] = (own_ref[:, half:] + recv_ref[:, half:]).astype(send_ref.dtype)


def fold_kernel(wide, own_ref, recv_ref, keep_ref, *sends):
    for k, out in enumerate((keep_ref, *sends)):
        at = slice(k * wide, (k + 1) * wide)
        out[...] = (own_ref[:, at] + recv_ref[:, at].astype(f32)).astype(out.dtype)


def final_kernel(base_ref, keep_ref, *refs):
    total = keep_ref[...]
    for r in refs[:-1]:
        total = total + r[...].astype(f32)
    refs[-1][...] = (base_ref[...].astype(f32) + total).astype(bf16)


def z_swapped(parts):
    arrived = [swap(part, QUAD * k) for k, part in reversed(list(enumerate(parts))) if k > 0]
    return [parts[0], *reversed(arrived)]


def z_gathered(x, outer):
    return stacked(z_swapped([x] * outer), 1)


def near_gathered(line, after=()):
    other = swap(line, 2)
    return [line, other, swap(stacked([line, other], 1, after), 1)]


def scattered(base, send, left, weight, outer, wide, y_type, z_type, beside=()):
    rows = base.shape[0]
    far = swap(send, 1)
    keep = call(
        functools.partial(scatter_kernel, wide, line_of(outer, 0, 2)),
        like((rows, 2 * outer * wide), f32),
        [left, weight],
    )
    keep, send = call(
        half_kernel, [like((rows, outer * wide), f32), like((rows, outer * wide), y_type)], [keep, far], beside
    )
    outs = [like((rows, wide), f32)] + [like((rows, wide), z_type)] * (outer - 1)
    keep, *sends = call(functools.partial(fold_kernel, wide), outs, [keep, swap(send, 2)], beside)
    arrived = [swap(s, QUAD * (k + 1)) for k, s in enumerate(sends)]
    return call(final_kernel, like((rows, wide), bf16), [base, keep, *arrived])


def local_pairs(
    x_rows, attn_gain, q_weight, o_weight, mlp_gain, gate_weight, up_weight, down_weight, kv_cache, block_mask
):
    rows, wide = x_rows.shape
    outer = lax.axis_size("seq") // QUAD
    columns = q_weight.shape[1]
    beside = [room(18432)]
    attn_gain = attn_gain.reshape(1, -1)
    mlp_gain = mlp_gain.reshape(1, -1)
    near = line_of(outer, 1, 3)

    size = 2 * kv_cache.shape[1] + rows
    own, send = call(
        functools.partial(pack_kernel, outer),
        [like((size, outer * HEAD_DIM), bf16)] * 2,
        [kv_cache, block_mask[:, :, 0]],
        beside,
    )
    other = swap(send, 2)
    x_line = z_swapped([x_rows] * outer)
    line = stacked(x_line, 1)
    routed = call(
        functools.partial(route_kernel, outer),
        [like((2 * size, HEAD_DIM), bf16)] * outer,
        [own, other],
        [*[], *beside],
    )
    cache = z_swapped(routed)
    x_parts = near_gathered(line)
    queries = call(
        functools.partial(query_kernel, outer, wide),
        like((rows, columns), bf16),
        [*x_parts, attn_gain, q_weight],
    )
    first = stacked(cache, 0, [queries])
    second = swap(first, 1)
    tall = like((columns // HEAD_DIM * rows, HEAD_DIM), f32)
    early = call(functools.partial(early_kernel, 2 * outer), [tall] * 3, [queries, first])
    left, send = call(
        functools.partial(attend_kernel, wide, near, 2 * outer),
        [like((rows, columns), bf16), like((rows, 2 * outer * wide), f32)],
        [queries, *early, second, o_weight],
    )
    stream = scattered(x_rows, send, left, o_weight, outer, wide, f32, f32, beside)
    parts = near_gathered(z_gathered(stream, outer))
    left, send = call(
        functools.partial(hidden_kernel, outer, wide, near),
        [like((rows, gate_weight.shape[1]), bf16), like((rows, 2 * outer * wide), f32)],
        [*parts, mlp_gain, gate_weight, up_weight, down_weight],
    )
    return scattered(stream, send, left, down_weight, outer, wide, bf16, f32)


def rms_norm(values, gain):
    wide = values.astype(f32)
    inverse = lax.rsqrt(jnp.mean(wide * wide, axis=-1, keepdims=True) + eps)
    return (wide * inverse * gain.astype(f32)).astype(bf16)


def combine_states(first, second):
    top_a, total_a, accum_a = first
    top_b, total_b, accum_b = second
    top = jnp.maximum(top_a, top_b)
    factor_a = jnp.exp(top_a - top)
    factor_b = jnp.exp(top_b - top)
    return (
        top,
        total_a * factor_a + total_b * factor_b,
        accum_a * factor_a[..., None] + accum_b * factor_b[..., None],
    )


def combined_all(x, axis, combine):
    everything = jax.tree.map(lambda part: lax.all_gather(part, axis), x)
    initial = jax.tree.map(lambda part: part[0], everything)

    def turn(k, so_far):
        return combine(so_far, jax.tree.map(lambda part: part[k], everything))

    return lax.fori_loop(1, lax.axis_size(axis), turn, initial)


def summed(weight, left):
    product = lax.dot_general(weight, left, (((0,), (1,)), ((), ())), preferred_element_type=f32)
    return lax.psum_scatter(product, "seq", scatter_dimension=0, tiled=True).T


def local_tokens(
    x_rows, attn_gain, q_weight, o_weight, mlp_gain, gate_weight, up_weight, down_weight, kv_cache, block_mask
):
    rows = x_rows.shape[0]
    group = HEADS // KV_HEADS
    key_len = kv_cache.shape[1]
    spans = key_len // BLOCK
    scale = 1.0 / HEAD_DIM**0.5
    normed = rms_norm(lax.all_gather(x_rows, "seq", axis=1, tiled=True), attn_gain)
    query_part = jnp.dot(normed, q_weight, preferred_element_type=f32).astype(bf16)
    queries = lax.all_gather(query_part, "seq", axis=1, tiled=True)

    def one_group(index):
        def cut(array, width):
            return lax.dynamic_slice_in_dim(array, index * width, width, 1)

        query_group = cut(queries, group * HEAD_DIM).reshape(rows, group, HEAD_DIM)
        scores = (
            jnp.einsum("rhd,kd->rhk", query_group, cut(kv_cache[0], HEAD_DIM), preferred_element_type=f32)
            * scale
        )
        scores = scores.reshape(rows, group, spans, BLOCK)
        live = (cut(block_mask, 1)[:, 0, :] == 1)[:, None, :, None]
        masked = jnp.where(live, scores, floor_score)
        top = jnp.max(masked, axis=(2, 3))
        weights = jnp.where(live, jnp.exp(masked - top[..., None, None]), 0.0)
        rounded = weights.astype(bf16).reshape(rows, group, key_len)
        accum = jnp.einsum("rhk,kd->rhd", rounded, cut(kv_cache[1], HEAD_DIM), preferred_element_type=f32)
        return (top, jnp.sum(weights, axis=(2, 3)), accum)

    states = lax.map(one_group, jnp.arange(KV_HEADS, dtype=jnp.int32))
    states = jax.tree.map(lambda part: jnp.moveaxis(part, 0, 1), states)
    columns = q_weight.shape[1]
    top, total, accum = combined_all(states, "seq", combine_states)
    attended = (accum / total[..., None]).reshape(rows, HEADS * HEAD_DIM).astype(bf16)
    attn_cols = lax.dynamic_slice_in_dim(attended, lax.axis_index("seq") * columns, columns, 1)
    stream = (x_rows.astype(f32) + summed(o_weight, attn_cols)).astype(bf16)
    normed_two = rms_norm(lax.all_gather(stream, "seq", axis=1, tiled=True), mlp_gain)
    gate = jnp.dot(normed_two, gate_weight, preferred_element_type=f32)
    upward = jnp.dot(normed_two, up_weight, preferred_element_type=f32)
    hidden = (jax.nn.silu(gate) * upward).astype(bf16)
    return (stream.astype(f32) + summed(down_weight, hidden)).astype(bf16)


def solution(mesh):
    pairs = mesh.shape["seq"] == 2 * KV_HEADS
    return jax.shard_map(
        local_pairs if pairs else local_tokens,
        mesh=mesh,
        in_specs=(
            P("group", "seq"),
            P(),
            P(None, "seq"),
            P("seq", None),
            P(),
            P(None, "seq"),
            P(None, "seq"),
            P("seq", None),
            P(None, ("group", "seq"), None),
            P("group", None, "seq"),
        ),
        out_specs=P("group", "seq"),
        check_vma=False,
    )
```

```python
import functools

import jax
import jax.numpy as jnp
from jax import lax
from jax.experimental import pallas as pl
from jax.experimental.pallas import tpu as pltpu
from jax.sharding import PartitionSpec as P

HEADS = 64
KV_HEADS = 8
HEAD_DIM = 128
BLOCK = 128
QUAD = 4

eps = 1e-05
floor_score = -1e30

bf16 = jnp.bfloat16
f32 = jnp.float32
VMEM = pl.BlockSpec(memory_space=pltpu.VMEM)


def call(body, outs, ins, beside=(), limit=4 * 2**20):
    count, extra = len(ins), len(beside)

    def kernel(*refs):
        body(*refs[:count], *refs[count + extra :])

    return pl.pallas_call(
        kernel,
        out_shape=outs,
        in_specs=[VMEM] * count + [pl.BlockSpec(memory_space=pl.ANY)] * extra,
        out_specs=jax.tree.map(lambda _: VMEM, outs),
        compiler_params=pltpu.CompilerParams(vmem_limit_bytes=limit),
    )(*ins, *beside)


def room(size):
    return pl.pallas_call(
        lambda out: None,
        out_shape=like((size, 1024), f32),
        out_specs=pl.BlockSpec(memory_space=pl.ANY),
    )()


def like(shape, dtype):
    return jax.ShapeDtypeStruct(shape, dtype)


def swap(x, distance):
    size = lax.axis_size("seq")
    return lax.ppermute(x, "seq", [(i, i ^ distance) for i in range(size)])


def live_lanes(mask, head, rows):
    lane = lax.broadcasted_iota(jnp.int32, mask.shape, 1)
    live = jnp.where((lane == head) & (mask == 1), 1.0, 0.0).astype(f32)
    return jnp.broadcast_to(jnp.sum(live, axis=1, keepdims=True), (rows, HEAD_DIM)).astype(bf16)


def pack_kernel(outer, kv_ref, mask_ref, own_ref, send_ref):
    y = (lax.axis_index("seq") // 2) % 2
    keys = kv_ref.shape[1]
    rows = mask_ref.shape[0]
    mask = mask_ref[...]
    for out, parity in ((send_ref, 1 - y), (own_ref, y)):
        for z in range(outer):
            head = 2 * z + parity
            cols = pl.ds(pl.multiple_of(head * HEAD_DIM, HEAD_DIM), HEAD_DIM)
            at = slice(z * HEAD_DIM, (z + 1) * HEAD_DIM)
            out[0:keys, at] = kv_ref[0, :, cols]
            out[keys : 2 * keys, at] = kv_ref[1, :, cols]
            out[2 * keys : 2 * keys + rows, at] = live_lanes(mask, head, rows)


def route_kernel(outer, own_ref, other_ref, *outs):
    z = lax.axis_index("seq") // QUAD
    size = own_ref.shape[0]
    for k in range(outer):
        peer = jnp.bitwise_xor(z, k)
        cols = pl.ds(pl.multiple_of(peer * HEAD_DIM, HEAD_DIM), HEAD_DIM)
        outs[k][0:size, :] = own_ref[:, cols]
        outs[k][size : 2 * size, :] = other_ref[:, cols]


def stack_kernel(axis, *refs):
    at = 0
    for ref in refs[:-1]:
        size = ref.shape[axis]
        if axis == 0:
            refs[-1][at : at + size, :] = ref[...]
        else:
            refs[-1][:, at : at + size] = ref[...]
        at += size


def stacked(parts, axis, beside=()):
    shape = list(parts[0].shape)
    shape[axis] = sum(p.shape[axis] for p in parts)
    return call(functools.partial(stack_kernel, axis), like(tuple(shape), parts[0].dtype), parts, beside)


def normed_chunks(wide, chunks, gain_ref):
    squares = None
    for source, load in chunks:
        v = load().astype(f32)
        s = jnp.sum(v * v, axis=1, keepdims=True)
        squares = s if squares is None else squares + s
    inverse = lax.rsqrt(squares / (len(chunks) * wide) + eps)
    for source, load in chunks:
        at = pl.ds(pl.multiple_of(source * wide, wide), wide)
        yield at, (load().astype(f32) * inverse * gain_ref[:, at].astype(f32)).astype(bf16)


def to_members(parts):
    size = lax.axis_size("seq")
    groups = [list(range(core, size, 2)) for core in range(2)]
    return lax.all_to_all(parts, "seq", 0, 0, axis_index_groups=groups, tiled=True)


def member(i, other):
    core = lax.axis_index("seq") % 2
    return 2 * i + (1 - core if other else core)


def line_of(outer, *nears):
    return [QUAD * k + j for j in nears for k in range(outer)]


def line_chunks(outer, wide, refs):
    me = lax.axis_index("seq")
    lines = (line_of(outer, 0), line_of(outer, 2), line_of(outer, 1, 3))
    return [
        (jnp.bitwise_xor(me, distance), lambda r=ref, i=i: r[:, i * wide : (i + 1) * wide])
        for ref, line in zip(refs, lines)
        for i, distance in enumerate(line)
    ]


def member_chunks(refs):
    return [
        (member(i, other), lambda r=ref, i=i: r[i])
        for other, ref in enumerate(refs)
        for i in range(ref.shape[0])
    ]


def query_kernel(outer, wide, *refs):
    gain_ref, w_ref, out_ref = refs[3:]
    total = None
    for at, chunk in normed_chunks(wide, line_chunks(outer, wide, refs[:3]), gain_ref):
        term = jnp.dot(chunk, w_ref[at, :], preferred_element_type=f32)
        total = term if total is None else total + term
    out_ref[...] = total.astype(bf16)


def scatter_dot(wide, other, left, w_ref, out_ref):
    for i in range(out_ref.shape[0]):
        at = pl.ds(pl.multiple_of(member(i, other) * wide, wide), wide)
        out_ref[i] = jnp.dot(left, w_ref[:, at], preferred_element_type=f32)


def keep_kernel(wide, left_ref, w_ref, out_ref):
    scatter_dot(wide, False, left_ref[...], w_ref, out_ref)


def span_states(spans, q_ref, cache):
    rows = q_ref.shape[0]
    heads = q_ref.shape[1] // HEAD_DIM
    scale = 1.0 / HEAD_DIM**0.5
    queries = jnp.concatenate(
        [q_ref[:, h * HEAD_DIM : (h + 1) * HEAD_DIM] for h in range(heads)], axis=0
    )
    states = []
    for ref in cache:
        size = ref.shape[0] // spans
        keys = (size - rows) // 2
        for k in range(spans):
            at = k * size
            live = ref[at + 2 * keys : at + size, :].astype(f32)
            live = jnp.concatenate([live] * heads, axis=0) > 0.5
            score = (
                lax.dot_general(
                    queries,
                    ref[at : at + keys, :],
                    (((1,), (1,)), ((), ())),
                    preferred_element_type=f32,
                )
                * scale
            )
            masked = jnp.where(live, score, floor_score)
            top = jnp.max(masked, axis=1, keepdims=True)
            weight = jnp.where(live, jnp.exp(masked - top), 0.0)
            total = jnp.sum(weight, axis=1, keepdims=True)
            accum = jnp.dot(
                weight.astype(bf16), ref[at + keys : at + 2 * keys, :], preferred_element_type=f32
            )
            states.append((top, total, accum))
    return states


def combined(states):
    top = functools.reduce(jnp.maximum, [s[0] for s in states])
    total = accum = None
    for t, s, a in states:
        factor = jnp.exp(t - top)
        total = s * factor if total is None else total + s * factor
        accum = a * factor if accum is None else accum + a * factor
    return top, total, accum


def early_kernel(spans, q_ref, *refs):
    cache, (top_ref, total_ref, accum_ref) = refs[:-3], refs[-3:]
    top, total, accum_ref[...] = combined(span_states(spans, q_ref, cache))
    top_ref[...] = jnp.broadcast_to(top, top_ref.shape)
    total_ref[...] = jnp.broadcast_to(total, total_ref.shape)


def attend_kernel(wide, spans, q_ref, top_ref, total_ref, accum_ref, *refs):
    cache, w_ref, left_ref, send_ref = refs[:-3], *refs[-3:]
    rows = q_ref.shape[0]
    heads = q_ref.shape[1] // HEAD_DIM
    states = span_states(spans, q_ref, cache)
    states.append((top_ref[:, 0:1], total_ref[:, 0:1], accum_ref[...]))
    _, total, accum = combined(states)
    attended = (accum / total).astype(bf16)
    attended = jnp.concatenate([attended[h * rows : (h + 1) * rows] for h in range(heads)], axis=1)
    left_ref[...] = attended
    scatter_dot(wide, True, attended, w_ref, send_ref)


def hidden_kernel(wide, *refs):
    gain_ref, gate_ref, up_ref, down_ref, left_ref, send_ref = refs[2:]
    gate = up = None
    for at, chunk in normed_chunks(wide, member_chunks(refs[:2]), gain_ref):
        g = jnp.dot(chunk, gate_ref[at, :], preferred_element_type=f32)
        u = jnp.dot(chunk, up_ref[at, :], preferred_element_type=f32)
        gate = g if gate is None else gate + g
        up = u if up is None else up + u
    hidden = (gate / (1.0 + jnp.exp(-gate)) * up).astype(bf16)
    left_ref[...] = hidden
    scatter_dot(wide, True, hidden, down_ref, send_ref)


def add_kernel(own_ref, recv_ref, out_ref):
    out_ref[...] = (own_ref[...] + recv_ref[...]).astype(out_ref.dtype)


def final_kernel(base_ref, parts_ref, *out_refs):
    total = parts_ref[0].astype(f32)
    for i in range(1, parts_ref.shape[0]):
        total = total + parts_ref[i].astype(f32)
    total = (base_ref[...].astype(f32) + total).astype(bf16)
    for out in out_refs:
        if len(out.shape) == 3:
            for i in range(out.shape[0]):
                out[i] = total
        else:
            out[...] = total


def z_swapped(parts):
    arrived = [swap(part, QUAD * k) for k, part in reversed(list(enumerate(parts))) if k > 0]
    return [parts[0], *reversed(arrived)]


def z_gathered(x, outer):
    return stacked(z_swapped([x] * outer), 1)


def near_gathered(line, after=()):
    other = swap(line, 2)
    return [line, other, swap(stacked([line, other], 1, after), 1)]


def scattered(base, send, left, weight, wide, kind, outs, beside=()):
    far = swap(send, 1)
    own = call(functools.partial(keep_kernel, wide), like(send.shape, f32), [left, weight])
    sums = call(add_kernel, like(send.shape, kind), [own, far], beside)
    return call(final_kernel, outs, [base, to_members(sums)], beside)


def local_pairs(
    x_rows, attn_gain, q_weight, o_weight, mlp_gain, gate_weight, up_weight, down_weight, kv_cache, block_mask
):
    rows, wide = x_rows.shape
    outer = lax.axis_size("seq") // QUAD
    columns = q_weight.shape[1]
    beside = [room(18432)]
    attn_gain = attn_gain.reshape(1, -1)
    mlp_gain = mlp_gain.reshape(1, -1)
    members = lax.axis_size("seq") // 2
    partial_sums = like((members, rows, wide), f32)
    own_columns = like((rows, wide), bf16)

    size = 2 * kv_cache.shape[1] + rows
    own, send = call(
        functools.partial(pack_kernel, outer),
        [like((size, outer * HEAD_DIM), bf16)] * 2,
        [kv_cache, block_mask[:, :, 0]],
        beside,
    )
    other = swap(send, 2)
    x_line = z_swapped([x_rows] * outer)
    line = stacked(x_line, 1)
    routed = call(
        functools.partial(route_kernel, outer),
        [like((2 * size, HEAD_DIM), bf16)] * outer,
        [own, other],
        [*[], *beside],
    )
    cache = z_swapped(routed)
    x_parts = near_gathered(line)
    queries = call(
        functools.partial(query_kernel, outer, wide),
        like((rows, columns), bf16),
        [*x_parts, attn_gain, q_weight],
    )
    first = stacked(cache, 0, [queries])
    second = swap(first, 1)
    tall = like((columns // HEAD_DIM * rows, HEAD_DIM), f32)
    early = call(functools.partial(early_kernel, 2 * outer), [tall] * 3, [queries, first])
    left, send = call(
        functools.partial(attend_kernel, wide, 2 * outer),
        [like((rows, columns), bf16), partial_sums],
        [queries, *early, second, o_weight],
    )
    stream, copies = scattered(
        x_rows, send, left, o_weight, wide, f32, [own_columns, like(partial_sums.shape, bf16)], beside
    )
    parts = to_members(copies)
    left, send = call(
        functools.partial(hidden_kernel, wide),
        [like((rows, gate_weight.shape[1]), bf16), partial_sums],
        [parts, swap(parts, 1), mlp_gain, gate_weight, up_weight, down_weight],
    )
    return scattered(stream, send, left, down_weight, wide, bf16, [own_columns])[0]


def rms_norm(values, gain):
    wide = values.astype(f32)
    inverse = lax.rsqrt(jnp.mean(wide * wide, axis=-1, keepdims=True) + eps)
    return (wide * inverse * gain.astype(f32)).astype(bf16)


def combine_states(first, second):
    top_a, total_a, accum_a = first
    top_b, total_b, accum_b = second
    top = jnp.maximum(top_a, top_b)
    factor_a = jnp.exp(top_a - top)
    factor_b = jnp.exp(top_b - top)
    return (
        top,
        total_a * factor_a + total_b * factor_b,
        accum_a * factor_a[..., None] + accum_b * factor_b[..., None],
    )


def combined_all(x, axis, combine):
    everything = jax.tree.map(lambda part: lax.all_gather(part, axis), x)
    initial = jax.tree.map(lambda part: part[0], everything)

    def turn(k, so_far):
        return combine(so_far, jax.tree.map(lambda part: part[k], everything))

    return lax.fori_loop(1, lax.axis_size(axis), turn, initial)


def summed(weight, left):
    product = lax.dot_general(weight, left, (((0,), (1,)), ((), ())), preferred_element_type=f32)
    return lax.psum_scatter(product, "seq", scatter_dimension=0, tiled=True).T


def local_tokens(
    x_rows, attn_gain, q_weight, o_weight, mlp_gain, gate_weight, up_weight, down_weight, kv_cache, block_mask
):
    rows = x_rows.shape[0]
    group = HEADS // KV_HEADS
    key_len = kv_cache.shape[1]
    spans = key_len // BLOCK
    scale = 1.0 / HEAD_DIM**0.5
    normed = rms_norm(lax.all_gather(x_rows, "seq", axis=1, tiled=True), attn_gain)
    query_part = jnp.dot(normed, q_weight, preferred_element_type=f32).astype(bf16)
    queries = lax.all_gather(query_part, "seq", axis=1, tiled=True)

    def one_group(index):
        def cut(array, width):
            return lax.dynamic_slice_in_dim(array, index * width, width, 1)

        query_group = cut(queries, group * HEAD_DIM).reshape(rows, group, HEAD_DIM)
        scores = (
            jnp.einsum("rhd,kd->rhk", query_group, cut(kv_cache[0], HEAD_DIM), preferred_element_type=f32)
            * scale
        )
        scores = scores.reshape(rows, group, spans, BLOCK)
        live = (cut(block_mask, 1)[:, 0, :] == 1)[:, None, :, None]
        masked = jnp.where(live, scores, floor_score)
        top = jnp.max(masked, axis=(2, 3))
        weights = jnp.where(live, jnp.exp(masked - top[..., None, None]), 0.0)
        rounded = weights.astype(bf16).reshape(rows, group, key_len)
        accum = jnp.einsum("rhk,kd->rhd", rounded, cut(kv_cache[1], HEAD_DIM), preferred_element_type=f32)
        return (top, jnp.sum(weights, axis=(2, 3)), accum)

    states = lax.map(one_group, jnp.arange(KV_HEADS, dtype=jnp.int32))
    states = jax.tree.map(lambda part: jnp.moveaxis(part, 0, 1), states)
    columns = q_weight.shape[1]
    top, total, accum = combined_all(states, "seq", combine_states)
    attended = (accum / total[..., None]).reshape(rows, HEADS * HEAD_DIM).astype(bf16)
    attn_cols = lax.dynamic_slice_in_dim(attended, lax.axis_index("seq") * columns, columns, 1)
    stream = (x_rows.astype(f32) + summed(o_weight, attn_cols)).astype(bf16)
    normed_two = rms_norm(lax.all_gather(stream, "seq", axis=1, tiled=True), mlp_gain)
    gate = jnp.dot(normed_two, gate_weight, preferred_element_type=f32)
    upward = jnp.dot(normed_two, up_weight, preferred_element_type=f32)
    hidden = (jax.nn.silu(gate) * upward).astype(bf16)
    return (stream.astype(f32) + summed(down_weight, hidden)).astype(bf16)


def solution(mesh):
    pairs = mesh.shape["seq"] == 2 * KV_HEADS
    return jax.shard_map(
        local_pairs if pairs else local_tokens,
        mesh=mesh,
        in_specs=(
            P("group", "seq"),
            P(),
            P(None, "seq"),
            P("seq", None),
            P(),
            P(None, "seq"),
            P(None, "seq"),
            P("seq", None),
            P(None, ("group", "seq"), None),
            P("group", None, "seq"),
        ),
        out_specs=P("group", "seq"),
        check_vma=False,
    )
```

```python
import functools

import jax
import jax.numpy as jnp
from jax import lax
from jax.experimental import pallas as pl
from jax.experimental.pallas import tpu as pltpu
from jax.sharding import PartitionSpec as P

HEADS = 64
KV_HEADS = 8
HEAD_DIM = 128
BLOCK = 128
QUAD = 4

eps = 1e-05
floor_score = -1e30

bf16 = jnp.bfloat16
f32 = jnp.float32
VMEM = pl.BlockSpec(memory_space=pltpu.VMEM)


def call(body, outs, ins, beside=(), limit=4 * 2**20):
    count, extra = len(ins), len(beside)

    def kernel(*refs):
        body(*refs[:count], *refs[count + extra :])

    return pl.pallas_call(
        kernel,
        out_shape=outs,
        in_specs=[VMEM] * count + [pl.BlockSpec(memory_space=pl.ANY)] * extra,
        out_specs=jax.tree.map(lambda _: VMEM, outs),
        compiler_params=pltpu.CompilerParams(vmem_limit_bytes=limit),
    )(*ins, *beside)


def room(size):
    return pl.pallas_call(
        lambda out: None,
        out_shape=like((size, 1024), f32),
        out_specs=pl.BlockSpec(memory_space=pl.ANY),
    )()


def like(shape, dtype):
    return jax.ShapeDtypeStruct(shape, dtype)


def swap(x, distance):
    size = lax.axis_size("seq")
    return lax.ppermute(x, "seq", [(i, i ^ distance) for i in range(size)])


def pack_kernel(outer, kv_ref, mask_ref, x_ref, held_ref, send_ref):
    me = lax.axis_index("seq")
    z, y = me // QUAD, (me // 2) % 2
    keys = kv_ref.shape[1]
    rows, wide = x_ref.shape
    lane = lax.broadcasted_iota(jnp.int32, (rows, HEAD_DIM), 1)
    mask = jnp.zeros((rows, HEAD_DIM), f32)
    for head in range(mask_ref.shape[1]):
        live = (mask_ref[:, head : head + 1] == 1).astype(f32)
        mask = jnp.where(lane == head, jnp.broadcast_to(live, mask.shape), mask)
    held_ref[:, 0:wide] = x_ref[...]
    held_ref[:, wide:] = mask.astype(bf16)
    for k in range(outer):
        head = 2 * jnp.bitwise_xor(z, k) + 1 - y
        cols = pl.ds(pl.multiple_of(head * HEAD_DIM, HEAD_DIM), HEAD_DIM)
        at = slice(k * HEAD_DIM, (k + 1) * HEAD_DIM)
        send_ref[0:keys, at] = kv_ref[0, :, cols]
        send_ref[keys : 2 * keys, at] = kv_ref[1, :, cols]


def z_slots(outer):
    order = list(range(outer - 1, 0, -1))
    return list(zip([0, *order[-1:], *order[:-1]], [0, *order]))


def z_distance(slot, core):
    return jnp.where(core == 0, slot[0], slot[1])


def route_kernel(outer, kv_ref, other_ref, *outs):
    me = lax.axis_index("seq")
    z, y = me // QUAD, (me // 2) % 2
    keys = kv_ref.shape[1]
    for slot, out in zip(z_slots(outer), outs):
        k = z_distance(slot, me % 2)
        head = 2 * jnp.bitwise_xor(z, k) + y
        cols = pl.ds(pl.multiple_of(head * HEAD_DIM, HEAD_DIM), HEAD_DIM)
        out[0:keys, :] = kv_ref[0, :, cols]
        out[keys : 2 * keys, :] = kv_ref[1, :, cols]
        out[2 * keys :, :] = other_ref[:, pl.ds(pl.multiple_of(k * HEAD_DIM, HEAD_DIM), HEAD_DIM)]


def stack_kernel(axis, *refs):
    at = 0
    for ref in refs[:-1]:
        size = ref.shape[axis]
        if axis == 0:
            refs[-1][at : at + size, :] = ref[...]
        else:
            refs[-1][:, at : at + size] = ref[...]
        at += size


def stacked(parts, axis, beside=()):
    shape = list(parts[0].shape)
    shape[axis] = sum(p.shape[axis] for p in parts)
    return call(functools.partial(stack_kernel, axis), like(tuple(shape), parts[0].dtype), parts, beside)


def normed_chunks(wide, chunks, gain_ref):
    squares = None
    for source, load in chunks:
        v = load().astype(f32)
        s = jnp.sum(v * v, axis=1, keepdims=True)
        squares = s if squares is None else squares + s
    inverse = lax.rsqrt(squares / (len(chunks) * wide) + eps)
    for source, load in chunks:
        at = pl.ds(pl.multiple_of(source * wide, wide), wide)
        yield at, (load().astype(f32) * inverse * gain_ref[:, at].astype(f32)).astype(bf16)


def to_members(parts):
    size = lax.axis_size("seq")
    groups = [list(range(core, size, 2)) for core in range(2)]
    return lax.all_to_all(parts, "seq", 0, 0, axis_index_groups=groups, tiled=True)


def member(i, other):
    core = lax.axis_index("seq") % 2
    return 2 * i + (1 - core if other else core)


def line_of(outer, *nears):
    return [QUAD * k + j for j in nears for k in range(outer)]


def line_chunks(outer, wide, refs):
    me = lax.axis_index("seq")
    lines = [line_of(outer, near) for near in range(QUAD)]
    step = wide + HEAD_DIM
    return [
        (jnp.bitwise_xor(me, distance), lambda r=ref, i=i: r[:, i * step : i * step + wide])
        for ref, line in zip(refs, lines)
        for i, distance in enumerate(line)
    ]


def line_mask(wide, ref, i):
    at = pl.multiple_of(i * (wide + HEAD_DIM) + wide, HEAD_DIM)
    tile = ref[:, pl.ds(at, HEAD_DIM)].astype(f32)
    lane = lax.broadcasted_iota(jnp.int32, tile.shape, 1)
    mine = jnp.where(lane == lax.axis_index("seq") // 2, tile, 0.0)
    return jnp.broadcast_to(jnp.sum(mine, axis=1, keepdims=True), tile.shape)


def member_chunks(refs):
    return [
        (member(i, other), lambda r=ref, i=i: r[i])
        for other, ref in enumerate(refs)
        for i in range(ref.shape[0])
    ]


def query_kernel(outer, wide, *refs):
    gain_ref, w_ref, out_ref = refs[QUAD:]
    total = None
    for at, chunk in normed_chunks(wide, line_chunks(outer, wide, refs[:QUAD]), gain_ref):
        term = jnp.dot(chunk, w_ref[at, :], preferred_element_type=f32)
        total = term if total is None else total + term
    out_ref[...] = total.astype(bf16)


def scatter_dot(wide, other, left, w_ref, out_ref):
    for i in range(out_ref.shape[0]):
        at = pl.ds(pl.multiple_of(member(i, other) * wide, wide), wide)
        out_ref[i] = jnp.dot(left, w_ref[:, at], preferred_element_type=f32)


def keep_kernel(wide, left_ref, w_ref, out_ref):
    scatter_dot(wide, False, left_ref[...], w_ref, out_ref)


def span_states(q_ref, cache_ref, masks):
    heads = q_ref.shape[1] // HEAD_DIM
    scale = 1.0 / HEAD_DIM**0.5
    keys = cache_ref.shape[0] // (2 * len(masks))
    queries = jnp.concatenate(
        [q_ref[:, h * HEAD_DIM : (h + 1) * HEAD_DIM] for h in range(heads)], axis=0
    )
    scores = [
        lax.dot_general(
            queries,
            cache_ref[2 * i * keys : (2 * i + 1) * keys, :],
            (((1,), (1,)), ((), ())),
            preferred_element_type=f32,
        )
        * scale
        for i in range(len(masks))
    ]
    lives = [jnp.concatenate([mask] * heads, axis=0) > 0.5 for mask in masks]
    scores = [jnp.where(live, score, floor_score) for live, score in zip(lives, scores)]
    tops = [jnp.max(score, axis=1, keepdims=True) for score in scores]
    weights = [
        jnp.where(live, jnp.exp(score - top), 0.0) for live, score, top in zip(lives, scores, tops)
    ]
    totals = [jnp.sum(weight, axis=1, keepdims=True) for weight in weights]
    accums = [
        jnp.dot(
            weight.astype(bf16),
            cache_ref[(2 * i + 1) * keys : (2 * i + 2) * keys, :],
            preferred_element_type=f32,
        )
        for i, weight in enumerate(weights)
    ]
    return list(zip(tops, totals, accums))


def combined(states):
    top = functools.reduce(jnp.maximum, [s[0] for s in states])
    total = accum = None
    for t, s, a in states:
        factor = jnp.exp(t - top)
        total = s * factor if total is None else total + s * factor
        accum = a * factor if accum is None else accum + a * factor
    return top, total, accum


def early_kernel(outer, wide, q_ref, cache_ref, line_ref, other_ref, top_ref, total_ref, accum_ref):
    core = lax.axis_index("seq") % 2
    masks = [
        line_mask(wide, ref, z_distance(slot, core))
        for slot in z_slots(outer)
        for ref in (line_ref, other_ref)
    ]
    top, total, accum_ref[...] = combined(span_states(q_ref, cache_ref, masks))
    top_ref[...] = jnp.broadcast_to(top, top_ref.shape)
    total_ref[...] = jnp.broadcast_to(total, total_ref.shape)


def attend_kernel(
    outer, wide, q_ref, top_ref, total_ref, accum_ref, cache_ref, core_ref, far_ref, w_ref, left_ref, send_ref
):
    rows = q_ref.shape[0]
    heads = q_ref.shape[1] // HEAD_DIM
    core = 1 - lax.axis_index("seq") % 2
    masks = [
        line_mask(wide, ref, z_distance(slot, core))
        for slot in z_slots(outer)
        for ref in (core_ref, far_ref)
    ]
    states = span_states(q_ref, cache_ref, masks)
    states.append((top_ref[:, 0:1], total_ref[:, 0:1], accum_ref[...]))
    _, total, accum = combined(states)
    attended = (accum / total).astype(bf16)
    attended = jnp.concatenate([attended[h * rows : (h + 1) * rows] for h in range(heads)], axis=1)
    left_ref[...] = attended
    scatter_dot(wide, True, attended, w_ref, send_ref)


def hidden_kernel(wide, *refs):
    gain_ref, gate_ref, up_ref, down_ref, left_ref, send_ref = refs[2:]
    gate = up = None
    for at, chunk in normed_chunks(wide, member_chunks(refs[:2]), gain_ref):
        g = jnp.dot(chunk, gate_ref[at, :], preferred_element_type=f32)
        u = jnp.dot(chunk, up_ref[at, :], preferred_element_type=f32)
        gate = g if gate is None else gate + g
        up = u if up is None else up + u
    hidden = (gate / (1.0 + jnp.exp(-gate)) * up).astype(bf16)
    left_ref[...] = hidden
    scatter_dot(wide, True, hidden, down_ref, send_ref)


def add_kernel(own_ref, recv_ref, out_ref):
    out_ref[...] = (own_ref[...] + recv_ref[...]).astype(out_ref.dtype)


def final_kernel(base_ref, parts_ref, *out_refs):
    total = parts_ref[0].astype(f32)
    for i in range(1, parts_ref.shape[0]):
        total = total + parts_ref[i].astype(f32)
    total = (base_ref[...].astype(f32) + total).astype(bf16)
    for out in out_refs:
        if len(out.shape) == 3:
            for i in range(out.shape[0]):
                out[i] = total
        else:
            out[...] = total


def z_swapped(parts):
    arrived = [swap(part, QUAD * k) for k, part in reversed(list(enumerate(parts))) if k > 0]
    return [parts[0], *reversed(arrived)]


def z_routed(parts):
    size = lax.axis_size("seq")
    return [parts[0]] + [
        lax.ppermute(part, "seq", [(i, i ^ QUAD * slot[i % 2]) for i in range(size)])
        for slot, part in list(zip(z_slots(len(parts)), parts))[1:]
    ]


def near_gathered(line):
    far, y, core = swap(line, 3), swap(line, 2), swap(line, 1)
    return [line, core, y, far]


def scattered(base, send, left, weight, wide, kind, outs, beside=()):
    far = swap(send, 1)
    own = call(functools.partial(keep_kernel, wide), like(send.shape, f32), [left, weight])
    sums = call(add_kernel, like(send.shape, kind), [own, far], beside)
    return call(final_kernel, outs, [base, to_members(sums)], beside)


def local_pairs(
    x_rows, attn_gain, q_weight, o_weight, mlp_gain, gate_weight, up_weight, down_weight, kv_cache, block_mask
):
    rows, wide = x_rows.shape
    outer = lax.axis_size("seq") // QUAD
    columns = q_weight.shape[1]
    beside = [room(18432)]
    attn_gain = attn_gain.reshape(1, -1)
    mlp_gain = mlp_gain.reshape(1, -1)
    members = lax.axis_size("seq") // 2
    partial_sums = like((members, rows, wide), f32)
    own_columns = like((rows, wide), bf16)

    keys = kv_cache.shape[1]
    held, send = call(
        functools.partial(pack_kernel, outer),
        [like((rows, wide + HEAD_DIM), bf16), like((2 * keys, outer * HEAD_DIM), bf16)],
        [kv_cache, block_mask[:, :, 0], x_rows],
        beside,
    )
    other = swap(send, 2)
    line = stacked(z_swapped([held] * outer), 1)
    routed = call(
        functools.partial(route_kernel, outer),
        [like((4 * keys, HEAD_DIM), bf16)] * outer,
        [kv_cache, other],
        [line, *beside],
    )
    routed = z_routed(routed)
    x_parts = near_gathered(line)
    queries = call(
        functools.partial(query_kernel, outer, wide),
        like((rows, columns), bf16),
        [*x_parts, attn_gain, q_weight],
    )
    cache = stacked(routed, 0, [queries])
    far_cache = swap(cache, 1)
    tall = like((columns // HEAD_DIM * rows, HEAD_DIM), f32)
    early = call(
        functools.partial(early_kernel, outer, wide), [tall] * 3, [queries, cache, *x_parts[0::2]]
    )
    left, send = call(
        functools.partial(attend_kernel, outer, wide),
        [like((rows, columns), bf16), partial_sums],
        [queries, *early, far_cache, *x_parts[1::2], o_weight],
    )
    stream, copies = scattered(
        x_rows, send, left, o_weight, wide, f32, [own_columns, like(partial_sums.shape, bf16)], beside
    )
    parts = to_members(copies)
    left, send = call(
        functools.partial(hidden_kernel, wide),
        [like((rows, gate_weight.shape[1]), bf16), partial_sums],
        [parts, swap(parts, 1), mlp_gain, gate_weight, up_weight, down_weight],
    )
    return scattered(stream, send, left, down_weight, wide, bf16, [own_columns])[0]


def rms_norm(values, gain):
    wide = values.astype(f32)
    inverse = lax.rsqrt(jnp.mean(wide * wide, axis=-1, keepdims=True) + eps)
    return (wide * inverse * gain.astype(f32)).astype(bf16)


def combine_states(first, second):
    top_a, total_a, accum_a = first
    top_b, total_b, accum_b = second
    top = jnp.maximum(top_a, top_b)
    factor_a = jnp.exp(top_a - top)
    factor_b = jnp.exp(top_b - top)
    return (
        top,
        total_a * factor_a + total_b * factor_b,
        accum_a * factor_a[..., None] + accum_b * factor_b[..., None],
    )


def combined_all(x, axis, combine):
    everything = jax.tree.map(lambda part: lax.all_gather(part, axis), x)
    initial = jax.tree.map(lambda part: part[0], everything)

    def turn(k, so_far):
        return combine(so_far, jax.tree.map(lambda part: part[k], everything))

    return lax.fori_loop(1, lax.axis_size(axis), turn, initial)


def summed(weight, left):
    product = lax.dot_general(weight, left, (((0,), (1,)), ((), ())), preferred_element_type=f32)
    return lax.psum_scatter(product, "seq", scatter_dimension=0, tiled=True).T


def local_tokens(
    x_rows, attn_gain, q_weight, o_weight, mlp_gain, gate_weight, up_weight, down_weight, kv_cache, block_mask
):
    rows = x_rows.shape[0]
    group = HEADS // KV_HEADS
    key_len = kv_cache.shape[1]
    spans = key_len // BLOCK
    scale = 1.0 / HEAD_DIM**0.5
    normed = rms_norm(lax.all_gather(x_rows, "seq", axis=1, tiled=True), attn_gain)
    query_part = jnp.dot(normed, q_weight, preferred_element_type=f32).astype(bf16)
    queries = lax.all_gather(query_part, "seq", axis=1, tiled=True)

    def one_group(index):
        def cut(array, width):
            return lax.dynamic_slice_in_dim(array, index * width, width, 1)

        query_group = cut(queries, group * HEAD_DIM).reshape(rows, group, HEAD_DIM)
        scores = (
            jnp.einsum("rhd,kd->rhk", query_group, cut(kv_cache[0], HEAD_DIM), preferred_element_type=f32)
            * scale
        )
        scores = scores.reshape(rows, group, spans, BLOCK)
        live = (cut(block_mask, 1)[:, 0, :] == 1)[:, None, :, None]
        masked = jnp.where(live, scores, floor_score)
        top = jnp.max(masked, axis=(2, 3))
        weights = jnp.where(live, jnp.exp(masked - top[..., None, None]), 0.0)
        rounded = weights.astype(bf16).reshape(rows, group, key_len)
        accum = jnp.einsum("rhk,kd->rhd", rounded, cut(kv_cache[1], HEAD_DIM), preferred_element_type=f32)
        return (top, jnp.sum(weights, axis=(2, 3)), accum)

    states = lax.map(one_group, jnp.arange(KV_HEADS, dtype=jnp.int32))
    states = jax.tree.map(lambda part: jnp.moveaxis(part, 0, 1), states)
    columns = q_weight.shape[1]
    top, total, accum = combined_all(states, "seq", combine_states)
    attended = (accum / total[..., None]).reshape(rows, HEADS * HEAD_DIM).astype(bf16)
    attn_cols = lax.dynamic_slice_in_dim(attended, lax.axis_index("seq") * columns, columns, 1)
    stream = (x_rows.astype(f32) + summed(o_weight, attn_cols)).astype(bf16)
    normed_two = rms_norm(lax.all_gather(stream, "seq", axis=1, tiled=True), mlp_gain)
    gate = jnp.dot(normed_two, gate_weight, preferred_element_type=f32)
    upward = jnp.dot(normed_two, up_weight, preferred_element_type=f32)
    hidden = (jax.nn.silu(gate) * upward).astype(bf16)
    return (stream.astype(f32) + summed(down_weight, hidden)).astype(bf16)


def solution(mesh):
    pairs = mesh.shape["seq"] == 2 * KV_HEADS
    return jax.shard_map(
        local_pairs if pairs else local_tokens,
        mesh=mesh,
        in_specs=(
            P("group", "seq"),
            P(),
            P(None, "seq"),
            P("seq", None),
            P(),
            P(None, "seq"),
            P(None, "seq"),
            P("seq", None),
            P(None, ("group", "seq"), None),
            P("group", None, "seq"),
        ),
        out_specs=P("group", "seq"),
        check_vma=False,
    )
```

```python
import functools

import jax
import jax.numpy as jnp
from jax import lax
from jax.experimental import pallas as pl
from jax.experimental.pallas import tpu as pltpu
from jax.sharding import PartitionSpec as P

HEADS = 64
KV_HEADS = 8
HEAD_DIM = 128
BLOCK = 128
QUAD = 4

eps = 1e-05
floor_score = -1e30

bf16 = jnp.bfloat16
f32 = jnp.float32
VMEM = pl.BlockSpec(memory_space=pltpu.VMEM)


def call(body, outs, ins, beside=(), limit=4 * 2**20):
    count, extra = len(ins), len(beside)

    def kernel(*refs):
        body(*refs[:count], *refs[count + extra :])

    return pl.pallas_call(
        kernel,
        out_shape=outs,
        in_specs=[VMEM] * count + [pl.BlockSpec(memory_space=pl.ANY)] * extra,
        out_specs=jax.tree.map(lambda _: VMEM, outs),
        compiler_params=pltpu.CompilerParams(vmem_limit_bytes=limit),
    )(*ins, *beside)


def room(size):
    return pl.pallas_call(
        lambda out: None,
        out_shape=like((size, 1024), f32),
        out_specs=pl.BlockSpec(memory_space=pl.ANY),
    )()


def like(shape, dtype):
    return jax.ShapeDtypeStruct(shape, dtype)


def swap(x, distance):
    size = lax.axis_size("seq")
    return lax.ppermute(x, "seq", [(i, i ^ distance) for i in range(size)])


def pack_kernel(outer, kv_ref, mask_ref, x_ref, send_ref, *outs):
    me = lax.axis_index("seq")
    z, y = me // QUAD, (me // 2) % 2
    keys = kv_ref.shape[1]
    rows = mask_ref.shape[0]
    pieces = [x_ref[:, at : at + HEAD_DIM] for at in range(0, x_ref.shape[1], HEAD_DIM)]
    lane = lax.broadcasted_iota(jnp.int32, (rows, HEAD_DIM), 1)
    mask = jnp.zeros((rows, HEAD_DIM), f32)
    for head in range(mask_ref.shape[1]):
        live = (mask_ref[:, head : head + 1] == 1).astype(f32)
        mask = jnp.where(lane == head, jnp.broadcast_to(live, mask.shape), mask)
    pieces.append(mask.astype(bf16))
    for k in range(outer):
        peer = jnp.bitwise_xor(z, k)
        cols = pl.ds(pl.multiple_of((2 * peer + y) * HEAD_DIM, HEAD_DIM), HEAD_DIM)
        outs[k][0:keys, :] = kv_ref[0, :, cols]
        for i, piece in enumerate(pieces):
            outs[k][keys + i * rows : keys + (i + 1) * rows, :] = piece
        cols = pl.ds(pl.multiple_of((2 * peer + 1 - y) * HEAD_DIM, HEAD_DIM), HEAD_DIM)
        at = slice(k * HEAD_DIM, (k + 1) * HEAD_DIM)
        send_ref[0:keys, at] = kv_ref[0, :, cols]
        send_ref[keys : 2 * keys, at] = kv_ref[1, :, cols]


def unpack_kernel(keys, *refs):
    line_ref = refs[-1]
    rows = line_ref.shape[0]
    at = 0
    for ref in refs[:-1]:
        for i in range((ref.shape[0] - keys) // rows):
            line_ref[:, at : at + HEAD_DIM] = ref[keys + i * rows : keys + (i + 1) * rows, :]
            at += HEAD_DIM


def z_slots(outer):
    order = list(range(outer - 1, 0, -1))
    return list(zip([0, *order[-1:], *order[:-1]], [0, *order]))


def z_distance(slot, core):
    return jnp.where(core == 0, slot[0], slot[1])


def route_kernel(outer, kv_ref, other_ref, *outs):
    me = lax.axis_index("seq")
    z, y = me // QUAD, (me // 2) % 2
    keys = kv_ref.shape[1]
    for slot, out in zip(z_slots(outer), outs):
        k = z_distance(slot, me % 2)
        head = 2 * jnp.bitwise_xor(z, k) + y
        cols = pl.ds(pl.multiple_of(head * HEAD_DIM, HEAD_DIM), HEAD_DIM)
        out[0:keys, :] = kv_ref[1, :, cols]
        out[keys:, :] = other_ref[:, pl.ds(pl.multiple_of(k * HEAD_DIM, HEAD_DIM), HEAD_DIM)]


def cache_kernel(outer, keys, *refs):
    firsts, rests, out_ref = refs[:outer], refs[outer : 2 * outer], refs[2 * outer]
    core = lax.axis_index("seq") % 2
    for i, slot in enumerate(z_slots(outer)):
        at = 4 * i * keys
        for at_core in range(2):

            @pl.when(core == at_core)
            def _():
                out_ref[at : at + keys, :] = firsts[slot[at_core]][0:keys, :]

        out_ref[at + keys : at + 4 * keys, :] = rests[i][...]


def stack_kernel(axis, *refs):
    at = 0
    for ref in refs[:-1]:
        size = ref.shape[axis]
        if axis == 0:
            refs[-1][at : at + size, :] = ref[...]
        else:
            refs[-1][:, at : at + size] = ref[...]
        at += size


def stacked(parts, axis, beside=()):
    shape = list(parts[0].shape)
    shape[axis] = sum(p.shape[axis] for p in parts)
    return call(functools.partial(stack_kernel, axis), like(tuple(shape), parts[0].dtype), parts, beside)


def normed_chunks(wide, chunks, gain_ref):
    squares = None
    for source, load in chunks:
        v = load().astype(f32)
        s = jnp.sum(v * v, axis=1, keepdims=True)
        squares = s if squares is None else squares + s
    inverse = lax.rsqrt(squares / (len(chunks) * wide) + eps)
    for source, load in chunks:
        at = pl.ds(pl.multiple_of(source * wide, wide), wide)
        yield at, (load().astype(f32) * inverse * gain_ref[:, at].astype(f32)).astype(bf16)


def to_members(parts):
    size = lax.axis_size("seq")
    groups = [list(range(core, size, 2)) for core in range(2)]
    return lax.all_to_all(parts, "seq", 0, 0, axis_index_groups=groups, tiled=True)


def member(i, other):
    core = lax.axis_index("seq") % 2
    return 2 * i + (1 - core if other else core)


def line_of(outer, *nears):
    return [QUAD * k + j for j in nears for k in range(outer)]


def line_chunks(outer, wide, refs):
    me = lax.axis_index("seq")
    lines = [line_of(outer, near) for near in range(QUAD)]
    step = wide + HEAD_DIM
    return [
        (jnp.bitwise_xor(me, distance), lambda r=ref, i=i: r[:, i * step : i * step + wide])
        for ref, line in zip(refs, lines)
        for i, distance in enumerate(line)
    ]


def line_mask(wide, ref, i):
    at = pl.multiple_of(i * (wide + HEAD_DIM) + wide, HEAD_DIM)
    tile = ref[:, pl.ds(at, HEAD_DIM)].astype(f32)
    lane = lax.broadcasted_iota(jnp.int32, tile.shape, 1)
    mine = jnp.where(lane == lax.axis_index("seq") // 2, tile, 0.0)
    return jnp.broadcast_to(jnp.sum(mine, axis=1, keepdims=True), tile.shape)


def member_chunks(refs):
    return [
        (member(i, other), lambda r=ref, i=i: r[i])
        for other, ref in enumerate(refs)
        for i in range(ref.shape[0])
    ]


def query_kernel(outer, wide, *refs):
    gain_ref, w_ref, out_ref = refs[QUAD:]
    total = None
    for at, chunk in normed_chunks(wide, line_chunks(outer, wide, refs[:QUAD]), gain_ref):
        term = jnp.dot(chunk, w_ref[at, :], preferred_element_type=f32)
        total = term if total is None else total + term
    out_ref[...] = total.astype(bf16)


def scatter_dot(wide, other, left, w_ref, out_ref):
    for i in range(out_ref.shape[0]):
        at = pl.ds(pl.multiple_of(member(i, other) * wide, wide), wide)
        out_ref[i] = jnp.dot(left, w_ref[:, at], preferred_element_type=f32)


def keep_kernel(wide, left_ref, w_ref, out_ref):
    scatter_dot(wide, False, left_ref[...], w_ref, out_ref)


def span_states(q_ref, cache_ref, masks):
    heads = q_ref.shape[1] // HEAD_DIM
    scale = 1.0 / HEAD_DIM**0.5
    keys = cache_ref.shape[0] // (2 * len(masks))
    queries = jnp.concatenate(
        [q_ref[:, h * HEAD_DIM : (h + 1) * HEAD_DIM] for h in range(heads)], axis=0
    )
    scores = [
        lax.dot_general(
            queries,
            cache_ref[2 * i * keys : (2 * i + 1) * keys, :],
            (((1,), (1,)), ((), ())),
            preferred_element_type=f32,
        )
        * scale
        for i in range(len(masks))
    ]
    lives = [jnp.concatenate([mask] * heads, axis=0) > 0.5 for mask in masks]
    scores = [jnp.where(live, score, floor_score) for live, score in zip(lives, scores)]
    tops = [jnp.max(score, axis=1, keepdims=True) for score in scores]
    weights = [
        jnp.where(live, jnp.exp(score - top), 0.0) for live, score, top in zip(lives, scores, tops)
    ]
    totals = [jnp.sum(weight, axis=1, keepdims=True) for weight in weights]
    accums = [
        jnp.dot(
            weight.astype(bf16),
            cache_ref[(2 * i + 1) * keys : (2 * i + 2) * keys, :],
            preferred_element_type=f32,
        )
        for i, weight in enumerate(weights)
    ]
    return list(zip(tops, totals, accums))


def combined(states):
    top = functools.reduce(jnp.maximum, [s[0] for s in states])
    total = accum = None
    for t, s, a in states:
        factor = jnp.exp(t - top)
        total = s * factor if total is None else total + s * factor
        accum = a * factor if accum is None else accum + a * factor
    return top, total, accum


def early_kernel(outer, wide, q_ref, cache_ref, line_ref, other_ref, top_ref, total_ref, accum_ref):
    core = lax.axis_index("seq") % 2
    masks = [
        line_mask(wide, ref, z_distance(slot, core))
        for slot in z_slots(outer)
        for ref in (line_ref, other_ref)
    ]
    top, total, accum_ref[...] = combined(span_states(q_ref, cache_ref, masks))
    top_ref[...] = jnp.broadcast_to(top, top_ref.shape)
    total_ref[...] = jnp.broadcast_to(total, total_ref.shape)


def attend_kernel(
    outer, wide, q_ref, top_ref, total_ref, accum_ref, cache_ref, core_ref, far_ref, w_ref, left_ref, send_ref
):
    rows = q_ref.shape[0]
    heads = q_ref.shape[1] // HEAD_DIM
    core = 1 - lax.axis_index("seq") % 2
    masks = [
        line_mask(wide, ref, z_distance(slot, core))
        for slot in z_slots(outer)
        for ref in (core_ref, far_ref)
    ]
    states = span_states(q_ref, cache_ref, masks)
    states.append((top_ref[:, 0:1], total_ref[:, 0:1], accum_ref[...]))
    _, total, accum = combined(states)
    attended = (accum / total).astype(bf16)
    attended = jnp.concatenate([attended[h * rows : (h + 1) * rows] for h in range(heads)], axis=1)
    left_ref[...] = attended
    scatter_dot(wide, True, attended, w_ref, send_ref)


def hidden_kernel(wide, *refs):
    gain_ref, gate_ref, up_ref, down_ref, left_ref, send_ref = refs[2:]
    gate = up = None
    for at, chunk in normed_chunks(wide, member_chunks(refs[:2]), gain_ref):
        g = jnp.dot(chunk, gate_ref[at, :], preferred_element_type=f32)
        u = jnp.dot(chunk, up_ref[at, :], preferred_element_type=f32)
        gate = g if gate is None else gate + g
        up = u if up is None else up + u
    hidden = (gate / (1.0 + jnp.exp(-gate)) * up).astype(bf16)
    left_ref[...] = hidden
    scatter_dot(wide, True, hidden, down_ref, send_ref)


def add_kernel(own_ref, recv_ref, out_ref):
    out_ref[...] = (own_ref[...] + recv_ref[...]).astype(out_ref.dtype)


def final_kernel(base_ref, parts_ref, *out_refs):
    total = parts_ref[0].astype(f32)
    for i in range(1, parts_ref.shape[0]):
        total = total + parts_ref[i].astype(f32)
    total = (base_ref[...].astype(f32) + total).astype(bf16)
    for out in out_refs:
        if len(out.shape) == 3:
            for i in range(out.shape[0]):
                out[i] = total
        else:
            out[...] = total


def z_swapped(parts):
    arrived = [swap(part, QUAD * k) for k, part in reversed(list(enumerate(parts))) if k > 0]
    return [parts[0], *reversed(arrived)]


def z_routed(parts):
    size = lax.axis_size("seq")
    return [parts[0]] + [
        lax.ppermute(part, "seq", [(i, i ^ QUAD * slot[i % 2]) for i in range(size)])
        for slot, part in list(zip(z_slots(len(parts)), parts))[1:]
    ]


def near_gathered(line):
    far, y, core = swap(line, 3), swap(line, 2), swap(line, 1)
    return [line, core, y, far]


def scattered(base, send, left, weight, wide, kind, outs, beside=()):
    far = swap(send, 1)
    own = call(functools.partial(keep_kernel, wide), like(send.shape, f32), [left, weight])
    sums = call(add_kernel, like(send.shape, kind), [own, far], beside)
    return call(final_kernel, outs, [base, to_members(sums)], beside)


def local_pairs(
    x_rows, attn_gain, q_weight, o_weight, mlp_gain, gate_weight, up_weight, down_weight, kv_cache, block_mask
):
    rows, wide = x_rows.shape
    outer = lax.axis_size("seq") // QUAD
    columns = q_weight.shape[1]
    beside = [room(18432)]
    attn_gain = attn_gain.reshape(1, -1)
    mlp_gain = mlp_gain.reshape(1, -1)
    members = lax.axis_size("seq") // 2
    partial_sums = like((members, rows, wide), f32)
    own_columns = like((rows, wide), bf16)

    keys = kv_cache.shape[1]
    step = wide + HEAD_DIM
    send, *firsts = call(
        functools.partial(pack_kernel, outer),
        [like((2 * keys, outer * HEAD_DIM), bf16)]
        + [like((keys + step // HEAD_DIM * rows, HEAD_DIM), bf16)] * outer,
        [kv_cache, block_mask[:, :, 0], x_rows],
        beside,
    )
    other = swap(send, 2)
    firsts = z_swapped(firsts)
    line = call(functools.partial(unpack_kernel, keys), like((rows, outer * step), bf16), firsts)
    routed = call(
        functools.partial(route_kernel, outer),
        [like((3 * keys, HEAD_DIM), bf16)] * outer,
        [kv_cache, other],
        [line, *beside],
    )
    routed = z_routed(routed)
    x_parts = near_gathered(line)
    queries = call(
        functools.partial(query_kernel, outer, wide),
        like((rows, columns), bf16),
        [*x_parts, attn_gain, q_weight],
    )
    cache = call(
        functools.partial(cache_kernel, outer, keys),
        like((4 * outer * keys, HEAD_DIM), bf16),
        [*firsts, *routed],
        [queries],
    )
    far_cache = swap(cache, 1)
    tall = like((columns // HEAD_DIM * rows, HEAD_DIM), f32)
    early = call(
        functools.partial(early_kernel, outer, wide), [tall] * 3, [queries, cache, *x_parts[0::2]]
    )
    left, send = call(
        functools.partial(attend_kernel, outer, wide),
        [like((rows, columns), bf16), partial_sums],
        [queries, *early, far_cache, *x_parts[1::2], o_weight],
    )
    stream, copies = scattered(
        x_rows, send, left, o_weight, wide, f32, [own_columns, like(partial_sums.shape, bf16)], beside
    )
    parts = to_members(copies)
    left, send = call(
        functools.partial(hidden_kernel, wide),
        [like((rows, gate_weight.shape[1]), bf16), partial_sums],
        [parts, swap(parts, 1), mlp_gain, gate_weight, up_weight, down_weight],
    )
    return scattered(stream, send, left, down_weight, wide, bf16, [own_columns])[0]


def rms_norm(values, gain):
    wide = values.astype(f32)
    inverse = lax.rsqrt(jnp.mean(wide * wide, axis=-1, keepdims=True) + eps)
    return (wide * inverse * gain.astype(f32)).astype(bf16)


def combine_states(first, second):
    top_a, total_a, accum_a = first
    top_b, total_b, accum_b = second
    top = jnp.maximum(top_a, top_b)
    factor_a = jnp.exp(top_a - top)
    factor_b = jnp.exp(top_b - top)
    return (
        top,
        total_a * factor_a + total_b * factor_b,
        accum_a * factor_a[..., None] + accum_b * factor_b[..., None],
    )


def combined_all(x, axis, combine):
    everything = jax.tree.map(lambda part: lax.all_gather(part, axis), x)
    initial = jax.tree.map(lambda part: part[0], everything)

    def turn(k, so_far):
        return combine(so_far, jax.tree.map(lambda part: part[k], everything))

    return lax.fori_loop(1, lax.axis_size(axis), turn, initial)


def summed(weight, left):
    product = lax.dot_general(weight, left, (((0,), (1,)), ((), ())), preferred_element_type=f32)
    return lax.psum_scatter(product, "seq", scatter_dimension=0, tiled=True).T


def local_tokens(
    x_rows, attn_gain, q_weight, o_weight, mlp_gain, gate_weight, up_weight, down_weight, kv_cache, block_mask
):
    rows = x_rows.shape[0]
    group = HEADS // KV_HEADS
    key_len = kv_cache.shape[1]
    spans = key_len // BLOCK
    scale = 1.0 / HEAD_DIM**0.5
    normed = rms_norm(lax.all_gather(x_rows, "seq", axis=1, tiled=True), attn_gain)
    query_part = jnp.dot(normed, q_weight, preferred_element_type=f32).astype(bf16)
    queries = lax.all_gather(query_part, "seq", axis=1, tiled=True)

    def one_group(index):
        def cut(array, width):
            return lax.dynamic_slice_in_dim(array, index * width, width, 1)

        query_group = cut(queries, group * HEAD_DIM).reshape(rows, group, HEAD_DIM)
        scores = (
            jnp.einsum("rhd,kd->rhk", query_group, cut(kv_cache[0], HEAD_DIM), preferred_element_type=f32)
            * scale
        )
        scores = scores.reshape(rows, group, spans, BLOCK)
        live = (cut(block_mask, 1)[:, 0, :] == 1)[:, None, :, None]
        masked = jnp.where(live, scores, floor_score)
        top = jnp.max(masked, axis=(2, 3))
        weights = jnp.where(live, jnp.exp(masked - top[..., None, None]), 0.0)
        rounded = weights.astype(bf16).reshape(rows, group, key_len)
        accum = jnp.einsum("rhk,kd->rhd", rounded, cut(kv_cache[1], HEAD_DIM), preferred_element_type=f32)
        return (top, jnp.sum(weights, axis=(2, 3)), accum)

    states = lax.map(one_group, jnp.arange(KV_HEADS, dtype=jnp.int32))
    states = jax.tree.map(lambda part: jnp.moveaxis(part, 0, 1), states)
    columns = q_weight.shape[1]
    top, total, accum = combined_all(states, "seq", combine_states)
    attended = (accum / total[..., None]).reshape(rows, HEADS * HEAD_DIM).astype(bf16)
    attn_cols = lax.dynamic_slice_in_dim(attended, lax.axis_index("seq") * columns, columns, 1)
    stream = (x_rows.astype(f32) + summed(o_weight, attn_cols)).astype(bf16)
    normed_two = rms_norm(lax.all_gather(stream, "seq", axis=1, tiled=True), mlp_gain)
    gate = jnp.dot(normed_two, gate_weight, preferred_element_type=f32)
    upward = jnp.dot(normed_two, up_weight, preferred_element_type=f32)
    hidden = (jax.nn.silu(gate) * upward).astype(bf16)
    return (stream.astype(f32) + summed(down_weight, hidden)).astype(bf16)


def solution(mesh):
    pairs = mesh.shape["seq"] == 2 * KV_HEADS
    return jax.shard_map(
        local_pairs if pairs else local_tokens,
        mesh=mesh,
        in_specs=(
            P("group", "seq"),
            P(),
            P(None, "seq"),
            P("seq", None),
            P(),
            P(None, "seq"),
            P(None, "seq"),
            P("seq", None),
            P(None, ("group", "seq"), None),
            P("group", None, "seq"),
        ),
        out_specs=P("group", "seq"),
        check_vma=False,
    )
```

```python
import functools

import jax
import jax.numpy as jnp
from jax import lax
from jax.experimental import pallas as pl
from jax.experimental.pallas import tpu as pltpu
from jax.sharding import PartitionSpec as P

HEADS = 64
KV_HEADS = 8
HEAD_DIM = 128
BLOCK = 128
QUAD = 4
RANGE = 32000.0
STEPS = 256.0

eps = 1e-05
floor_score = -1e30

bf16 = jnp.bfloat16
f32 = jnp.float32
VMEM = pl.BlockSpec(memory_space=pltpu.VMEM)


def call(body, outs, ins, beside=(), limit=4 * 2**20):
    count, extra = len(ins), len(beside)

    def kernel(*refs):
        body(*refs[:count], *refs[count + extra :])

    return pl.pallas_call(
        kernel,
        out_shape=outs,
        in_specs=[VMEM] * count + [pl.BlockSpec(memory_space=pl.ANY)] * extra,
        out_specs=jax.tree.map(lambda _: VMEM, outs),
        compiler_params=pltpu.CompilerParams(vmem_limit_bytes=limit),
    )(*ins, *beside)


def room(size):
    return pl.pallas_call(
        lambda out: None,
        out_shape=like((size, 1024), f32),
        out_specs=pl.BlockSpec(memory_space=pl.ANY),
    )()


def like(shape, dtype):
    return jax.ShapeDtypeStruct(shape, dtype)


def swap(x, distance):
    size = lax.axis_size("seq")
    return lax.ppermute(x, "seq", [(i, i ^ distance) for i in range(size)])


def pack_kernel(outer, kv_ref, mask_ref, x_ref, send_ref, *outs):
    me = lax.axis_index("seq")
    z, y = me // QUAD, (me // 2) % 2
    keys = kv_ref.shape[1]
    rows = mask_ref.shape[0]
    pieces = [x_ref[:, at : at + HEAD_DIM] for at in range(0, x_ref.shape[1], HEAD_DIM)]
    lane = lax.broadcasted_iota(jnp.int32, (rows, HEAD_DIM), 1)
    mask = jnp.zeros((rows, HEAD_DIM), f32)
    for head in range(mask_ref.shape[1]):
        live = (mask_ref[:, head : head + 1] == 1).astype(f32)
        mask = jnp.where(lane == head, jnp.broadcast_to(live, mask.shape), mask)
    pieces.append(mask.astype(bf16))
    for k in range(outer):
        peer = jnp.bitwise_xor(z, k)
        cols = pl.ds(pl.multiple_of((2 * peer + y) * HEAD_DIM, HEAD_DIM), HEAD_DIM)
        outs[k][0:keys, :] = kv_ref[0, :, cols]
        for i, piece in enumerate(pieces):
            outs[k][keys + i * rows : keys + (i + 1) * rows, :] = piece
        cols = pl.ds(pl.multiple_of((2 * peer + 1 - y) * HEAD_DIM, HEAD_DIM), HEAD_DIM)
        at = slice(k * HEAD_DIM, (k + 1) * HEAD_DIM)
        send_ref[0:keys, at] = kv_ref[0, :, cols]
        send_ref[keys : 2 * keys, at] = kv_ref[1, :, cols]


def unpack_kernel(keys, *refs):
    line_ref = refs[-1]
    rows = line_ref.shape[0]
    at = 0
    for ref in refs[:-1]:
        for i in range((ref.shape[0] - keys) // rows):
            line_ref[:, at : at + HEAD_DIM] = ref[keys + i * rows : keys + (i + 1) * rows, :]
            at += HEAD_DIM


def z_slots(outer):
    order = list(range(outer - 1, 0, -1))
    return list(zip([0, *order[-1:], *order[:-1]], [0, *order]))


def z_distance(slot, core):
    return jnp.where(core == 0, slot[0], slot[1])


def route_kernel(outer, kv_ref, other_ref, *outs):
    me = lax.axis_index("seq")
    z, y = me // QUAD, (me // 2) % 2
    keys = kv_ref.shape[1]
    for slot, out in zip(z_slots(outer), outs):
        k = z_distance(slot, me % 2)
        head = 2 * jnp.bitwise_xor(z, k) + y
        cols = pl.ds(pl.multiple_of(head * HEAD_DIM, HEAD_DIM), HEAD_DIM)
        out[0:keys, :] = kv_ref[1, :, cols]
        out[keys:, :] = other_ref[:, pl.ds(pl.multiple_of(k * HEAD_DIM, HEAD_DIM), HEAD_DIM)]


def cache_kernel(outer, keys, *refs):
    firsts, rests, out_ref = refs[:outer], refs[outer : 2 * outer], refs[2 * outer]
    core = lax.axis_index("seq") % 2
    for i, slot in enumerate(z_slots(outer)):
        at = 4 * i * keys
        for at_core in range(2):

            @pl.when(core == at_core)
            def _():
                out_ref[at : at + keys, :] = firsts[slot[at_core]][0:keys, :]

        out_ref[at + keys : at + 4 * keys, :] = rests[i][...]


def stack_kernel(axis, *refs):
    at = 0
    for ref in refs[:-1]:
        size = ref.shape[axis]
        if axis == 0:
            refs[-1][at : at + size, :] = ref[...]
        else:
            refs[-1][:, at : at + size] = ref[...]
        at += size


def stacked(parts, axis, beside=()):
    shape = list(parts[0].shape)
    shape[axis] = sum(p.shape[axis] for p in parts)
    return call(functools.partial(stack_kernel, axis), like(tuple(shape), parts[0].dtype), parts, beside)


def normed_chunks(wide, chunks, gain_ref):
    squares = None
    for source, load in chunks:
        v = load().astype(f32)
        s = jnp.sum(v * v, axis=1, keepdims=True)
        squares = s if squares is None else squares + s
    inverse = lax.rsqrt(squares / (len(chunks) * wide) + eps)
    for source, load in chunks:
        at = pl.ds(pl.multiple_of(source * wide, wide), wide)
        yield at, (load().astype(f32) * inverse * gain_ref[:, at].astype(f32)).astype(bf16)


def to_members(parts):
    size = lax.axis_size("seq")
    groups = [list(range(core, size, 2)) for core in range(2)]
    return lax.all_to_all(parts, "seq", 0, 0, axis_index_groups=groups, tiled=True)


def member(i, other):
    core = lax.axis_index("seq") % 2
    return 2 * i + (1 - core if other else core)


def line_of(outer, *nears):
    return [QUAD * k + j for j in nears for k in range(outer)]


def line_chunks(outer, wide, refs):
    me = lax.axis_index("seq")
    lines = [line_of(outer, near) for near in range(QUAD)]
    step = wide + HEAD_DIM
    return [
        (jnp.bitwise_xor(me, distance), lambda r=ref, i=i: r[:, i * step : i * step + wide])
        for ref, line in zip(refs, lines)
        for i, distance in enumerate(line)
    ]


def line_mask(wide, ref, i):
    at = pl.multiple_of(i * (wide + HEAD_DIM) + wide, HEAD_DIM)
    tile = ref[:, pl.ds(at, HEAD_DIM)].astype(f32)
    lane = lax.broadcasted_iota(jnp.int32, tile.shape, 1)
    mine = jnp.where(lane == lax.axis_index("seq") // 2, tile, 0.0)
    return jnp.broadcast_to(jnp.sum(mine, axis=1, keepdims=True), tile.shape)


def member_chunks(refs):
    return [
        (member(i, other), lambda r=ref, i=i: r[i])
        for other, ref in enumerate(refs)
        for i in range(ref.shape[0])
    ]


def query_kernel(outer, wide, *refs):
    gain_ref, w_ref, out_ref = refs[QUAD:]
    total = None
    for at, chunk in normed_chunks(wide, line_chunks(outer, wide, refs[:QUAD]), gain_ref):
        term = jnp.dot(chunk, w_ref[at, :], preferred_element_type=f32)
        total = term if total is None else total + term
    out_ref[...] = total.astype(bf16)


def scatter_dot(wide, other, left, w_ref, out_ref):
    for i in range(out_ref.shape[0]):
        at = pl.ds(pl.multiple_of(member(i, other) * wide, wide), wide)
        out_ref[i] = jnp.dot(left, w_ref[:, at], preferred_element_type=f32)


def keep_kernel(wide, left_ref, w_ref, out_ref):
    scatter_dot(wide, False, left_ref[...], w_ref, out_ref)


def span_states(q_ref, cache_ref, masks):
    heads = q_ref.shape[1] // HEAD_DIM
    scale = 1.0 / HEAD_DIM**0.5
    keys = cache_ref.shape[0] // (2 * len(masks))
    queries = jnp.concatenate(
        [q_ref[:, h * HEAD_DIM : (h + 1) * HEAD_DIM] for h in range(heads)], axis=0
    )
    scores = [
        lax.dot_general(
            queries,
            cache_ref[2 * i * keys : (2 * i + 1) * keys, :],
            (((1,), (1,)), ((), ())),
            preferred_element_type=f32,
        )
        * scale
        for i in range(len(masks))
    ]
    lives = [jnp.concatenate([mask] * heads, axis=0) > 0.5 for mask in masks]
    scores = [jnp.where(live, score, floor_score) for live, score in zip(lives, scores)]
    tops = [jnp.max(score, axis=1, keepdims=True) for score in scores]
    weights = [
        jnp.where(live, jnp.exp(score - top), 0.0) for live, score, top in zip(lives, scores, tops)
    ]
    totals = [jnp.sum(weight, axis=1, keepdims=True) for weight in weights]
    accums = [
        jnp.dot(
            weight.astype(bf16),
            cache_ref[(2 * i + 1) * keys : (2 * i + 2) * keys, :],
            preferred_element_type=f32,
        )
        for i, weight in enumerate(weights)
    ]
    return list(zip(tops, totals, accums))


def combined(states):
    top = functools.reduce(jnp.maximum, [s[0] for s in states])
    total = accum = None
    for t, s, a in states:
        factor = jnp.exp(t - top)
        total = s * factor if total is None else total + s * factor
        accum = a * factor if accum is None else accum + a * factor
    return top, total, accum


def early_kernel(outer, wide, q_ref, cache_ref, line_ref, other_ref, top_ref, total_ref, accum_ref):
    core = lax.axis_index("seq") % 2
    masks = [
        line_mask(wide, ref, z_distance(slot, core))
        for slot in z_slots(outer)
        for ref in (line_ref, other_ref)
    ]
    top, total, accum_ref[...] = combined(span_states(q_ref, cache_ref, masks))
    top_ref[...] = jnp.broadcast_to(top, top_ref.shape)
    total_ref[...] = jnp.broadcast_to(total, total_ref.shape)


def attend_kernel(
    outer, wide, q_ref, top_ref, total_ref, accum_ref, cache_ref, core_ref, far_ref, w_ref, left_ref, send_ref
):
    rows = q_ref.shape[0]
    heads = q_ref.shape[1] // HEAD_DIM
    core = 1 - lax.axis_index("seq") % 2
    masks = [
        line_mask(wide, ref, z_distance(slot, core))
        for slot in z_slots(outer)
        for ref in (core_ref, far_ref)
    ]
    states = span_states(q_ref, cache_ref, masks)
    states.append((top_ref[:, 0:1], total_ref[:, 0:1], accum_ref[...]))
    _, total, accum = combined(states)
    attended = (accum / total).astype(bf16)
    attended = jnp.concatenate([attended[h * rows : (h + 1) * rows] for h in range(heads)], axis=1)
    left_ref[...] = attended
    scatter_dot(wide, True, attended, w_ref, send_ref)


def hidden_kernel(wide, *refs):
    gain_ref, gate_ref, up_ref, down_ref, left_ref, send_ref = refs[2:]
    gate = up = None
    for at, chunk in normed_chunks(wide, member_chunks(refs[:2]), gain_ref):
        g = jnp.dot(chunk, gate_ref[at, :], preferred_element_type=f32)
        u = jnp.dot(chunk, up_ref[at, :], preferred_element_type=f32)
        gate = g if gate is None else gate + g
        up = u if up is None else up + u
    hidden = (gate / (1.0 + jnp.exp(-gate)) * up).astype(bf16)
    left_ref[...] = hidden
    scatter_dot(wide, True, hidden, down_ref, send_ref)


def add_kernel(own_ref, recv_ref, out_ref):
    out_ref[...] = (own_ref[...] + recv_ref[...]).astype(out_ref.dtype)


def code_kernel(own_ref, recv_ref, out_ref):
    members, rows, wide = own_ref.shape
    sums = [own_ref[i] + recv_ref[i] for i in range(members)]
    largest = functools.reduce(jnp.maximum, [jnp.max(jnp.abs(s), axis=1, keepdims=True) for s in sums])
    level = jnp.ceil(jnp.log(jnp.maximum(largest, 1e-30)) * STEPS)
    scale = jnp.exp(level * (-1.0 / STEPS)) * RANGE
    level = jnp.broadcast_to(level, (rows, HEAD_DIM)).astype(jnp.int32).astype(jnp.int16)
    for i, s in enumerate(sums):
        out_ref[i, :, 0:wide] = jnp.round(s * scale).astype(jnp.int32).astype(jnp.int16)
        out_ref[i, :, wide:] = level


def decoded(ref, i, wide):
    level = ref[i, :, wide:].astype(jnp.int32).astype(f32)[:, 0:1]
    scale = jnp.exp(level * (1.0 / STEPS)) * (1.0 / RANGE)
    return ref[i, :, 0:wide].astype(jnp.int32).astype(f32) * scale


def final_kernel(base_ref, parts_ref, *out_refs):
    wide = base_ref.shape[1]
    load = lambda i: parts_ref[i].astype(f32)
    if parts_ref.dtype == jnp.int16:
        load = lambda i: decoded(parts_ref, i, wide)
    total = load(0)
    for i in range(1, parts_ref.shape[0]):
        total = total + load(i)
    total = (base_ref[...].astype(f32) + total).astype(bf16)
    for out in out_refs:
        if len(out.shape) == 3:
            for i in range(out.shape[0]):
                out[i] = total
        else:
            out[...] = total


def z_swapped(parts):
    arrived = [swap(part, QUAD * k) for k, part in reversed(list(enumerate(parts))) if k > 0]
    return [parts[0], *reversed(arrived)]


def z_routed(parts):
    size = lax.axis_size("seq")
    return [parts[0]] + [
        lax.ppermute(part, "seq", [(i, i ^ QUAD * slot[i % 2]) for i in range(size)])
        for slot, part in list(zip(z_slots(len(parts)), parts))[1:]
    ]


def near_gathered(line):
    far, y, core = swap(line, 3), swap(line, 2), swap(line, 1)
    return [line, core, y, far]


def scattered(base, send, left, weight, wide, kind, outs, beside=()):
    far = swap(send, 1)
    own = call(functools.partial(keep_kernel, wide), like(send.shape, f32), [left, weight])
    if kind == jnp.int16:
        members, rows, _ = send.shape
        sums = call(code_kernel, like((members, rows, wide + HEAD_DIM), kind), [own, far], beside)
    else:
        sums = call(add_kernel, like(send.shape, kind), [own, far], beside)
    return call(final_kernel, outs, [base, to_members(sums)], beside)


def local_pairs(
    x_rows, attn_gain, q_weight, o_weight, mlp_gain, gate_weight, up_weight, down_weight, kv_cache, block_mask
):
    rows, wide = x_rows.shape
    outer = lax.axis_size("seq") // QUAD
    columns = q_weight.shape[1]
    beside = [room(18432)]
    attn_gain = attn_gain.reshape(1, -1)
    mlp_gain = mlp_gain.reshape(1, -1)
    members = lax.axis_size("seq") // 2
    partial_sums = like((members, rows, wide), f32)
    own_columns = like((rows, wide), bf16)

    keys = kv_cache.shape[1]
    step = wide + HEAD_DIM
    send, *firsts = call(
        functools.partial(pack_kernel, outer),
        [like((2 * keys, outer * HEAD_DIM), bf16)]
        + [like((keys + step // HEAD_DIM * rows, HEAD_DIM), bf16)] * outer,
        [kv_cache, block_mask[:, :, 0], x_rows],
        beside,
    )
    other = swap(send, 2)
    firsts = z_swapped(firsts)
    line = call(functools.partial(unpack_kernel, keys), like((rows, outer * step), bf16), firsts)
    routed = call(
        functools.partial(route_kernel, outer),
        [like((3 * keys, HEAD_DIM), bf16)] * outer,
        [kv_cache, other],
        [line, *beside],
    )
    routed = z_routed(routed)
    x_parts = near_gathered(line)
    queries = call(
        functools.partial(query_kernel, outer, wide),
        like((rows, columns), bf16),
        [*x_parts, attn_gain, q_weight],
    )
    cache = call(
        functools.partial(cache_kernel, outer, keys),
        like((4 * outer * keys, HEAD_DIM), bf16),
        [*firsts, *routed],
        [queries],
    )
    far_cache = swap(cache, 1)
    tall = like((columns // HEAD_DIM * rows, HEAD_DIM), f32)
    early = call(
        functools.partial(early_kernel, outer, wide), [tall] * 3, [queries, cache, *x_parts[0::2]]
    )
    left, send = call(
        functools.partial(attend_kernel, outer, wide),
        [like((rows, columns), bf16), partial_sums],
        [queries, *early, far_cache, *x_parts[1::2], o_weight],
    )
    stream, copies = scattered(
        x_rows, send, left, o_weight, wide, jnp.int16, [own_columns, like(partial_sums.shape, bf16)], beside
    )
    parts = to_members(copies)
    left, send = call(
        functools.partial(hidden_kernel, wide),
        [like((rows, gate_weight.shape[1]), bf16), partial_sums],
        [parts, swap(parts, 1), mlp_gain, gate_weight, up_weight, down_weight],
    )
    return scattered(stream, send, left, down_weight, wide, bf16, [own_columns])[0]


def rms_norm(values, gain):
    wide = values.astype(f32)
    inverse = lax.rsqrt(jnp.mean(wide * wide, axis=-1, keepdims=True) + eps)
    return (wide * inverse * gain.astype(f32)).astype(bf16)


def combine_states(first, second):
    top_a, total_a, accum_a = first
    top_b, total_b, accum_b = second
    top = jnp.maximum(top_a, top_b)
    factor_a = jnp.exp(top_a - top)
    factor_b = jnp.exp(top_b - top)
    return (
        top,
        total_a * factor_a + total_b * factor_b,
        accum_a * factor_a[..., None] + accum_b * factor_b[..., None],
    )


def combined_all(x, axis, combine):
    everything = jax.tree.map(lambda part: lax.all_gather(part, axis), x)
    initial = jax.tree.map(lambda part: part[0], everything)

    def turn(k, so_far):
        return combine(so_far, jax.tree.map(lambda part: part[k], everything))

    return lax.fori_loop(1, lax.axis_size(axis), turn, initial)


def summed(weight, left):
    product = lax.dot_general(weight, left, (((0,), (1,)), ((), ())), preferred_element_type=f32)
    return lax.psum_scatter(product, "seq", scatter_dimension=0, tiled=True).T


def local_tokens(
    x_rows, attn_gain, q_weight, o_weight, mlp_gain, gate_weight, up_weight, down_weight, kv_cache, block_mask
):
    rows = x_rows.shape[0]
    group = HEADS // KV_HEADS
    key_len = kv_cache.shape[1]
    spans = key_len // BLOCK
    scale = 1.0 / HEAD_DIM**0.5
    normed = rms_norm(lax.all_gather(x_rows, "seq", axis=1, tiled=True), attn_gain)
    query_part = jnp.dot(normed, q_weight, preferred_element_type=f32).astype(bf16)
    queries = lax.all_gather(query_part, "seq", axis=1, tiled=True)

    def one_group(index):
        def cut(array, width):
            return lax.dynamic_slice_in_dim(array, index * width, width, 1)

        query_group = cut(queries, group * HEAD_DIM).reshape(rows, group, HEAD_DIM)
        scores = (
            jnp.einsum("rhd,kd->rhk", query_group, cut(kv_cache[0], HEAD_DIM), preferred_element_type=f32)
            * scale
        )
        scores = scores.reshape(rows, group, spans, BLOCK)
        live = (cut(block_mask, 1)[:, 0, :] == 1)[:, None, :, None]
        masked = jnp.where(live, scores, floor_score)
        top = jnp.max(masked, axis=(2, 3))
        weights = jnp.where(live, jnp.exp(masked - top[..., None, None]), 0.0)
        rounded = weights.astype(bf16).reshape(rows, group, key_len)
        accum = jnp.einsum("rhk,kd->rhd", rounded, cut(kv_cache[1], HEAD_DIM), preferred_element_type=f32)
        return (top, jnp.sum(weights, axis=(2, 3)), accum)

    states = lax.map(one_group, jnp.arange(KV_HEADS, dtype=jnp.int32))
    states = jax.tree.map(lambda part: jnp.moveaxis(part, 0, 1), states)
    columns = q_weight.shape[1]
    top, total, accum = combined_all(states, "seq", combine_states)
    attended = (accum / total[..., None]).reshape(rows, HEADS * HEAD_DIM).astype(bf16)
    attn_cols = lax.dynamic_slice_in_dim(attended, lax.axis_index("seq") * columns, columns, 1)
    stream = (x_rows.astype(f32) + summed(o_weight, attn_cols)).astype(bf16)
    normed_two = rms_norm(lax.all_gather(stream, "seq", axis=1, tiled=True), mlp_gain)
    gate = jnp.dot(normed_two, gate_weight, preferred_element_type=f32)
    upward = jnp.dot(normed_two, up_weight, preferred_element_type=f32)
    hidden = (jax.nn.silu(gate) * upward).astype(bf16)
    return (stream.astype(f32) + summed(down_weight, hidden)).astype(bf16)


def solution(mesh):
    pairs = mesh.shape["seq"] == 2 * KV_HEADS
    return jax.shard_map(
        local_pairs if pairs else local_tokens,
        mesh=mesh,
        in_specs=(
            P("group", "seq"),
            P(),
            P(None, "seq"),
            P("seq", None),
            P(),
            P(None, "seq"),
            P(None, "seq"),
            P("seq", None),
            P(None, ("group", "seq"), None),
            P("group", None, "seq"),
        ),
        out_specs=P("group", "seq"),
        check_vma=False,
    )
```

```python
import functools

import jax
import jax.numpy as jnp
from jax import lax
from jax.experimental import pallas as pl
from jax.experimental.pallas import tpu as pltpu
from jax.sharding import PartitionSpec as P

HEADS = 64
KV_HEADS = 8
HEAD_DIM = 128
BLOCK = 128
QUAD = 4
RANGE = 32000.0
STEPS = 256.0

eps = 1e-05
floor_score = -1e30

bf16 = jnp.bfloat16
f32 = jnp.float32
VMEM = pl.BlockSpec(memory_space=pltpu.VMEM)


def call(body, outs, ins, beside=(), limit=4 * 2**20):
    count, extra = len(ins), len(beside)

    def kernel(*refs):
        body(*refs[:count], *refs[count + extra :])

    return pl.pallas_call(
        kernel,
        out_shape=outs,
        in_specs=[VMEM] * count + [pl.BlockSpec(memory_space=pl.ANY)] * extra,
        out_specs=jax.tree.map(lambda _: VMEM, outs),
        compiler_params=pltpu.CompilerParams(vmem_limit_bytes=limit),
    )(*ins, *beside)


def room(size):
    return pl.pallas_call(
        lambda out: None,
        out_shape=like((size, 1024), f32),
        out_specs=pl.BlockSpec(memory_space=pl.ANY),
    )()


def like(shape, dtype):
    return jax.ShapeDtypeStruct(shape, dtype)


def swap(x, distance):
    size = lax.axis_size("seq")
    return lax.ppermute(x, "seq", [(i, i ^ distance) for i in range(size)])


def pack_kernel(outer, kv_ref, mask_ref, x_ref, send_ref, *outs):
    me = lax.axis_index("seq")
    z, y = me // QUAD, (me // 2) % 2
    keys = kv_ref.shape[1]
    rows = mask_ref.shape[0]
    pieces = [x_ref[:, at : at + HEAD_DIM] for at in range(0, x_ref.shape[1], HEAD_DIM)]
    lane = lax.broadcasted_iota(jnp.int32, (rows, HEAD_DIM), 1)
    mask = jnp.zeros((rows, HEAD_DIM), f32)
    for head in range(mask_ref.shape[1]):
        live = (mask_ref[:, head : head + 1] == 1).astype(f32)
        mask = jnp.where(lane == head, jnp.broadcast_to(live, mask.shape), mask)
    pieces.append(mask.astype(bf16))
    for k in range(outer):
        peer = jnp.bitwise_xor(z, k)
        cols = pl.ds(pl.multiple_of((2 * peer + y) * HEAD_DIM, HEAD_DIM), HEAD_DIM)
        outs[k][0:keys, :] = kv_ref[0, :, cols]
        for i, piece in enumerate(pieces):
            outs[k][keys + i * rows : keys + (i + 1) * rows, :] = piece
        cols = pl.ds(pl.multiple_of((2 * peer + 1 - y) * HEAD_DIM, HEAD_DIM), HEAD_DIM)
        at = slice(k * HEAD_DIM, (k + 1) * HEAD_DIM)
        send_ref[0:keys, at] = kv_ref[0, :, cols]
        send_ref[keys : 2 * keys, at] = kv_ref[1, :, cols]


def unpack_kernel(keys, *refs):
    line_ref = refs[-1]
    rows = line_ref.shape[0]
    at = 0
    for ref in refs[:-1]:
        for i in range((ref.shape[0] - keys) // rows):
            line_ref[:, at : at + HEAD_DIM] = ref[keys + i * rows : keys + (i + 1) * rows, :]
            at += HEAD_DIM


def z_slots(outer):
    order = list(range(outer - 1, 0, -1))
    return list(zip([0, *order[-1:], *order[:-1]], [0, *order]))


def z_distance(slot, core):
    return jnp.where(core == 0, slot[0], slot[1])


def route_kernel(outer, kv_ref, other_ref, *outs):
    me = lax.axis_index("seq")
    z, y = me // QUAD, (me // 2) % 2
    keys = kv_ref.shape[1]
    for slot, out in zip(z_slots(outer), outs):
        k = z_distance(slot, me % 2)
        head = 2 * jnp.bitwise_xor(z, k) + y
        cols = pl.ds(pl.multiple_of(head * HEAD_DIM, HEAD_DIM), HEAD_DIM)
        out[0:keys, :] = kv_ref[1, :, cols]
        out[keys:, :] = other_ref[:, pl.ds(pl.multiple_of(k * HEAD_DIM, HEAD_DIM), HEAD_DIM)]


def cache_kernel(outer, keys, *refs):
    firsts, rests, out_ref = refs[:outer], refs[outer : 2 * outer], refs[2 * outer]
    core = lax.axis_index("seq") % 2
    for i, slot in enumerate(z_slots(outer)):
        at = 4 * i * keys
        for at_core in range(2):

            @pl.when(core == at_core)
            def _():
                out_ref[at : at + keys, :] = firsts[slot[at_core]][0:keys, :]

        out_ref[at + keys : at + 4 * keys, :] = rests[i][...]


def stack_kernel(axis, *refs):
    at = 0
    for ref in refs[:-1]:
        size = ref.shape[axis]
        if axis == 0:
            refs[-1][at : at + size, :] = ref[...]
        else:
            refs[-1][:, at : at + size] = ref[...]
        at += size


def stacked(parts, axis, beside=()):
    shape = list(parts[0].shape)
    shape[axis] = sum(p.shape[axis] for p in parts)
    return call(functools.partial(stack_kernel, axis), like(tuple(shape), parts[0].dtype), parts, beside)


def normed_chunks(wide, chunks, gain_ref):
    squares = None
    for source, load in chunks:
        v = load().astype(f32)
        s = jnp.sum(v * v, axis=1, keepdims=True)
        squares = s if squares is None else squares + s
    inverse = lax.rsqrt(squares / (len(chunks) * wide) + eps)
    for source, load in chunks:
        at = pl.ds(pl.multiple_of(source * wide, wide), wide)
        yield at, (load().astype(f32) * inverse * gain_ref[:, at].astype(f32)).astype(bf16)


def to_members(parts):
    size = lax.axis_size("seq")
    groups = [list(range(core, size, 2)) for core in range(2)]
    return lax.all_to_all(parts, "seq", 0, 0, axis_index_groups=groups, tiled=True)


def member(i, other):
    core = lax.axis_index("seq") % 2
    return 2 * i + (1 - core if other else core)


def line_of(outer, *nears):
    return [QUAD * k + j for j in nears for k in range(outer)]


def line_chunks(outer, wide, refs):
    me = lax.axis_index("seq")
    lines = [line_of(outer, near) for near in range(QUAD)]
    step = wide + HEAD_DIM
    return [
        (jnp.bitwise_xor(me, distance), lambda r=ref, i=i: r[:, i * step : i * step + wide])
        for ref, line in zip(refs, lines)
        for i, distance in enumerate(line)
    ]


def line_mask(wide, ref, i):
    at = pl.multiple_of(i * (wide + HEAD_DIM) + wide, HEAD_DIM)
    tile = ref[:, pl.ds(at, HEAD_DIM)].astype(f32)
    lane = lax.broadcasted_iota(jnp.int32, tile.shape, 1)
    mine = jnp.where(lane == lax.axis_index("seq") // 2, tile, 0.0)
    return jnp.broadcast_to(jnp.sum(mine, axis=1, keepdims=True), tile.shape)


def member_chunks(refs):
    return [
        (member(i, other), lambda r=ref, i=i: r[i])
        for other, ref in enumerate(refs)
        for i in range(ref.shape[0])
    ]


def query_kernel(outer, wide, *refs):
    gain_ref, w_ref, out_ref = refs[QUAD:]
    total = None
    for at, chunk in normed_chunks(wide, line_chunks(outer, wide, refs[:QUAD]), gain_ref):
        term = jnp.dot(chunk, w_ref[at, :], preferred_element_type=f32)
        total = term if total is None else total + term
    out_ref[...] = total.astype(bf16)


def scatter_dot(wide, other, left, w_ref, out_ref):
    for i in range(out_ref.shape[0]):
        at = pl.ds(pl.multiple_of(member(i, other) * wide, wide), wide)
        out_ref[i] = jnp.dot(left, w_ref[:, at], preferred_element_type=f32)


def keep_kernel(wide, left_ref, w_ref, out_ref):
    scatter_dot(wide, False, left_ref[...], w_ref, out_ref)


def span_states(q_ref, cache_ref, masks):
    heads = q_ref.shape[1] // HEAD_DIM
    scale = 1.0 / HEAD_DIM**0.5
    keys = cache_ref.shape[0] // (2 * len(masks))
    queries = jnp.concatenate(
        [q_ref[:, h * HEAD_DIM : (h + 1) * HEAD_DIM] for h in range(heads)], axis=0
    )
    scores = [
        lax.dot_general(
            queries,
            cache_ref[2 * i * keys : (2 * i + 1) * keys, :],
            (((1,), (1,)), ((), ())),
            preferred_element_type=f32,
        )
        * scale
        for i in range(len(masks))
    ]
    lives = [jnp.concatenate([mask] * heads, axis=0) > 0.5 for mask in masks]
    scores = [jnp.where(live, score, floor_score) for live, score in zip(lives, scores)]
    tops = [jnp.max(score, axis=1, keepdims=True) for score in scores]
    weights = [
        jnp.where(live, jnp.exp(score - top), 0.0) for live, score, top in zip(lives, scores, tops)
    ]
    totals = [jnp.sum(weight, axis=1, keepdims=True) for weight in weights]
    accums = [
        jnp.dot(
            weight.astype(bf16),
            cache_ref[(2 * i + 1) * keys : (2 * i + 2) * keys, :],
            preferred_element_type=f32,
        )
        for i, weight in enumerate(weights)
    ]
    return list(zip(tops, totals, accums))


def combined(states):
    top = functools.reduce(jnp.maximum, [s[0] for s in states])
    total = accum = None
    for t, s, a in states:
        factor = jnp.exp(t - top)
        total = s * factor if total is None else total + s * factor
        accum = a * factor if accum is None else accum + a * factor
    return top, total, accum


def early_kernel(outer, wide, q_ref, cache_ref, line_ref, other_ref, top_ref, total_ref, accum_ref):
    core = lax.axis_index("seq") % 2
    masks = [
        line_mask(wide, ref, z_distance(slot, core))
        for slot in z_slots(outer)
        for ref in (line_ref, other_ref)
    ]
    top, total, accum_ref[...] = combined(span_states(q_ref, cache_ref, masks))
    top_ref[...] = jnp.broadcast_to(top, top_ref.shape)
    total_ref[...] = jnp.broadcast_to(total, total_ref.shape)


def attend_kernel(
    outer, wide, q_ref, top_ref, total_ref, accum_ref, cache_ref, core_ref, far_ref, w_ref, left_ref, send_ref
):
    rows = q_ref.shape[0]
    heads = q_ref.shape[1] // HEAD_DIM
    core = 1 - lax.axis_index("seq") % 2
    masks = [
        line_mask(wide, ref, z_distance(slot, core))
        for slot in z_slots(outer)
        for ref in (core_ref, far_ref)
    ]
    states = span_states(q_ref, cache_ref, masks)
    states.append((top_ref[:, 0:1], total_ref[:, 0:1], accum_ref[...]))
    _, total, accum = combined(states)
    attended = (accum / total).astype(bf16)
    attended = jnp.concatenate([attended[h * rows : (h + 1) * rows] for h in range(heads)], axis=1)
    left_ref[...] = attended
    scatter_dot(wide, True, attended, w_ref, send_ref)


def hidden_kernel(wide, *refs):
    gain_ref, gate_ref, up_ref, down_ref, left_ref, send_ref = refs[2:]
    gate = up = None
    for at, chunk in normed_chunks(wide, member_chunks(refs[:2]), gain_ref):
        g = jnp.dot(chunk, gate_ref[at, :], preferred_element_type=f32)
        u = jnp.dot(chunk, up_ref[at, :], preferred_element_type=f32)
        gate = g if gate is None else gate + g
        up = u if up is None else up + u
    hidden = (gate / (1.0 + jnp.exp(-gate)) * up).astype(bf16)
    left_ref[...] = hidden
    scatter_dot(wide, True, hidden, down_ref, send_ref)


def add_kernel(own_ref, recv_ref, out_ref):
    out_ref[...] = (own_ref[...] + recv_ref[...]).astype(out_ref.dtype)


def code_kernel(own_ref, recv_ref, out_ref):
    members, rows, wide = own_ref.shape
    sums = [own_ref[i] + recv_ref[i] for i in range(members)]
    largest = functools.reduce(jnp.maximum, [jnp.max(jnp.abs(s), axis=1, keepdims=True) for s in sums])
    level = jnp.ceil(jnp.log(jnp.maximum(largest, 1e-30)) * STEPS)
    scale = jnp.exp(level * (-1.0 / STEPS)) * RANGE
    level = jnp.broadcast_to(level, (rows, HEAD_DIM)).astype(jnp.int32).astype(jnp.int16)
    for i, s in enumerate(sums):
        out_ref[i, :, 0:wide] = jnp.round(s * scale).astype(jnp.int32).astype(jnp.int16)
        out_ref[i, :, wide:] = level


def decoded(ref, i, wide):
    level = ref[i, :, wide:].astype(jnp.int32).astype(f32)[:, 0:1]
    scale = jnp.exp(level * (1.0 / STEPS)) * (1.0 / RANGE)
    return ref[i, :, 0:wide].astype(jnp.int32).astype(f32) * scale


def final_kernel(base_ref, parts_ref, *out_refs):
    wide = base_ref.shape[1]
    load = lambda i: parts_ref[i].astype(f32)
    if parts_ref.dtype == jnp.int16:
        load = lambda i: decoded(parts_ref, i, wide)
    total = load(0)
    for i in range(1, parts_ref.shape[0]):
        total = total + load(i)
    total = (base_ref[...].astype(f32) + total).astype(bf16)
    for out in out_refs:
        if len(out.shape) == 3:
            for i in range(out.shape[0]):
                out[i] = total
        else:
            out[...] = total


def z_swapped(parts):
    arrived = [swap(part, QUAD * k) for k, part in reversed(list(enumerate(parts))) if k > 0]
    return [parts[0], *reversed(arrived)]


def z_routed(parts):
    size = lax.axis_size("seq")
    return [parts[0]] + [
        lax.ppermute(part, "seq", [(i, i ^ QUAD * slot[i % 2]) for i in range(size)])
        for slot, part in list(zip(z_slots(len(parts)), parts))[1:]
    ]


def near_gathered(line):
    y = swap(line, 2)
    core, far = swap(line, 1), swap(y, 1)
    return [line, core, y, far]


def scattered(base, send, left, weight, wide, kind, outs, beside=()):
    far = swap(send, 1)
    own = call(functools.partial(keep_kernel, wide), like(send.shape, f32), [left, weight])
    if kind == jnp.int16:
        members, rows, _ = send.shape
        sums = call(code_kernel, like((members, rows, wide + HEAD_DIM), kind), [own, far], beside)
    else:
        sums = call(add_kernel, like(send.shape, kind), [own, far], beside)
    return call(final_kernel, outs, [base, to_members(sums)], beside)


def local_pairs(
    x_rows, attn_gain, q_weight, o_weight, mlp_gain, gate_weight, up_weight, down_weight, kv_cache, block_mask
):
    rows, wide = x_rows.shape
    outer = lax.axis_size("seq") // QUAD
    columns = q_weight.shape[1]
    beside = [room(18432)]
    attn_gain = attn_gain.reshape(1, -1)
    mlp_gain = mlp_gain.reshape(1, -1)
    members = lax.axis_size("seq") // 2
    partial_sums = like((members, rows, wide), f32)
    own_columns = like((rows, wide), bf16)

    keys = kv_cache.shape[1]
    step = wide + HEAD_DIM
    send, *firsts = call(
        functools.partial(pack_kernel, outer),
        [like((2 * keys, outer * HEAD_DIM), bf16)]
        + [like((keys + step // HEAD_DIM * rows, HEAD_DIM), bf16)] * outer,
        [kv_cache, block_mask[:, :, 0], x_rows],
        beside,
    )
    other = swap(send, 2)
    firsts = z_swapped(firsts)
    line = call(functools.partial(unpack_kernel, keys), like((rows, outer * step), bf16), firsts)
    routed = call(
        functools.partial(route_kernel, outer),
        [like((3 * keys, HEAD_DIM), bf16)] * outer,
        [kv_cache, other],
        [line, *beside],
    )
    routed = z_routed(routed)
    x_parts = near_gathered(line)
    queries = call(
        functools.partial(query_kernel, outer, wide),
        like((rows, columns), bf16),
        [*x_parts, attn_gain, q_weight],
    )
    cache = call(
        functools.partial(cache_kernel, outer, keys),
        like((4 * outer * keys, HEAD_DIM), bf16),
        [*firsts, *routed],
        [queries],
    )
    far_cache = swap(cache, 1)
    tall = like((columns // HEAD_DIM * rows, HEAD_DIM), f32)
    early = call(
        functools.partial(early_kernel, outer, wide), [tall] * 3, [queries, cache, *x_parts[0::2]]
    )
    left, send = call(
        functools.partial(attend_kernel, outer, wide),
        [like((rows, columns), bf16), partial_sums],
        [queries, *early, far_cache, *x_parts[1::2], o_weight],
    )
    stream, copies = scattered(
        x_rows, send, left, o_weight, wide, jnp.int16, [own_columns, like(partial_sums.shape, bf16)], beside
    )
    parts = to_members(copies)
    left, send = call(
        functools.partial(hidden_kernel, wide),
        [like((rows, gate_weight.shape[1]), bf16), partial_sums],
        [parts, swap(parts, 1), mlp_gain, gate_weight, up_weight, down_weight],
    )
    return scattered(stream, send, left, down_weight, wide, bf16, [own_columns])[0]


def rms_norm(values, gain):
    wide = values.astype(f32)
    inverse = lax.rsqrt(jnp.mean(wide * wide, axis=-1, keepdims=True) + eps)
    return (wide * inverse * gain.astype(f32)).astype(bf16)


def combine_states(first, second):
    top_a, total_a, accum_a = first
    top_b, total_b, accum_b = second
    top = jnp.maximum(top_a, top_b)
    factor_a = jnp.exp(top_a - top)
    factor_b = jnp.exp(top_b - top)
    return (
        top,
        total_a * factor_a + total_b * factor_b,
        accum_a * factor_a[..., None] + accum_b * factor_b[..., None],
    )


def combined_all(x, axis, combine):
    everything = jax.tree.map(lambda part: lax.all_gather(part, axis), x)
    initial = jax.tree.map(lambda part: part[0], everything)

    def turn(k, so_far):
        return combine(so_far, jax.tree.map(lambda part: part[k], everything))

    return lax.fori_loop(1, lax.axis_size(axis), turn, initial)


def summed(weight, left):
    product = lax.dot_general(weight, left, (((0,), (1,)), ((), ())), preferred_element_type=f32)
    return lax.psum_scatter(product, "seq", scatter_dimension=0, tiled=True).T


def local_tokens(
    x_rows, attn_gain, q_weight, o_weight, mlp_gain, gate_weight, up_weight, down_weight, kv_cache, block_mask
):
    rows = x_rows.shape[0]
    group = HEADS // KV_HEADS
    key_len = kv_cache.shape[1]
    spans = key_len // BLOCK
    scale = 1.0 / HEAD_DIM**0.5
    normed = rms_norm(lax.all_gather(x_rows, "seq", axis=1, tiled=True), attn_gain)
    query_part = jnp.dot(normed, q_weight, preferred_element_type=f32).astype(bf16)
    queries = lax.all_gather(query_part, "seq", axis=1, tiled=True)

    def one_group(index):
        def cut(array, width):
            return lax.dynamic_slice_in_dim(array, index * width, width, 1)

        query_group = cut(queries, group * HEAD_DIM).reshape(rows, group, HEAD_DIM)
        scores = (
            jnp.einsum("rhd,kd->rhk", query_group, cut(kv_cache[0], HEAD_DIM), preferred_element_type=f32)
            * scale
        )
        scores = scores.reshape(rows, group, spans, BLOCK)
        live = (cut(block_mask, 1)[:, 0, :] == 1)[:, None, :, None]
        masked = jnp.where(live, scores, floor_score)
        top = jnp.max(masked, axis=(2, 3))
        weights = jnp.where(live, jnp.exp(masked - top[..., None, None]), 0.0)
        rounded = weights.astype(bf16).reshape(rows, group, key_len)
        accum = jnp.einsum("rhk,kd->rhd", rounded, cut(kv_cache[1], HEAD_DIM), preferred_element_type=f32)
        return (top, jnp.sum(weights, axis=(2, 3)), accum)

    states = lax.map(one_group, jnp.arange(KV_HEADS, dtype=jnp.int32))
    states = jax.tree.map(lambda part: jnp.moveaxis(part, 0, 1), states)
    columns = q_weight.shape[1]
    top, total, accum = combined_all(states, "seq", combine_states)
    attended = (accum / total[..., None]).reshape(rows, HEADS * HEAD_DIM).astype(bf16)
    attn_cols = lax.dynamic_slice_in_dim(attended, lax.axis_index("seq") * columns, columns, 1)
    stream = (x_rows.astype(f32) + summed(o_weight, attn_cols)).astype(bf16)
    normed_two = rms_norm(lax.all_gather(stream, "seq", axis=1, tiled=True), mlp_gain)
    gate = jnp.dot(normed_two, gate_weight, preferred_element_type=f32)
    upward = jnp.dot(normed_two, up_weight, preferred_element_type=f32)
    hidden = (jax.nn.silu(gate) * upward).astype(bf16)
    return (stream.astype(f32) + summed(down_weight, hidden)).astype(bf16)


def solution(mesh):
    pairs = mesh.shape["seq"] == 2 * KV_HEADS
    return jax.shard_map(
        local_pairs if pairs else local_tokens,
        mesh=mesh,
        in_specs=(
            P("group", "seq"),
            P(),
            P(None, "seq"),
            P("seq", None),
            P(),
            P(None, "seq"),
            P(None, "seq"),
            P("seq", None),
            P(None, ("group", "seq"), None),
            P("group", None, "seq"),
        ),
        out_specs=P("group", "seq"),
        check_vma=False,
    )
```

```python
import functools

import jax
import jax.numpy as jnp
from jax import lax
from jax.experimental import pallas as pl
from jax.experimental.pallas import tpu as pltpu
from jax.sharding import PartitionSpec as P

HEADS = 64
KV_HEADS = 8
HEAD_DIM = 128
BLOCK = 128
QUAD = 4
RANGE = 32000.0
STEPS = 256.0

eps = 1e-05
floor_score = -1e30

bf16 = jnp.bfloat16
f32 = jnp.float32
VMEM = pl.BlockSpec(memory_space=pltpu.VMEM)


def call(body, outs, ins, beside=(), limit=4 * 2**20):
    count, extra = len(ins), len(beside)

    def kernel(*refs):
        body(*refs[:count], *refs[count + extra :])

    return pl.pallas_call(
        kernel,
        out_shape=outs,
        in_specs=[VMEM] * count + [pl.BlockSpec(memory_space=pl.ANY)] * extra,
        out_specs=jax.tree.map(lambda _: VMEM, outs),
        compiler_params=pltpu.CompilerParams(vmem_limit_bytes=limit),
    )(*ins, *beside)


def room(size):
    return pl.pallas_call(
        lambda out: None,
        out_shape=like((size, 1024), f32),
        out_specs=pl.BlockSpec(memory_space=pl.ANY),
    )()


def like(shape, dtype):
    return jax.ShapeDtypeStruct(shape, dtype)


def swap(x, distance):
    size = lax.axis_size("seq")
    return lax.ppermute(x, "seq", [(i, i ^ distance) for i in range(size)])


def pack_kernel(outer, kv_ref, mask_ref, x_ref, send_ref, *outs):
    me = lax.axis_index("seq")
    z, y = me // QUAD, (me // 2) % 2
    keys = kv_ref.shape[1]
    rows = mask_ref.shape[0]
    pieces = [x_ref[:, at : at + HEAD_DIM] for at in range(0, x_ref.shape[1], HEAD_DIM)]
    lane = lax.broadcasted_iota(jnp.int32, (rows, HEAD_DIM), 1)
    mask = jnp.zeros((rows, HEAD_DIM), f32)
    for head in range(mask_ref.shape[1]):
        live = (mask_ref[:, head : head + 1] == 1).astype(f32)
        mask = jnp.where(lane == head, jnp.broadcast_to(live, mask.shape), mask)
    pieces.append(mask.astype(bf16))
    for k in range(outer):
        peer = jnp.bitwise_xor(z, k)
        cols = pl.ds(pl.multiple_of((2 * peer + y) * HEAD_DIM, HEAD_DIM), HEAD_DIM)
        outs[k][0:keys, :] = kv_ref[0, :, cols]
        for i, piece in enumerate(pieces):
            outs[k][keys + i * rows : keys + (i + 1) * rows, :] = piece
        cols = pl.ds(pl.multiple_of((2 * peer + 1 - y) * HEAD_DIM, HEAD_DIM), HEAD_DIM)
        at = slice(k * HEAD_DIM, (k + 1) * HEAD_DIM)
        send_ref[0:keys, at] = kv_ref[0, :, cols]
        send_ref[keys : 2 * keys, at] = kv_ref[1, :, cols]


def unpack_kernel(keys, *refs):
    line_ref = refs[-1]
    rows = line_ref.shape[0]
    at = 0
    for ref in refs[:-1]:
        for i in range((ref.shape[0] - keys) // rows):
            line_ref[:, at : at + HEAD_DIM] = ref[keys + i * rows : keys + (i + 1) * rows, :]
            at += HEAD_DIM


def z_slots(outer):
    order = list(range(outer - 1, 0, -1))
    return list(zip([0, *order[-1:], *order[:-1]], [0, *order]))


def z_distance(slot, core):
    return jnp.where(core == 0, slot[0], slot[1])


def route_kernel(outer, kv_ref, other_ref, *outs):
    me = lax.axis_index("seq")
    z, y = me // QUAD, (me // 2) % 2
    keys = kv_ref.shape[1]
    for slot, out in zip(z_slots(outer), outs):
        k = z_distance(slot, me % 2)
        head = 2 * jnp.bitwise_xor(z, k) + y
        cols = pl.ds(pl.multiple_of(head * HEAD_DIM, HEAD_DIM), HEAD_DIM)
        out[0:keys, :] = kv_ref[1, :, cols]
        out[keys:, :] = other_ref[:, pl.ds(pl.multiple_of(k * HEAD_DIM, HEAD_DIM), HEAD_DIM)]


def cache_kernel(outer, keys, *refs):
    firsts, rests, out_ref = refs[:outer], refs[outer : 2 * outer], refs[2 * outer]
    core = lax.axis_index("seq") % 2
    for i, slot in enumerate(z_slots(outer)):
        at = 4 * i * keys
        for at_core in range(2):

            @pl.when(core == at_core)
            def _():
                out_ref[at : at + keys, :] = firsts[slot[at_core]][0:keys, :]

        out_ref[at + keys : at + 4 * keys, :] = rests[i][...]


def stack_kernel(axis, *refs):
    at = 0
    for ref in refs[:-1]:
        size = ref.shape[axis]
        if axis == 0:
            refs[-1][at : at + size, :] = ref[...]
        else:
            refs[-1][:, at : at + size] = ref[...]
        at += size


def stacked(parts, axis, beside=()):
    shape = list(parts[0].shape)
    shape[axis] = sum(p.shape[axis] for p in parts)
    return call(functools.partial(stack_kernel, axis), like(tuple(shape), parts[0].dtype), parts, beside)


def normed_chunks(wide, chunks, gain_ref):
    squares = None
    for source, load in chunks:
        v = load().astype(f32)
        s = jnp.sum(v * v, axis=1, keepdims=True)
        squares = s if squares is None else squares + s
    inverse = lax.rsqrt(squares / (len(chunks) * wide) + eps)
    for source, load in chunks:
        at = pl.ds(pl.multiple_of(source * wide, wide), wide)
        yield at, (load().astype(f32) * inverse * gain_ref[:, at].astype(f32)).astype(bf16)


def to_members(parts):
    size = lax.axis_size("seq")
    groups = [list(range(core, size, 2)) for core in range(2)]
    return lax.all_to_all(parts, "seq", 0, 0, axis_index_groups=groups, tiled=True)


def member(i, other):
    core = lax.axis_index("seq") % 2
    return 2 * i + (1 - core if other else core)


def line_of(outer, *nears):
    return [QUAD * k + j for j in nears for k in range(outer)]


def line_chunks(outer, wide, refs):
    me = lax.axis_index("seq")
    lines = [line_of(outer, near) for near in range(QUAD)]
    step = wide + HEAD_DIM
    return [
        (jnp.bitwise_xor(me, distance), lambda r=ref, i=i: r[:, i * step : i * step + wide])
        for ref, line in zip(refs, lines)
        for i, distance in enumerate(line)
    ]


def line_mask(wide, ref, i):
    at = pl.multiple_of(i * (wide + HEAD_DIM) + wide, HEAD_DIM)
    tile = ref[:, pl.ds(at, HEAD_DIM)].astype(f32)
    lane = lax.broadcasted_iota(jnp.int32, tile.shape, 1)
    mine = jnp.where(lane == lax.axis_index("seq") // 2, tile, 0.0)
    return jnp.broadcast_to(jnp.sum(mine, axis=1, keepdims=True), tile.shape)


def in_line(near, z):
    return QUAD * z + jnp.bitwise_xor(lax.axis_index("seq") % QUAD, near)


def z_line_chunks(wide, refs):
    return [
        (in_line(near, z), lambda r=ref, z=z: r[:, z * wide : (z + 1) * wide])
        for near, ref in enumerate(refs)
        for z in range(ref.shape[1] // wide)
    ]


def query_kernel(outer, wide, *refs):
    gain_ref, w_ref, out_ref = refs[QUAD:]
    total = None
    for at, chunk in normed_chunks(wide, line_chunks(outer, wide, refs[:QUAD]), gain_ref):
        term = jnp.dot(chunk, w_ref[at, :], preferred_element_type=f32)
        total = term if total is None else total + term
    out_ref[...] = total.astype(bf16)


def scatter_dot(wide, other, left, w_ref, out_ref):
    for i in range(out_ref.shape[0]):
        at = pl.ds(pl.multiple_of(member(i, other) * wide, wide), wide)
        out_ref[i] = jnp.dot(left, w_ref[:, at], preferred_element_type=f32)


def line_dot(wide, nears, left, w_ref, out_ref):
    outer = out_ref.shape[1] // (len(nears) * wide)
    for i, near in enumerate(nears):
        for z in range(outer):
            at = pl.ds(pl.multiple_of(in_line(near, z) * wide, wide), wide)
            to = (i * outer + z) * wide
            out_ref[:, to : to + wide] = jnp.dot(left, w_ref[:, at], preferred_element_type=f32)


def keep_kernel(wide, left_ref, w_ref, out_ref):
    scatter_dot(wide, False, left_ref[...], w_ref, out_ref)


def keep_line_kernel(wide, left_ref, w_ref, out_ref):
    line_dot(wide, (0, 2), left_ref[...], w_ref, out_ref)


def span_states(q_ref, cache_ref, masks):
    heads = q_ref.shape[1] // HEAD_DIM
    scale = 1.0 / HEAD_DIM**0.5
    keys = cache_ref.shape[0] // (2 * len(masks))
    queries = jnp.concatenate(
        [q_ref[:, h * HEAD_DIM : (h + 1) * HEAD_DIM] for h in range(heads)], axis=0
    )
    scores = [
        lax.dot_general(
            queries,
            cache_ref[2 * i * keys : (2 * i + 1) * keys, :],
            (((1,), (1,)), ((), ())),
            preferred_element_type=f32,
        )
        * scale
        for i in range(len(masks))
    ]
    lives = [jnp.concatenate([mask] * heads, axis=0) > 0.5 for mask in masks]
    scores = [jnp.where(live, score, floor_score) for live, score in zip(lives, scores)]
    tops = [jnp.max(score, axis=1, keepdims=True) for score in scores]
    weights = [
        jnp.where(live, jnp.exp(score - top), 0.0) for live, score, top in zip(lives, scores, tops)
    ]
    totals = [jnp.sum(weight, axis=1, keepdims=True) for weight in weights]
    accums = [
        jnp.dot(
            weight.astype(bf16),
            cache_ref[(2 * i + 1) * keys : (2 * i + 2) * keys, :],
            preferred_element_type=f32,
        )
        for i, weight in enumerate(weights)
    ]
    return list(zip(tops, totals, accums))


def combined(states):
    top = functools.reduce(jnp.maximum, [s[0] for s in states])
    total = accum = None
    for t, s, a in states:
        factor = jnp.exp(t - top)
        total = s * factor if total is None else total + s * factor
        accum = a * factor if accum is None else accum + a * factor
    return top, total, accum


def early_kernel(outer, wide, q_ref, cache_ref, line_ref, other_ref, top_ref, total_ref, accum_ref):
    core = lax.axis_index("seq") % 2
    masks = [
        line_mask(wide, ref, z_distance(slot, core))
        for slot in z_slots(outer)
        for ref in (line_ref, other_ref)
    ]
    top, total, accum_ref[...] = combined(span_states(q_ref, cache_ref, masks))
    top_ref[...] = jnp.broadcast_to(top, top_ref.shape)
    total_ref[...] = jnp.broadcast_to(total, total_ref.shape)


def attend_kernel(
    outer, wide, q_ref, top_ref, total_ref, accum_ref, cache_ref, core_ref, far_ref, w_ref, left_ref, send_ref
):
    rows = q_ref.shape[0]
    heads = q_ref.shape[1] // HEAD_DIM
    core = 1 - lax.axis_index("seq") % 2
    masks = [
        line_mask(wide, ref, z_distance(slot, core))
        for slot in z_slots(outer)
        for ref in (core_ref, far_ref)
    ]
    states = span_states(q_ref, cache_ref, masks)
    states.append((top_ref[:, 0:1], total_ref[:, 0:1], accum_ref[...]))
    _, total, accum = combined(states)
    attended = (accum / total).astype(bf16)
    attended = jnp.concatenate([attended[h * rows : (h + 1) * rows] for h in range(heads)], axis=1)
    left_ref[...] = attended
    line_dot(wide, (1, 3), attended, w_ref, send_ref)


def hidden_kernel(wide, *refs):
    gain_ref, gate_ref, up_ref, down_ref, left_ref, send_ref = refs[QUAD:]
    gate = up = None
    for at, chunk in normed_chunks(wide, z_line_chunks(wide, refs[:QUAD]), gain_ref):
        g = jnp.dot(chunk, gate_ref[at, :], preferred_element_type=f32)
        u = jnp.dot(chunk, up_ref[at, :], preferred_element_type=f32)
        gate = g if gate is None else gate + g
        up = u if up is None else up + u
    hidden = (gate / (1.0 + jnp.exp(-gate)) * up).astype(bf16)
    left_ref[...] = hidden
    scatter_dot(wide, True, hidden, down_ref, send_ref)


def add_kernel(own_ref, recv_ref, out_ref):
    out_ref[...] = (own_ref[...] + recv_ref[...]).astype(out_ref.dtype)


def coded(out_ref, sums):
    rows, wide = sums.shape
    largest = jnp.max(jnp.abs(sums), axis=1, keepdims=True)
    level = jnp.ceil(jnp.log(jnp.maximum(largest, 1e-30)) * STEPS)
    scale = jnp.exp(level * (-1.0 / STEPS)) * RANGE
    out_ref[:, 0:wide] = jnp.round(sums * scale).astype(jnp.int32).astype(jnp.int16)
    level = jnp.broadcast_to(level, (rows, HEAD_DIM)).astype(jnp.int32)
    out_ref[:, wide:] = level.astype(jnp.int16)


def decoded(ref):
    wide = ref.shape[1] - HEAD_DIM
    level = ref[:, wide:].astype(jnp.int32).astype(f32)[:, 0:1]
    scale = jnp.exp(level * (1.0 / STEPS)) * (1.0 / RANGE)
    return ref[:, 0:wide].astype(jnp.int32).astype(f32) * scale


def chip_kernel(own_ref, recv_ref, keep_ref, send_ref):
    half = own_ref.shape[1] // 2
    keep_ref[...] = own_ref[:, :half] + recv_ref[:, :half]
    coded(send_ref, own_ref[:, half:] + recv_ref[:, half:])


def pair_kernel(keep_ref, recv_ref, out_ref):
    coded(out_ref, keep_ref[...] + decoded(recv_ref))


def stream_kernel(wide, x_ref, *refs):
    parts, (line_ref, own_ref) = refs[:-2], refs[-2:]
    z = lax.axis_index("seq") // QUAD
    sums = [decoded(part) for part in parts]
    while len(sums) > 1:
        sums = [first + second for first, second in zip(sums[0::2], sums[1::2])]
    for to in range(len(parts)):
        at = pl.multiple_of(jnp.bitwise_xor(z, to) * (wide + HEAD_DIM), HEAD_DIM)
        cols = slice(to * wide, (to + 1) * wide)
        line_ref[:, cols] = (x_ref[:, pl.ds(at, wide)].astype(f32) + sums[0][:, cols]).astype(bf16)
    own_ref[...] = line_ref[:, pl.ds(pl.multiple_of(z * wide, wide), wide)]


def final_kernel(base_ref, parts_ref, out_ref):
    total = parts_ref[0].astype(f32)
    for i in range(1, parts_ref.shape[0]):
        total = total + parts_ref[i].astype(f32)
    out_ref[...] = (base_ref[...].astype(f32) + total).astype(bf16)


def z_swapped(parts):
    arrived = [swap(part, QUAD * k) for k, part in reversed(list(enumerate(parts))) if k > 0]
    return [parts[0], *reversed(arrived)]


def z_routed(parts):
    size = lax.axis_size("seq")
    return [parts[0]] + [
        lax.ppermute(part, "seq", [(i, i ^ QUAD * slot[i % 2]) for i in range(size)])
        for slot, part in list(zip(z_slots(len(parts)), parts))[1:]
    ]


def near_gathered(line):
    y = swap(line, 2)
    core, far = swap(line, 1), swap(y, 1)
    return [line, core, y, far]


def updated(x_line, send, left, weight, wide, beside):
    rows, columns = send.shape
    half = columns // 2
    code = like((rows, half + HEAD_DIM), jnp.int16)
    far = swap(send, 1)
    own = call(functools.partial(keep_line_kernel, wide), like(send.shape, f32), [left, weight])
    keep, send = call(chip_kernel, [like((rows, half), f32), code], [own, far], beside)
    sums = call(pair_kernel, code, [keep, swap(send, 2)], beside)
    return call(
        functools.partial(stream_kernel, wide),
        [like((rows, half), bf16), like((rows, wide), bf16)],
        [x_line, *z_routed([sums] * (half // wide))],
    )


def scattered(base, send, left, weight, wide):
    far = swap(send, 1)
    own = call(functools.partial(keep_kernel, wide), like(send.shape, f32), [left, weight])
    sums = call(add_kernel, like(send.shape, bf16), [own, far])
    return call(final_kernel, like(base.shape, bf16), [base, to_members(sums)])


def local_pairs(
    x_rows, attn_gain, q_weight, o_weight, mlp_gain, gate_weight, up_weight, down_weight, kv_cache, block_mask
):
    rows, wide = x_rows.shape
    outer = lax.axis_size("seq") // QUAD
    columns = q_weight.shape[1]
    beside = [room(18432)]
    attn_gain = attn_gain.reshape(1, -1)
    mlp_gain = mlp_gain.reshape(1, -1)
    members = lax.axis_size("seq") // 2
    partial_sums = like((members, rows, wide), f32)

    keys = kv_cache.shape[1]
    step = wide + HEAD_DIM
    send, *firsts = call(
        functools.partial(pack_kernel, outer),
        [like((2 * keys, outer * HEAD_DIM), bf16)]
        + [like((keys + step // HEAD_DIM * rows, HEAD_DIM), bf16)] * outer,
        [kv_cache, block_mask[:, :, 0], x_rows],
        beside,
    )
    other = swap(send, 2)
    firsts = z_swapped(firsts)
    line = call(functools.partial(unpack_kernel, keys), like((rows, outer * step), bf16), firsts)
    routed = call(
        functools.partial(route_kernel, outer),
        [like((3 * keys, HEAD_DIM), bf16)] * outer,
        [kv_cache, other],
        [line, *beside],
    )
    routed = z_routed(routed)
    x_parts = near_gathered(line)
    queries = call(
        functools.partial(query_kernel, outer, wide),
        like((rows, columns), bf16),
        [*x_parts, attn_gain, q_weight],
    )
    cache = call(
        functools.partial(cache_kernel, outer, keys),
        like((4 * outer * keys, HEAD_DIM), bf16),
        [*firsts, *routed],
        [queries],
    )
    far_cache = swap(cache, 1)
    tall = like((columns // HEAD_DIM * rows, HEAD_DIM), f32)
    early = call(
        functools.partial(early_kernel, outer, wide), [tall] * 3, [queries, cache, *x_parts[0::2]]
    )
    left, send = call(
        functools.partial(attend_kernel, outer, wide),
        [like((rows, columns), bf16), like((rows, 2 * outer * wide), f32)],
        [queries, *early, far_cache, *x_parts[1::2], o_weight],
    )
    line, stream = updated(x_parts[0], send, left, o_weight, wide, beside)
    left, send = call(
        functools.partial(hidden_kernel, wide),
        [like((rows, gate_weight.shape[1]), bf16), partial_sums],
        [*near_gathered(line), mlp_gain, gate_weight, up_weight, down_weight],
    )
    return scattered(stream, send, left, down_weight, wide)


def rms_norm(values, gain):
    wide = values.astype(f32)
    inverse = lax.rsqrt(jnp.mean(wide * wide, axis=-1, keepdims=True) + eps)
    return (wide * inverse * gain.astype(f32)).astype(bf16)


def combine_states(first, second):
    top_a, total_a, accum_a = first
    top_b, total_b, accum_b = second
    top = jnp.maximum(top_a, top_b)
    factor_a = jnp.exp(top_a - top)
    factor_b = jnp.exp(top_b - top)
    return (
        top,
        total_a * factor_a + total_b * factor_b,
        accum_a * factor_a[..., None] + accum_b * factor_b[..., None],
    )


def combined_all(x, axis, combine):
    everything = jax.tree.map(lambda part: lax.all_gather(part, axis), x)
    initial = jax.tree.map(lambda part: part[0], everything)

    def turn(k, so_far):
        return combine(so_far, jax.tree.map(lambda part: part[k], everything))

    return lax.fori_loop(1, lax.axis_size(axis), turn, initial)


def summed(weight, left):
    product = lax.dot_general(weight, left, (((0,), (1,)), ((), ())), preferred_element_type=f32)
    return lax.psum_scatter(product, "seq", scatter_dimension=0, tiled=True).T


def local_tokens(
    x_rows, attn_gain, q_weight, o_weight, mlp_gain, gate_weight, up_weight, down_weight, kv_cache, block_mask
):
    rows = x_rows.shape[0]
    group = HEADS // KV_HEADS
    key_len = kv_cache.shape[1]
    spans = key_len // BLOCK
    scale = 1.0 / HEAD_DIM**0.5
    normed = rms_norm(lax.all_gather(x_rows, "seq", axis=1, tiled=True), attn_gain)
    query_part = jnp.dot(normed, q_weight, preferred_element_type=f32).astype(bf16)
    queries = lax.all_gather(query_part, "seq", axis=1, tiled=True)

    def one_group(index):
        def cut(array, width):
            return lax.dynamic_slice_in_dim(array, index * width, width, 1)

        query_group = cut(queries, group * HEAD_DIM).reshape(rows, group, HEAD_DIM)
        scores = (
            jnp.einsum("rhd,kd->rhk", query_group, cut(kv_cache[0], HEAD_DIM), preferred_element_type=f32)
            * scale
        )
        scores = scores.reshape(rows, group, spans, BLOCK)
        live = (cut(block_mask, 1)[:, 0, :] == 1)[:, None, :, None]
        masked = jnp.where(live, scores, floor_score)
        top = jnp.max(masked, axis=(2, 3))
        weights = jnp.where(live, jnp.exp(masked - top[..., None, None]), 0.0)
        rounded = weights.astype(bf16).reshape(rows, group, key_len)
        accum = jnp.einsum("rhk,kd->rhd", rounded, cut(kv_cache[1], HEAD_DIM), preferred_element_type=f32)
        return (top, jnp.sum(weights, axis=(2, 3)), accum)

    states = lax.map(one_group, jnp.arange(KV_HEADS, dtype=jnp.int32))
    states = jax.tree.map(lambda part: jnp.moveaxis(part, 0, 1), states)
    columns = q_weight.shape[1]
    top, total, accum = combined_all(states, "seq", combine_states)
    attended = (accum / total[..., None]).reshape(rows, HEADS * HEAD_DIM).astype(bf16)
    attn_cols = lax.dynamic_slice_in_dim(attended, lax.axis_index("seq") * columns, columns, 1)
    stream = (x_rows.astype(f32) + summed(o_weight, attn_cols)).astype(bf16)
    normed_two = rms_norm(lax.all_gather(stream, "seq", axis=1, tiled=True), mlp_gain)
    gate = jnp.dot(normed_two, gate_weight, preferred_element_type=f32)
    upward = jnp.dot(normed_two, up_weight, preferred_element_type=f32)
    hidden = (jax.nn.silu(gate) * upward).astype(bf16)
    return (stream.astype(f32) + summed(down_weight, hidden)).astype(bf16)


def solution(mesh):
    pairs = mesh.shape["seq"] == 2 * KV_HEADS
    return jax.shard_map(
        local_pairs if pairs else local_tokens,
        mesh=mesh,
        in_specs=(
            P("group", "seq"),
            P(),
            P(None, "seq"),
            P("seq", None),
            P(),
            P(None, "seq"),
            P(None, "seq"),
            P("seq", None),
            P(None, ("group", "seq"), None),
            P("group", None, "seq"),
        ),
        out_specs=P("group", "seq"),
        check_vma=False,
    )
```

```python
import functools

import jax
import jax.numpy as jnp
from jax import lax
from jax.experimental import pallas as pl
from jax.experimental.pallas import tpu as pltpu
from jax.sharding import PartitionSpec as P

HEADS = 64
KV_HEADS = 8
HEAD_DIM = 128
BLOCK = 128
QUAD = 4
RANGE = 32000.0
STEPS = 256.0
Z_ORDER = ((0, 3, 1, 2), (0, 2, 3, 1))

eps = 1e-05
floor_score = -1e30

bf16 = jnp.bfloat16
f32 = jnp.float32
VMEM = pl.BlockSpec(memory_space=pltpu.VMEM)


def call(body, outs, ins, beside=(), limit=4 * 2**20):
    count, extra = len(ins), len(beside)

    def kernel(*refs):
        body(*refs[:count], *refs[count + extra :])

    return pl.pallas_call(
        kernel,
        out_shape=outs,
        in_specs=[VMEM] * count + [pl.BlockSpec(memory_space=pl.ANY)] * extra,
        out_specs=jax.tree.map(lambda _: VMEM, outs),
        compiler_params=pltpu.CompilerParams(vmem_limit_bytes=limit),
    )(*ins, *beside)


def room(size):
    return pl.pallas_call(
        lambda out: None,
        out_shape=like((size, 1024), f32),
        out_specs=pl.BlockSpec(memory_space=pl.ANY),
    )()


def like(shape, dtype):
    return jax.ShapeDtypeStruct(shape, dtype)


def swap(x, distance):
    size = lax.axis_size("seq")
    return lax.ppermute(x, "seq", [(i, i ^ distance) for i in range(size)])


def pack_kernel(outer, kv_ref, mask_ref, x_ref, send_ref, *outs):
    me = lax.axis_index("seq")
    z, y = me // QUAD, (me // 2) % 2
    keys = kv_ref.shape[1]
    rows = mask_ref.shape[0]
    pieces = [x_ref[:, at : at + HEAD_DIM] for at in range(0, x_ref.shape[1], HEAD_DIM)]
    lane = lax.broadcasted_iota(jnp.int32, (rows, HEAD_DIM), 1)
    mask = jnp.zeros((rows, HEAD_DIM), f32)
    for head in range(mask_ref.shape[1]):
        live = (mask_ref[:, head : head + 1] == 1).astype(f32)
        mask = jnp.where(lane == head, jnp.broadcast_to(live, mask.shape), mask)
    pieces.append(mask.astype(bf16))
    for k in range(outer):
        peer = jnp.bitwise_xor(z, k)
        cols = pl.ds(pl.multiple_of((2 * peer + y) * HEAD_DIM, HEAD_DIM), HEAD_DIM)
        outs[k][0:keys, :] = kv_ref[0, :, cols]
        for i, piece in enumerate(pieces):
            outs[k][keys + i * rows : keys + (i + 1) * rows, :] = piece
        cols = pl.ds(pl.multiple_of((2 * peer + 1 - y) * HEAD_DIM, HEAD_DIM), HEAD_DIM)
        at = slice(k * HEAD_DIM, (k + 1) * HEAD_DIM)
        send_ref[0:keys, at] = kv_ref[0, :, cols]
        send_ref[keys : 2 * keys, at] = kv_ref[1, :, cols]


def unpack_kernel(keys, *refs):
    line_ref = refs[-1]
    rows = line_ref.shape[0]
    at = 0
    for ref in refs[:-1]:
        for i in range((ref.shape[0] - keys) // rows):
            line_ref[:, at : at + HEAD_DIM] = ref[keys + i * rows : keys + (i + 1) * rows, :]
            at += HEAD_DIM


def z_distance(slot, core):
    return jnp.where(core == 0, Z_ORDER[0][slot], Z_ORDER[1][slot])


def route_kernel(outer, kv_ref, other_ref, *outs):
    me = lax.axis_index("seq")
    z, y = me // QUAD, (me // 2) % 2
    keys = kv_ref.shape[1]
    for slot, out in enumerate(outs):
        k = z_distance(slot, me % 2)
        head = 2 * jnp.bitwise_xor(z, k) + y
        cols = pl.ds(pl.multiple_of(head * HEAD_DIM, HEAD_DIM), HEAD_DIM)
        out[0:keys, :] = kv_ref[1, :, cols]
        out[keys:, :] = other_ref[:, pl.ds(pl.multiple_of(k * HEAD_DIM, HEAD_DIM), HEAD_DIM)]


def cache_kernel(outer, keys, *refs):
    firsts, rests, out_ref = refs[:outer], refs[outer : 2 * outer], refs[2 * outer]
    core = lax.axis_index("seq") % 2
    for i in range(outer):
        at = 4 * i * keys
        for at_core in range(2):

            @pl.when(core == at_core)
            def _():
                out_ref[at : at + keys, :] = firsts[Z_ORDER[at_core][i]][0:keys, :]

        out_ref[at + keys : at + 4 * keys, :] = rests[i][...]


def stack_kernel(axis, *refs):
    at = 0
    for ref in refs[:-1]:
        size = ref.shape[axis]
        if axis == 0:
            refs[-1][at : at + size, :] = ref[...]
        else:
            refs[-1][:, at : at + size] = ref[...]
        at += size


def stacked(parts, axis, beside=()):
    shape = list(parts[0].shape)
    shape[axis] = sum(p.shape[axis] for p in parts)
    return call(functools.partial(stack_kernel, axis), like(tuple(shape), parts[0].dtype), parts, beside)


def normed_chunks(wide, chunks, gain_ref):
    squares = None
    for source, load in chunks:
        v = load().astype(f32)
        s = jnp.sum(v * v, axis=1, keepdims=True)
        squares = s if squares is None else squares + s
    inverse = lax.rsqrt(squares / (len(chunks) * wide) + eps)
    for source, load in chunks:
        at = pl.ds(pl.multiple_of(source * wide, wide), wide)
        yield at, (load().astype(f32) * inverse * gain_ref[:, at].astype(f32)).astype(bf16)


def to_members(parts):
    size = lax.axis_size("seq")
    groups = [list(range(core, size, 2)) for core in range(2)]
    return lax.all_to_all(parts, "seq", 0, 0, axis_index_groups=groups, tiled=True)


def member(i, other):
    core = lax.axis_index("seq") % 2
    return 2 * i + (1 - core if other else core)


def line_of(outer, *nears):
    return [QUAD * k + j for j in nears for k in range(outer)]


def line_chunks(outer, wide, refs):
    me = lax.axis_index("seq")
    lines = [line_of(outer, near) for near in range(QUAD)]
    step = wide + HEAD_DIM
    return [
        (jnp.bitwise_xor(me, distance), lambda r=ref, i=i: r[:, i * step : i * step + wide])
        for ref, line in zip(refs, lines)
        for i, distance in enumerate(line)
    ]


def line_mask(wide, ref, i):
    at = pl.multiple_of(i * (wide + HEAD_DIM) + wide, HEAD_DIM)
    tile = ref[:, pl.ds(at, HEAD_DIM)].astype(f32)
    lane = lax.broadcasted_iota(jnp.int32, tile.shape, 1)
    mine = jnp.where(lane == lax.axis_index("seq") // 2, tile, 0.0)
    return jnp.broadcast_to(jnp.sum(mine, axis=1, keepdims=True), tile.shape)


def in_line(near, z):
    return QUAD * z + jnp.bitwise_xor(lax.axis_index("seq") % QUAD, near)


def z_line_chunks(wide, refs):
    return [
        (in_line(near, z), lambda r=ref, z=z: r[:, z * wide : (z + 1) * wide])
        for near, ref in enumerate(refs)
        for z in range(ref.shape[1] // wide)
    ]


def query_kernel(outer, wide, *refs):
    gain_ref, w_ref, out_ref = refs[QUAD:]
    total = None
    for at, chunk in normed_chunks(wide, line_chunks(outer, wide, refs[:QUAD]), gain_ref):
        term = jnp.dot(chunk, w_ref[at, :], preferred_element_type=f32)
        total = term if total is None else total + term
    out_ref[...] = total.astype(bf16)


def scatter_dot(wide, other, left, w_ref, out_ref):
    for i in range(out_ref.shape[0]):
        at = pl.ds(pl.multiple_of(member(i, other) * wide, wide), wide)
        out_ref[i] = jnp.dot(left, w_ref[:, at], preferred_element_type=f32)


def line_dot(wide, nears, left, w_ref, out_ref):
    outer = out_ref.shape[1] // (len(nears) * wide)
    for i, near in enumerate(nears):
        for z in range(outer):
            at = pl.ds(pl.multiple_of(in_line(near, z) * wide, wide), wide)
            to = (i * outer + z) * wide
            out_ref[:, to : to + wide] = jnp.dot(left, w_ref[:, at], preferred_element_type=f32)


def keep_kernel(wide, left_ref, w_ref, out_ref):
    scatter_dot(wide, False, left_ref[...], w_ref, out_ref)


def keep_line_kernel(wide, left_ref, w_ref, out_ref):
    line_dot(wide, (0, 2), left_ref[...], w_ref, out_ref)


def span_states(q_ref, cache_ref, masks):
    heads = q_ref.shape[1] // HEAD_DIM
    scale = 1.0 / HEAD_DIM**0.5
    keys = cache_ref.shape[0] // (2 * len(masks))
    queries = jnp.concatenate(
        [q_ref[:, h * HEAD_DIM : (h + 1) * HEAD_DIM] for h in range(heads)], axis=0
    )
    scores = [
        lax.dot_general(
            queries,
            cache_ref[2 * i * keys : (2 * i + 1) * keys, :],
            (((1,), (1,)), ((), ())),
            preferred_element_type=f32,
        )
        * scale
        for i in range(len(masks))
    ]
    lives = [jnp.concatenate([mask] * heads, axis=0) > 0.5 for mask in masks]
    scores = [jnp.where(live, score, floor_score) for live, score in zip(lives, scores)]
    tops = [jnp.max(score, axis=1, keepdims=True) for score in scores]
    weights = [
        jnp.where(live, jnp.exp(score - top), 0.0) for live, score, top in zip(lives, scores, tops)
    ]
    totals = [jnp.sum(weight, axis=1, keepdims=True) for weight in weights]
    accums = [
        jnp.dot(
            weight.astype(bf16),
            cache_ref[(2 * i + 1) * keys : (2 * i + 2) * keys, :],
            preferred_element_type=f32,
        )
        for i, weight in enumerate(weights)
    ]
    return list(zip(tops, totals, accums))


def combined(states):
    top = functools.reduce(jnp.maximum, [s[0] for s in states])
    total = accum = None
    for t, s, a in states:
        factor = jnp.exp(t - top)
        total = s * factor if total is None else total + s * factor
        accum = a * factor if accum is None else accum + a * factor
    return top, total, accum


def early_kernel(outer, wide, q_ref, cache_ref, line_ref, other_ref, top_ref, total_ref, accum_ref):
    core = lax.axis_index("seq") % 2
    masks = [
        line_mask(wide, ref, z_distance(slot, core))
        for slot in range(outer)
        for ref in (line_ref, other_ref)
    ]
    top, total, accum_ref[...] = combined(span_states(q_ref, cache_ref, masks))
    top_ref[...] = jnp.broadcast_to(top, top_ref.shape)
    total_ref[...] = jnp.broadcast_to(total, total_ref.shape)


def attend_kernel(
    outer, wide, q_ref, top_ref, total_ref, accum_ref, cache_ref, core_ref, far_ref, w_ref, left_ref, send_ref
):
    rows = q_ref.shape[0]
    heads = q_ref.shape[1] // HEAD_DIM
    core = 1 - lax.axis_index("seq") % 2
    masks = [
        line_mask(wide, ref, z_distance(slot, core))
        for slot in range(outer)
        for ref in (core_ref, far_ref)
    ]
    states = span_states(q_ref, cache_ref, masks)
    states.append((top_ref[:, 0:1], total_ref[:, 0:1], accum_ref[...]))
    _, total, accum = combined(states)
    attended = (accum / total).astype(bf16)
    attended = jnp.concatenate([attended[h * rows : (h + 1) * rows] for h in range(heads)], axis=1)
    left_ref[...] = attended
    line_dot(wide, (1, 3), attended, w_ref, send_ref)


def hidden_kernel(wide, *refs):
    gain_ref, gate_ref, up_ref, down_ref, left_ref, send_ref = refs[QUAD:]
    gate = up = None
    for at, chunk in normed_chunks(wide, z_line_chunks(wide, refs[:QUAD]), gain_ref):
        g = jnp.dot(chunk, gate_ref[at, :], preferred_element_type=f32)
        u = jnp.dot(chunk, up_ref[at, :], preferred_element_type=f32)
        gate = g if gate is None else gate + g
        up = u if up is None else up + u
    hidden = (gate / (1.0 + jnp.exp(-gate)) * up).astype(bf16)
    left_ref[...] = hidden
    scatter_dot(wide, True, hidden, down_ref, send_ref)


def add_kernel(own_ref, recv_ref, out_ref):
    out_ref[...] = (own_ref[...] + recv_ref[...]).astype(out_ref.dtype)


def coded(out_ref, sums):
    rows, wide = sums.shape
    largest = jnp.max(jnp.abs(sums), axis=1, keepdims=True)
    level = jnp.ceil(jnp.log(jnp.maximum(largest, 1e-30)) * STEPS)
    scale = jnp.exp(level * (-1.0 / STEPS)) * RANGE
    out_ref[:, 0:wide] = jnp.round(sums * scale).astype(jnp.int32).astype(jnp.int16)
    level = jnp.broadcast_to(level, (rows, HEAD_DIM)).astype(jnp.int32)
    out_ref[:, wide:] = level.astype(jnp.int16)


def decoded(ref):
    wide = ref.shape[1] - HEAD_DIM
    level = ref[:, wide:].astype(jnp.int32).astype(f32)[:, 0:1]
    scale = jnp.exp(level * (1.0 / STEPS)) * (1.0 / RANGE)
    return ref[:, 0:wide].astype(jnp.int32).astype(f32) * scale


def chip_kernel(own_ref, recv_ref, keep_ref, send_ref):
    half = own_ref.shape[1] // 2
    keep_ref[...] = own_ref[:, :half] + recv_ref[:, :half]
    coded(send_ref, own_ref[:, half:] + recv_ref[:, half:])


def pair_kernel(keep_ref, recv_ref, out_ref):
    coded(out_ref, keep_ref[...] + decoded(recv_ref))


def stream_kernel(wide, x_ref, *refs):
    parts, (line_ref, own_ref) = refs[:-2], refs[-2:]
    z = lax.axis_index("seq") // QUAD
    sums = [decoded(part) for part in parts]
    while len(sums) > 1:
        sums = [first + second for first, second in zip(sums[0::2], sums[1::2])]
    for to in range(len(parts)):
        at = pl.multiple_of(jnp.bitwise_xor(z, to) * (wide + HEAD_DIM), HEAD_DIM)
        cols = slice(to * wide, (to + 1) * wide)
        line_ref[:, cols] = (x_ref[:, pl.ds(at, wide)].astype(f32) + sums[0][:, cols]).astype(bf16)
    own_ref[...] = line_ref[:, pl.ds(pl.multiple_of(z * wide, wide), wide)]


def final_kernel(base_ref, parts_ref, out_ref):
    total = parts_ref[0].astype(f32)
    for i in range(1, parts_ref.shape[0]):
        total = total + parts_ref[i].astype(f32)
    out_ref[...] = (base_ref[...].astype(f32) + total).astype(bf16)


def z_swapped(parts):
    arrived = [swap(part, QUAD * k) for k, part in reversed(list(enumerate(parts))) if k > 0]
    return [parts[0], *reversed(arrived)]


def z_routed(parts):
    size = lax.axis_size("seq")
    return [parts[0]] + [
        lax.ppermute(part, "seq", [(i, i ^ QUAD * Z_ORDER[i % 2][slot]) for i in range(size)])
        for slot, part in list(enumerate(parts))[1:]
    ]


def near_gathered(line):
    y = swap(line, 2)
    core, far = swap(line, 1), swap(y, 1)
    return [line, core, y, far]


def updated(x_line, send, left, weight, wide, beside):
    rows, columns = send.shape
    half = columns // 2
    code = like((rows, half + HEAD_DIM), jnp.int16)
    far = swap(send, 1)
    own = call(functools.partial(keep_line_kernel, wide), like(send.shape, f32), [left, weight])
    keep, send = call(chip_kernel, [like((rows, half), f32), code], [own, far], beside)
    sums = call(pair_kernel, code, [keep, swap(send, 2)], beside)
    return call(
        functools.partial(stream_kernel, wide),
        [like((rows, half), bf16), like((rows, wide), bf16)],
        [x_line, *z_routed([sums] * (half // wide))],
    )


def scattered(base, send, left, weight, wide):
    far = swap(send, 1)
    own = call(functools.partial(keep_kernel, wide), like(send.shape, f32), [left, weight])
    sums = call(add_kernel, like(send.shape, bf16), [own, far])
    return call(final_kernel, like(base.shape, bf16), [base, to_members(sums)])


def local_pairs(
    x_rows, attn_gain, q_weight, o_weight, mlp_gain, gate_weight, up_weight, down_weight, kv_cache, block_mask
):
    rows, wide = x_rows.shape
    outer = lax.axis_size("seq") // QUAD
    columns = q_weight.shape[1]
    beside = [room(18432)]
    attn_gain = attn_gain.reshape(1, -1)
    mlp_gain = mlp_gain.reshape(1, -1)
    members = lax.axis_size("seq") // 2
    partial_sums = like((members, rows, wide), f32)

    keys = kv_cache.shape[1]
    step = wide + HEAD_DIM
    send, *firsts = call(
        functools.partial(pack_kernel, outer),
        [like((2 * keys, outer * HEAD_DIM), bf16)]
        + [like((keys + step // HEAD_DIM * rows, HEAD_DIM), bf16)] * outer,
        [kv_cache, block_mask[:, :, 0], x_rows],
        beside,
    )
    other = swap(send, 2)
    firsts = z_swapped(firsts)
    line = call(functools.partial(unpack_kernel, keys), like((rows, outer * step), bf16), firsts)
    routed = call(
        functools.partial(route_kernel, outer),
        [like((3 * keys, HEAD_DIM), bf16)] * outer,
        [kv_cache, other],
        [line, *beside],
    )
    routed = z_routed(routed)
    x_parts = near_gathered(line)
    queries = call(
        functools.partial(query_kernel, outer, wide),
        like((rows, columns), bf16),
        [*x_parts, attn_gain, q_weight],
    )
    cache = call(
        functools.partial(cache_kernel, outer, keys),
        like((4 * outer * keys, HEAD_DIM), bf16),
        [*firsts, *routed],
        [queries],
    )
    far_cache = swap(cache, 1)
    tall = like((columns // HEAD_DIM * rows, HEAD_DIM), f32)
    early = call(
        functools.partial(early_kernel, outer, wide), [tall] * 3, [queries, cache, *x_parts[0::2]]
    )
    left, send = call(
        functools.partial(attend_kernel, outer, wide),
        [like((rows, columns), bf16), like((rows, 2 * outer * wide), f32)],
        [queries, *early, far_cache, *x_parts[1::2], o_weight],
    )
    line, stream = updated(x_parts[0], send, left, o_weight, wide, beside)
    left, send = call(
        functools.partial(hidden_kernel, wide),
        [like((rows, gate_weight.shape[1]), bf16), partial_sums],
        [*near_gathered(line), mlp_gain, gate_weight, up_weight, down_weight],
    )
    return scattered(stream, send, left, down_weight, wide)


def rms_norm(values, gain):
    wide = values.astype(f32)
    inverse = lax.rsqrt(jnp.mean(wide * wide, axis=-1, keepdims=True) + eps)
    return (wide * inverse * gain.astype(f32)).astype(bf16)


def combine_states(first, second):
    top_a, total_a, accum_a = first
    top_b, total_b, accum_b = second
    top = jnp.maximum(top_a, top_b)
    factor_a = jnp.exp(top_a - top)
    factor_b = jnp.exp(top_b - top)
    return (
        top,
        total_a * factor_a + total_b * factor_b,
        accum_a * factor_a[..., None] + accum_b * factor_b[..., None],
    )


def combined_all(x, axis, combine):
    everything = jax.tree.map(lambda part: lax.all_gather(part, axis), x)
    initial = jax.tree.map(lambda part: part[0], everything)

    def turn(k, so_far):
        return combine(so_far, jax.tree.map(lambda part: part[k], everything))

    return lax.fori_loop(1, lax.axis_size(axis), turn, initial)


def summed(weight, left):
    product = lax.dot_general(weight, left, (((0,), (1,)), ((), ())), preferred_element_type=f32)
    return lax.psum_scatter(product, "seq", scatter_dimension=0, tiled=True).T


def local_tokens(
    x_rows, attn_gain, q_weight, o_weight, mlp_gain, gate_weight, up_weight, down_weight, kv_cache, block_mask
):
    rows = x_rows.shape[0]
    group = HEADS // KV_HEADS
    key_len = kv_cache.shape[1]
    spans = key_len // BLOCK
    scale = 1.0 / HEAD_DIM**0.5
    normed = rms_norm(lax.all_gather(x_rows, "seq", axis=1, tiled=True), attn_gain)
    query_part = jnp.dot(normed, q_weight, preferred_element_type=f32).astype(bf16)
    queries = lax.all_gather(query_part, "seq", axis=1, tiled=True)

    def one_group(index):
        def cut(array, width):
            return lax.dynamic_slice_in_dim(array, index * width, width, 1)

        query_group = cut(queries, group * HEAD_DIM).reshape(rows, group, HEAD_DIM)
        scores = (
            jnp.einsum("rhd,kd->rhk", query_group, cut(kv_cache[0], HEAD_DIM), preferred_element_type=f32)
            * scale
        )
        scores = scores.reshape(rows, group, spans, BLOCK)
        live = (cut(block_mask, 1)[:, 0, :] == 1)[:, None, :, None]
        masked = jnp.where(live, scores, floor_score)
        top = jnp.max(masked, axis=(2, 3))
        weights = jnp.where(live, jnp.exp(masked - top[..., None, None]), 0.0)
        rounded = weights.astype(bf16).reshape(rows, group, key_len)
        accum = jnp.einsum("rhk,kd->rhd", rounded, cut(kv_cache[1], HEAD_DIM), preferred_element_type=f32)
        return (top, jnp.sum(weights, axis=(2, 3)), accum)

    states = lax.map(one_group, jnp.arange(KV_HEADS, dtype=jnp.int32))
    states = jax.tree.map(lambda part: jnp.moveaxis(part, 0, 1), states)
    columns = q_weight.shape[1]
    top, total, accum = combined_all(states, "seq", combine_states)
    attended = (accum / total[..., None]).reshape(rows, HEADS * HEAD_DIM).astype(bf16)
    attn_cols = lax.dynamic_slice_in_dim(attended, lax.axis_index("seq") * columns, columns, 1)
    stream = (x_rows.astype(f32) + summed(o_weight, attn_cols)).astype(bf16)
    normed_two = rms_norm(lax.all_gather(stream, "seq", axis=1, tiled=True), mlp_gain)
    gate = jnp.dot(normed_two, gate_weight, preferred_element_type=f32)
    upward = jnp.dot(normed_two, up_weight, preferred_element_type=f32)
    hidden = (jax.nn.silu(gate) * upward).astype(bf16)
    return (stream.astype(f32) + summed(down_weight, hidden)).astype(bf16)


def solution(mesh):
    pairs = mesh.shape["seq"] == 2 * KV_HEADS
    return jax.shard_map(
        local_pairs if pairs else local_tokens,
        mesh=mesh,
        in_specs=(
            P("group", "seq"),
            P(),
            P(None, "seq"),
            P("seq", None),
            P(),
            P(None, "seq"),
            P(None, "seq"),
            P("seq", None),
            P(None, ("group", "seq"), None),
            P("group", None, "seq"),
        ),
        out_specs=P("group", "seq"),
        check_vma=False,
    )
```

```python
import functools

import jax
import jax.numpy as jnp
from jax import lax
from jax.experimental import pallas as pl
from jax.experimental.pallas import tpu as pltpu
from jax.sharding import PartitionSpec as P

HEADS = 64
KV_HEADS = 8
HEAD_DIM = 128
BLOCK = 128
QUAD = 4
RANGE = 32000.0
STEPS = 256.0
Z_ORDER = ((0, 3, 1, 2), (0, 2, 3, 1))

eps = 1e-05
floor_score = -1e30

bf16 = jnp.bfloat16
f32 = jnp.float32
VMEM = pl.BlockSpec(memory_space=pltpu.VMEM)


def call(body, outs, ins, beside=(), limit=4 * 2**20):
    count, extra = len(ins), len(beside)

    def kernel(*refs):
        body(*refs[:count], *refs[count + extra :])

    return pl.pallas_call(
        kernel,
        out_shape=outs,
        in_specs=[VMEM] * count + [pl.BlockSpec(memory_space=pl.ANY)] * extra,
        out_specs=jax.tree.map(lambda _: VMEM, outs),
        compiler_params=pltpu.CompilerParams(vmem_limit_bytes=limit),
    )(*ins, *beside)


def room(size):
    return pl.pallas_call(
        lambda out: None,
        out_shape=like((size, 1024), f32),
        out_specs=pl.BlockSpec(memory_space=pl.ANY),
    )()


def like(shape, dtype):
    return jax.ShapeDtypeStruct(shape, dtype)


def swap(x, distance):
    size = lax.axis_size("seq")
    return lax.ppermute(x, "seq", [(i, i ^ distance) for i in range(size)])


def pack_kernel(outer, kv_ref, mask_ref, x_ref, send_ref, *outs):
    me = lax.axis_index("seq")
    z, y = me // QUAD, (me // 2) % 2
    keys = kv_ref.shape[1]
    rows = mask_ref.shape[0]
    pieces = [x_ref[:, at : at + HEAD_DIM] for at in range(0, x_ref.shape[1], HEAD_DIM)]
    lane = lax.broadcasted_iota(jnp.int32, (rows, HEAD_DIM), 1)
    mask = jnp.zeros((rows, HEAD_DIM), f32)
    for head in range(mask_ref.shape[1]):
        live = (mask_ref[:, head : head + 1] == 1).astype(f32)
        mask = jnp.where(lane == head, jnp.broadcast_to(live, mask.shape), mask)
    pieces.append(mask.astype(bf16))
    for k in range(outer):
        peer = jnp.bitwise_xor(z, k)
        cols = pl.ds(pl.multiple_of((2 * peer + y) * HEAD_DIM, HEAD_DIM), HEAD_DIM)
        outs[k][0:keys, :] = kv_ref[0, :, cols]
        for i, piece in enumerate(pieces):
            outs[k][keys + i * rows : keys + (i + 1) * rows, :] = piece
        cols = pl.ds(pl.multiple_of((2 * peer + 1 - y) * HEAD_DIM, HEAD_DIM), HEAD_DIM)
        at = slice(k * HEAD_DIM, (k + 1) * HEAD_DIM)
        send_ref[0:keys, at] = kv_ref[0, :, cols]
        send_ref[keys : 2 * keys, at] = kv_ref[1, :, cols]


def unpack_kernel(keys, *refs):
    line_ref = refs[-1]
    rows = line_ref.shape[0]
    at = 0
    for ref in refs[:-1]:
        for i in range((ref.shape[0] - keys) // rows):
            line_ref[:, at : at + HEAD_DIM] = ref[keys + i * rows : keys + (i + 1) * rows, :]
            at += HEAD_DIM


def z_distance(slot, core):
    return jnp.where(core == 0, Z_ORDER[0][slot], Z_ORDER[1][slot])


def route_kernel(outer, kv_ref, other_ref, *outs):
    me = lax.axis_index("seq")
    z, y = me // QUAD, (me // 2) % 2
    keys = kv_ref.shape[1]
    for slot, out in enumerate(outs):
        k = z_distance(slot, me % 2)
        head = 2 * jnp.bitwise_xor(z, k) + y
        cols = pl.ds(pl.multiple_of(head * HEAD_DIM, HEAD_DIM), HEAD_DIM)
        out[0:keys, :] = kv_ref[1, :, cols]
        out[keys:, :] = other_ref[:, pl.ds(pl.multiple_of(k * HEAD_DIM, HEAD_DIM), HEAD_DIM)]


def cache_kernel(outer, keys, *refs):
    firsts, rests, out_ref = refs[:outer], refs[outer : 2 * outer], refs[2 * outer]
    core = lax.axis_index("seq") % 2
    for i in range(outer):
        at = 4 * i * keys
        for at_core in range(2):

            @pl.when(core == at_core)
            def _():
                out_ref[at : at + keys, :] = firsts[Z_ORDER[at_core][i]][0:keys, :]

        out_ref[at + keys : at + 4 * keys, :] = rests[i][...]


def stack_kernel(axis, *refs):
    at = 0
    for ref in refs[:-1]:
        size = ref.shape[axis]
        if axis == 0:
            refs[-1][at : at + size, :] = ref[...]
        else:
            refs[-1][:, at : at + size] = ref[...]
        at += size


def stacked(parts, axis, beside=()):
    shape = list(parts[0].shape)
    shape[axis] = sum(p.shape[axis] for p in parts)
    return call(functools.partial(stack_kernel, axis), like(tuple(shape), parts[0].dtype), parts, beside)


def normed_chunks(wide, chunks, gain_ref):
    squares = None
    for source, load in chunks:
        v = load().astype(f32)
        s = jnp.sum(v * v, axis=1, keepdims=True)
        squares = s if squares is None else squares + s
    inverse = lax.rsqrt(squares / (len(chunks) * wide) + eps)
    for source, load in chunks:
        at = pl.ds(pl.multiple_of(source * wide, wide), wide)
        yield at, (load().astype(f32) * inverse * gain_ref[:, at].astype(f32)).astype(bf16)


def to_members(parts):
    size = lax.axis_size("seq")
    groups = [list(range(core, size, 2)) for core in range(2)]
    return lax.all_to_all(parts, "seq", 0, 0, axis_index_groups=groups, tiled=True)


def member(i, other):
    core = lax.axis_index("seq") % 2
    return 2 * i + (1 - core if other else core)


def line_of(outer, *nears):
    return [QUAD * k + j for j in nears for k in range(outer)]


def line_chunks(outer, wide, refs):
    me = lax.axis_index("seq")
    lines = [line_of(outer, near) for near in range(QUAD)]
    step = wide + HEAD_DIM
    return [
        (jnp.bitwise_xor(me, distance), lambda r=ref, i=i: r[:, i * step : i * step + wide])
        for ref, line in zip(refs, lines)
        for i, distance in enumerate(line)
    ]


def line_mask(wide, ref, i):
    at = pl.multiple_of(i * (wide + HEAD_DIM) + wide, HEAD_DIM)
    tile = ref[:, pl.ds(at, HEAD_DIM)].astype(f32)
    lane = lax.broadcasted_iota(jnp.int32, tile.shape, 1)
    mine = jnp.where(lane == lax.axis_index("seq") // 2, tile, 0.0)
    return jnp.broadcast_to(jnp.sum(mine, axis=1, keepdims=True), tile.shape)


def in_line(near, z):
    return QUAD * z + jnp.bitwise_xor(lax.axis_index("seq") % QUAD, near)


def z_line_chunks(wide, refs):
    return [
        (in_line(near, z), lambda r=ref, z=z: r[:, z * wide : (z + 1) * wide])
        for near, ref in enumerate(refs)
        for z in range(ref.shape[1] // wide)
    ]


def query_kernel(outer, wide, *refs):
    gain_ref, w_ref, out_ref = refs[QUAD:]
    total = None
    for at, chunk in normed_chunks(wide, line_chunks(outer, wide, refs[:QUAD]), gain_ref):
        term = jnp.dot(chunk, w_ref[at, :], preferred_element_type=f32)
        total = term if total is None else total + term
    out_ref[...] = total.astype(bf16)


def scatter_dot(wide, other, left, w_ref, out_ref):
    for i in range(out_ref.shape[0]):
        at = pl.ds(pl.multiple_of(member(i, other) * wide, wide), wide)
        out_ref[i] = jnp.dot(left, w_ref[:, at], preferred_element_type=f32)


def line_dot(wide, nears, left, w_ref, out_ref):
    outer = out_ref.shape[1] // (len(nears) * wide)
    for i, near in enumerate(nears):
        for z in range(outer):
            at = pl.ds(pl.multiple_of(in_line(near, z) * wide, wide), wide)
            to = (i * outer + z) * wide
            out_ref[:, to : to + wide] = jnp.dot(left, w_ref[:, at], preferred_element_type=f32)


def keep_kernel(wide, left_ref, w_ref, out_ref):
    scatter_dot(wide, False, left_ref[...], w_ref, out_ref)


def line_kernel(wide, near, left_ref, w_ref, out_ref):
    line_dot(wide, (near,), left_ref[...], w_ref, out_ref)


def span_states(q_ref, cache_ref, masks):
    heads = q_ref.shape[1] // HEAD_DIM
    scale = 1.0 / HEAD_DIM**0.5
    keys = cache_ref.shape[0] // (2 * len(masks))
    queries = jnp.concatenate(
        [q_ref[:, h * HEAD_DIM : (h + 1) * HEAD_DIM] for h in range(heads)], axis=0
    )
    scores = [
        lax.dot_general(
            queries,
            cache_ref[2 * i * keys : (2 * i + 1) * keys, :],
            (((1,), (1,)), ((), ())),
            preferred_element_type=f32,
        )
        * scale
        for i in range(len(masks))
    ]
    lives = [jnp.concatenate([mask] * heads, axis=0) > 0.5 for mask in masks]
    scores = [jnp.where(live, score, floor_score) for live, score in zip(lives, scores)]
    tops = [jnp.max(score, axis=1, keepdims=True) for score in scores]
    weights = [
        jnp.where(live, jnp.exp(score - top), 0.0) for live, score, top in zip(lives, scores, tops)
    ]
    totals = [jnp.sum(weight, axis=1, keepdims=True) for weight in weights]
    accums = [
        jnp.dot(
            weight.astype(bf16),
            cache_ref[(2 * i + 1) * keys : (2 * i + 2) * keys, :],
            preferred_element_type=f32,
        )
        for i, weight in enumerate(weights)
    ]
    return list(zip(tops, totals, accums))


def combined(states):
    top = functools.reduce(jnp.maximum, [s[0] for s in states])
    total = accum = None
    for t, s, a in states:
        factor = jnp.exp(t - top)
        total = s * factor if total is None else total + s * factor
        accum = a * factor if accum is None else accum + a * factor
    return top, total, accum


def early_kernel(outer, wide, q_ref, cache_ref, line_ref, other_ref, top_ref, total_ref, accum_ref):
    core = lax.axis_index("seq") % 2
    masks = [
        line_mask(wide, ref, z_distance(slot, core))
        for slot in range(outer)
        for ref in (line_ref, other_ref)
    ]
    top, total, accum_ref[...] = combined(span_states(q_ref, cache_ref, masks))
    top_ref[...] = jnp.broadcast_to(top, top_ref.shape)
    total_ref[...] = jnp.broadcast_to(total, total_ref.shape)


def attend_kernel(
    outer, wide, q_ref, top_ref, total_ref, accum_ref, cache_ref, core_ref, far_ref, w_ref, left_ref, send_ref
):
    rows = q_ref.shape[0]
    heads = q_ref.shape[1] // HEAD_DIM
    core = 1 - lax.axis_index("seq") % 2
    masks = [
        line_mask(wide, ref, z_distance(slot, core))
        for slot in range(outer)
        for ref in (core_ref, far_ref)
    ]
    states = span_states(q_ref, cache_ref, masks)
    states.append((top_ref[:, 0:1], total_ref[:, 0:1], accum_ref[...]))
    _, total, accum = combined(states)
    attended = (accum / total).astype(bf16)
    attended = jnp.concatenate([attended[h * rows : (h + 1) * rows] for h in range(heads)], axis=1)
    left_ref[...] = attended
    line_dot(wide, (3,), attended, w_ref, send_ref)


def hidden_kernel(wide, *refs):
    gain_ref, gate_ref, up_ref, down_ref, left_ref, send_ref = refs[QUAD:]
    gate = up = None
    for at, chunk in normed_chunks(wide, z_line_chunks(wide, refs[:QUAD]), gain_ref):
        g = jnp.dot(chunk, gate_ref[at, :], preferred_element_type=f32)
        u = jnp.dot(chunk, up_ref[at, :], preferred_element_type=f32)
        gate = g if gate is None else gate + g
        up = u if up is None else up + u
    hidden = (gate / (1.0 + jnp.exp(-gate)) * up).astype(bf16)
    left_ref[...] = hidden
    scatter_dot(wide, True, hidden, down_ref, send_ref)


def add_kernel(own_ref, recv_ref, out_ref):
    out_ref[...] = (own_ref[...] + recv_ref[...]).astype(out_ref.dtype)


def coded(out_ref, sums):
    rows, wide = sums.shape
    largest = jnp.max(jnp.abs(sums), axis=1, keepdims=True)
    level = jnp.ceil(jnp.log(jnp.maximum(largest, 1e-30)) * STEPS)
    scale = jnp.exp(level * (-1.0 / STEPS)) * RANGE
    out_ref[:, 0:wide] = jnp.round(sums * scale).astype(jnp.int32).astype(jnp.int16)
    level = jnp.broadcast_to(level, (rows, HEAD_DIM)).astype(jnp.int32)
    out_ref[:, wide:] = level.astype(jnp.int16)


def decoded(ref):
    wide = ref.shape[1] - HEAD_DIM
    level = ref[:, wide:].astype(jnp.int32).astype(f32)[:, 0:1]
    scale = jnp.exp(level * (1.0 / STEPS)) * (1.0 / RANGE)
    return ref[:, 0:wide].astype(jnp.int32).astype(f32) * scale


def chip_kernel(own_ref, core_ref, out_ref):
    coded(out_ref, own_ref[...] + core_ref[...])


def pair_kernel(own_ref, core_ref, y_ref, out_ref):
    coded(out_ref, own_ref[...] + core_ref[...] + decoded(y_ref))


def stream_kernel(wide, x_ref, *refs):
    parts, (line_ref, own_ref) = refs[:-2], refs[-2:]
    z = lax.axis_index("seq") // QUAD
    sums = [decoded(part) for part in parts]
    while len(sums) > 1:
        sums = [first + second for first, second in zip(sums[0::2], sums[1::2])]
    for to in range(len(parts)):
        at = pl.multiple_of(jnp.bitwise_xor(z, to) * (wide + HEAD_DIM), HEAD_DIM)
        cols = slice(to * wide, (to + 1) * wide)
        line_ref[:, cols] = (x_ref[:, pl.ds(at, wide)].astype(f32) + sums[0][:, cols]).astype(bf16)
    own_ref[...] = line_ref[:, pl.ds(pl.multiple_of(z * wide, wide), wide)]


def final_kernel(base_ref, parts_ref, out_ref):
    total = parts_ref[0].astype(f32)
    for i in range(1, parts_ref.shape[0]):
        total = total + parts_ref[i].astype(f32)
    out_ref[...] = (base_ref[...].astype(f32) + total).astype(bf16)


def z_swapped(parts):
    arrived = [swap(part, QUAD * k) for k, part in reversed(list(enumerate(parts))) if k > 0]
    return [parts[0], *reversed(arrived)]


def z_routed(parts):
    size = lax.axis_size("seq")
    return [parts[0]] + [
        lax.ppermute(part, "seq", [(i, i ^ QUAD * Z_ORDER[i % 2][slot]) for i in range(size)])
        for slot, part in list(enumerate(parts))[1:]
    ]


def near_gathered(line):
    y = swap(line, 2)
    core, far = swap(line, 1), swap(y, 1)
    return [line, core, y, far]


def updated(x_line, send, left, weight, wide, beside):
    rows, half = send.shape
    line = like((rows, half), f32)
    code = like((rows, half + HEAD_DIM), jnp.int16)
    far = swap(send, 1)
    second = call(functools.partial(line_kernel, wide, 2), line, [left, weight])
    second = call(chip_kernel, code, [second, far])
    arrived = swap(second, 2)
    core = swap(call(functools.partial(line_kernel, wide, 1), line, [left, weight]), 1)
    own = call(functools.partial(line_kernel, wide, 0), line, [left, weight], [second])
    sums = call(pair_kernel, code, [own, core, arrived], beside * 2)
    return call(
        functools.partial(stream_kernel, wide),
        [like((rows, half), bf16), like((rows, wide), bf16)],
        [x_line, *z_routed([sums] * (half // wide))],
    )


def scattered(base, send, left, weight, wide):
    far = swap(send, 1)
    own = call(functools.partial(keep_kernel, wide), like(send.shape, f32), [left, weight])
    sums = call(add_kernel, like(send.shape, bf16), [own, far])
    return call(final_kernel, like(base.shape, bf16), [base, to_members(sums)])


def local_pairs(
    x_rows, attn_gain, q_weight, o_weight, mlp_gain, gate_weight, up_weight, down_weight, kv_cache, block_mask
):
    rows, wide = x_rows.shape
    outer = lax.axis_size("seq") // QUAD
    columns = q_weight.shape[1]
    beside = [room(18432)]
    attn_gain = attn_gain.reshape(1, -1)
    mlp_gain = mlp_gain.reshape(1, -1)
    members = lax.axis_size("seq") // 2
    partial_sums = like((members, rows, wide), f32)

    keys = kv_cache.shape[1]
    step = wide + HEAD_DIM
    send, *firsts = call(
        functools.partial(pack_kernel, outer),
        [like((2 * keys, outer * HEAD_DIM), bf16)]
        + [like((keys + step // HEAD_DIM * rows, HEAD_DIM), bf16)] * outer,
        [kv_cache, block_mask[:, :, 0], x_rows],
        beside,
    )
    other = swap(send, 2)
    firsts = z_swapped(firsts)
    line = call(functools.partial(unpack_kernel, keys), like((rows, outer * step), bf16), firsts)
    routed = call(
        functools.partial(route_kernel, outer),
        [like((3 * keys, HEAD_DIM), bf16)] * outer,
        [kv_cache, other],
        [line, *beside],
    )
    routed = z_routed(routed)
    x_parts = near_gathered(line)
    queries = call(
        functools.partial(query_kernel, outer, wide),
        like((rows, columns), bf16),
        [*x_parts, attn_gain, q_weight],
    )
    cache = call(
        functools.partial(cache_kernel, outer, keys),
        like((4 * outer * keys, HEAD_DIM), bf16),
        [*firsts, *routed],
        [queries],
    )
    far_cache = swap(cache, 1)
    tall = like((columns // HEAD_DIM * rows, HEAD_DIM), f32)
    early = call(
        functools.partial(early_kernel, outer, wide), [tall] * 3, [queries, cache, *x_parts[0::2]]
    )
    left, send = call(
        functools.partial(attend_kernel, outer, wide),
        [like((rows, columns), bf16), like((rows, outer * wide), f32)],
        [queries, *early, far_cache, *x_parts[1::2], o_weight],
    )
    line, stream = updated(x_parts[0], send, left, o_weight, wide, beside)
    left, send = call(
        functools.partial(hidden_kernel, wide),
        [like((rows, gate_weight.shape[1]), bf16), partial_sums],
        [*near_gathered(line), mlp_gain, gate_weight, up_weight, down_weight],
    )
    return scattered(stream, send, left, down_weight, wide)


def rms_norm(values, gain):
    wide = values.astype(f32)
    inverse = lax.rsqrt(jnp.mean(wide * wide, axis=-1, keepdims=True) + eps)
    return (wide * inverse * gain.astype(f32)).astype(bf16)


def combine_states(first, second):
    top_a, total_a, accum_a = first
    top_b, total_b, accum_b = second
    top = jnp.maximum(top_a, top_b)
    factor_a = jnp.exp(top_a - top)
    factor_b = jnp.exp(top_b - top)
    return (
        top,
        total_a * factor_a + total_b * factor_b,
        accum_a * factor_a[..., None] + accum_b * factor_b[..., None],
    )


def combined_all(x, axis, combine):
    everything = jax.tree.map(lambda part: lax.all_gather(part, axis), x)
    initial = jax.tree.map(lambda part: part[0], everything)

    def turn(k, so_far):
        return combine(so_far, jax.tree.map(lambda part: part[k], everything))

    return lax.fori_loop(1, lax.axis_size(axis), turn, initial)


def summed(weight, left):
    product = lax.dot_general(weight, left, (((0,), (1,)), ((), ())), preferred_element_type=f32)
    return lax.psum_scatter(product, "seq", scatter_dimension=0, tiled=True).T


def local_tokens(
    x_rows, attn_gain, q_weight, o_weight, mlp_gain, gate_weight, up_weight, down_weight, kv_cache, block_mask
):
    rows = x_rows.shape[0]
    group = HEADS // KV_HEADS
    key_len = kv_cache.shape[1]
    spans = key_len // BLOCK
    scale = 1.0 / HEAD_DIM**0.5
    normed = rms_norm(lax.all_gather(x_rows, "seq", axis=1, tiled=True), attn_gain)
    query_part = jnp.dot(normed, q_weight, preferred_element_type=f32).astype(bf16)
    queries = lax.all_gather(query_part, "seq", axis=1, tiled=True)

    def one_group(index):
        def cut(array, width):
            return lax.dynamic_slice_in_dim(array, index * width, width, 1)

        query_group = cut(queries, group * HEAD_DIM).reshape(rows, group, HEAD_DIM)
        scores = (
            jnp.einsum("rhd,kd->rhk", query_group, cut(kv_cache[0], HEAD_DIM), preferred_element_type=f32)
            * scale
        )
        scores = scores.reshape(rows, group, spans, BLOCK)
        live = (cut(block_mask, 1)[:, 0, :] == 1)[:, None, :, None]
        masked = jnp.where(live, scores, floor_score)
        top = jnp.max(masked, axis=(2, 3))
        weights = jnp.where(live, jnp.exp(masked - top[..., None, None]), 0.0)
        rounded = weights.astype(bf16).reshape(rows, group, key_len)
        accum = jnp.einsum("rhk,kd->rhd", rounded, cut(kv_cache[1], HEAD_DIM), preferred_element_type=f32)
        return (top, jnp.sum(weights, axis=(2, 3)), accum)

    states = lax.map(one_group, jnp.arange(KV_HEADS, dtype=jnp.int32))
    states = jax.tree.map(lambda part: jnp.moveaxis(part, 0, 1), states)
    columns = q_weight.shape[1]
    top, total, accum = combined_all(states, "seq", combine_states)
    attended = (accum / total[..., None]).reshape(rows, HEADS * HEAD_DIM).astype(bf16)
    attn_cols = lax.dynamic_slice_in_dim(attended, lax.axis_index("seq") * columns, columns, 1)
    stream = (x_rows.astype(f32) + summed(o_weight, attn_cols)).astype(bf16)
    normed_two = rms_norm(lax.all_gather(stream, "seq", axis=1, tiled=True), mlp_gain)
    gate = jnp.dot(normed_two, gate_weight, preferred_element_type=f32)
    upward = jnp.dot(normed_two, up_weight, preferred_element_type=f32)
    hidden = (jax.nn.silu(gate) * upward).astype(bf16)
    return (stream.astype(f32) + summed(down_weight, hidden)).astype(bf16)


def solution(mesh):
    pairs = mesh.shape["seq"] == 2 * KV_HEADS
    return jax.shard_map(
        local_pairs if pairs else local_tokens,
        mesh=mesh,
        in_specs=(
            P("group", "seq"),
            P(),
            P(None, "seq"),
            P("seq", None),
            P(),
            P(None, "seq"),
            P(None, "seq"),
            P("seq", None),
            P(None, ("group", "seq"), None),
            P("group", None, "seq"),
        ),
        out_specs=P("group", "seq"),
        check_vma=False,
    )
```

```python
import functools

import jax
import jax.numpy as jnp
from jax import lax
from jax.experimental import pallas as pl
from jax.experimental.pallas import tpu as pltpu
from jax.sharding import PartitionSpec as P

HEADS = 64
KV_HEADS = 8
HEAD_DIM = 128
BLOCK = 128
QUAD = 4
RANGE = 32000.0
STEPS = 256.0
Z_ORDER = ((0, 3, 1, 2), (0, 2, 3, 1))

eps = 1e-05
floor_score = -1e30

bf16 = jnp.bfloat16
f32 = jnp.float32
VMEM = pl.BlockSpec(memory_space=pltpu.VMEM)


def call(body, outs, ins, beside=(), limit=4 * 2**20):
    count, extra = len(ins), len(beside)

    def kernel(*refs):
        body(*refs[:count], *refs[count + extra :])

    return pl.pallas_call(
        kernel,
        out_shape=outs,
        in_specs=[VMEM] * count + [pl.BlockSpec(memory_space=pl.ANY)] * extra,
        out_specs=jax.tree.map(lambda _: VMEM, outs),
        compiler_params=pltpu.CompilerParams(vmem_limit_bytes=limit),
    )(*ins, *beside)


def room(size):
    return pl.pallas_call(
        lambda out: None,
        out_shape=like((size, 1024), f32),
        out_specs=pl.BlockSpec(memory_space=pl.ANY),
    )()


def like(shape, dtype):
    return jax.ShapeDtypeStruct(shape, dtype)


def swap(x, distance):
    size = lax.axis_size("seq")
    return lax.ppermute(x, "seq", [(i, i ^ distance) for i in range(size)])


def pack_kernel(outer, kv_ref, mask_ref, x_ref, send_ref, *outs):
    me = lax.axis_index("seq")
    z, y = me // QUAD, (me // 2) % 2
    keys = kv_ref.shape[1]
    rows = mask_ref.shape[0]
    pieces = [x_ref[:, at : at + HEAD_DIM] for at in range(0, x_ref.shape[1], HEAD_DIM)]
    lane = lax.broadcasted_iota(jnp.int32, (rows, HEAD_DIM), 1)
    mask = jnp.zeros((rows, HEAD_DIM), f32)
    for head in range(mask_ref.shape[1]):
        live = (mask_ref[:, head : head + 1] == 1).astype(f32)
        mask = jnp.where(lane == head, jnp.broadcast_to(live, mask.shape), mask)
    pieces.append(mask.astype(bf16))
    for k in range(outer):
        peer = jnp.bitwise_xor(z, k)
        cols = pl.ds(pl.multiple_of((2 * peer + y) * HEAD_DIM, HEAD_DIM), HEAD_DIM)
        outs[k][0:keys, :] = kv_ref[0, :, cols]
        for i, piece in enumerate(pieces):
            outs[k][keys + i * rows : keys + (i + 1) * rows, :] = piece
        cols = pl.ds(pl.multiple_of((2 * peer + 1 - y) * HEAD_DIM, HEAD_DIM), HEAD_DIM)
        at = slice(k * HEAD_DIM, (k + 1) * HEAD_DIM)
        send_ref[0:keys, at] = kv_ref[0, :, cols]
        send_ref[keys : 2 * keys, at] = kv_ref[1, :, cols]


def unpack_kernel(keys, *refs):
    line_ref = refs[-1]
    rows = line_ref.shape[0]
    at = 0
    for ref in refs[:-1]:
        for i in range((ref.shape[0] - keys) // rows):
            line_ref[:, at : at + HEAD_DIM] = ref[keys + i * rows : keys + (i + 1) * rows, :]
            at += HEAD_DIM


def z_distance(slot, core):
    return jnp.where(core == 0, Z_ORDER[0][slot], Z_ORDER[1][slot])


def route_kernel(outer, kv_ref, other_ref, *outs):
    me = lax.axis_index("seq")
    z, y = me // QUAD, (me // 2) % 2
    keys = kv_ref.shape[1]
    for slot, out in enumerate(outs):
        k = z_distance(slot, me % 2)
        head = 2 * jnp.bitwise_xor(z, k) + y
        cols = pl.ds(pl.multiple_of(head * HEAD_DIM, HEAD_DIM), HEAD_DIM)
        out[0:keys, :] = kv_ref[1, :, cols]
        out[keys:, :] = other_ref[:, pl.ds(pl.multiple_of(k * HEAD_DIM, HEAD_DIM), HEAD_DIM)]


def cache_kernel(outer, keys, *refs):
    firsts, rests, out_ref = refs[:outer], refs[outer : 2 * outer], refs[2 * outer]
    core = lax.axis_index("seq") % 2
    for i in range(outer):
        at = 4 * i * keys
        for at_core in range(2):

            @pl.when(core == at_core)
            def _():
                out_ref[at : at + keys, :] = firsts[Z_ORDER[at_core][i]][0:keys, :]

        out_ref[at + keys : at + 4 * keys, :] = rests[i][...]


def stack_kernel(axis, *refs):
    at = 0
    for ref in refs[:-1]:
        size = ref.shape[axis]
        if axis == 0:
            refs[-1][at : at + size, :] = ref[...]
        else:
            refs[-1][:, at : at + size] = ref[...]
        at += size


def stacked(parts, axis, beside=()):
    shape = list(parts[0].shape)
    shape[axis] = sum(p.shape[axis] for p in parts)
    return call(functools.partial(stack_kernel, axis), like(tuple(shape), parts[0].dtype), parts, beside)


def normed_chunks(wide, chunks, gain_ref):
    squares = None
    for source, load in chunks:
        v = load().astype(f32)
        s = jnp.sum(v * v, axis=1, keepdims=True)
        squares = s if squares is None else squares + s
    inverse = lax.rsqrt(squares / (len(chunks) * wide) + eps)
    for source, load in chunks:
        at = pl.ds(pl.multiple_of(source * wide, wide), wide)
        yield at, (load().astype(f32) * inverse * gain_ref[:, at].astype(f32)).astype(bf16)


def to_members(parts):
    size = lax.axis_size("seq")
    groups = [list(range(core, size, 2)) for core in range(2)]
    return lax.all_to_all(parts, "seq", 0, 0, axis_index_groups=groups, tiled=True)


def member(i, other):
    core = lax.axis_index("seq") % 2
    return 2 * i + (1 - core if other else core)


def line_of(outer, *nears):
    return [QUAD * k + j for j in nears for k in range(outer)]


def line_chunks(outer, wide, refs):
    me = lax.axis_index("seq")
    lines = [line_of(outer, near) for near in range(QUAD)]
    step = wide + HEAD_DIM
    return [
        (jnp.bitwise_xor(me, distance), lambda r=ref, i=i: r[:, i * step : i * step + wide])
        for ref, line in zip(refs, lines)
        for i, distance in enumerate(line)
    ]


def line_mask(wide, ref, i):
    at = pl.multiple_of(i * (wide + HEAD_DIM) + wide, HEAD_DIM)
    tile = ref[:, pl.ds(at, HEAD_DIM)].astype(f32)
    lane = lax.broadcasted_iota(jnp.int32, tile.shape, 1)
    mine = jnp.where(lane == lax.axis_index("seq") // 2, tile, 0.0)
    return jnp.broadcast_to(jnp.sum(mine, axis=1, keepdims=True), tile.shape)


def in_line(near, z):
    return QUAD * z + jnp.bitwise_xor(lax.axis_index("seq") % QUAD, near)


def z_line_chunks(wide, refs):
    return [
        (in_line(near, z), lambda r=ref, z=z: r[:, z * wide : (z + 1) * wide])
        for near, ref in enumerate(refs)
        for z in range(ref.shape[1] // wide)
    ]


def query_kernel(outer, wide, *refs):
    gain_ref, w_ref, out_ref = refs[QUAD:]
    total = None
    for at, chunk in normed_chunks(wide, line_chunks(outer, wide, refs[:QUAD]), gain_ref):
        term = jnp.dot(chunk, w_ref[at, :], preferred_element_type=f32)
        total = term if total is None else total + term
    out_ref[...] = total.astype(bf16)


def scatter_dot(wide, other, left, w_ref, out_ref):
    for i in range(out_ref.shape[0]):
        at = pl.ds(pl.multiple_of(member(i, other) * wide, wide), wide)
        out_ref[i] = jnp.dot(left, w_ref[:, at], preferred_element_type=f32)


def line_dot(wide, nears, left, w_ref, out_ref):
    outer = out_ref.shape[1] // (len(nears) * wide)
    for i, near in enumerate(nears):
        for z in range(outer):
            at = pl.ds(pl.multiple_of(in_line(near, z) * wide, wide), wide)
            to = (i * outer + z) * wide
            out_ref[:, to : to + wide] = jnp.dot(left, w_ref[:, at], preferred_element_type=f32)


def keep_kernel(wide, left_ref, w_ref, out_ref):
    scatter_dot(wide, False, left_ref[...], w_ref, out_ref)


def line_kernel(wide, near, left_ref, w_ref, out_ref):
    line_dot(wide, (near,), left_ref[...], w_ref, out_ref)


def span_states(q_ref, cache_ref, masks):
    heads = q_ref.shape[1] // HEAD_DIM
    scale = 1.0 / HEAD_DIM**0.5
    keys = cache_ref.shape[0] // (2 * len(masks))
    queries = jnp.concatenate(
        [q_ref[:, h * HEAD_DIM : (h + 1) * HEAD_DIM] for h in range(heads)], axis=0
    )
    scores = [
        lax.dot_general(
            queries,
            cache_ref[2 * i * keys : (2 * i + 1) * keys, :],
            (((1,), (1,)), ((), ())),
            preferred_element_type=f32,
        )
        * scale
        for i in range(len(masks))
    ]
    lives = [jnp.concatenate([mask] * heads, axis=0) > 0.5 for mask in masks]
    scores = [jnp.where(live, score, floor_score) for live, score in zip(lives, scores)]
    tops = [jnp.max(score, axis=1, keepdims=True) for score in scores]
    weights = [
        jnp.where(live, jnp.exp(score - top), 0.0) for live, score, top in zip(lives, scores, tops)
    ]
    totals = [jnp.sum(weight, axis=1, keepdims=True) for weight in weights]
    accums = [
        jnp.dot(
            weight.astype(bf16),
            cache_ref[(2 * i + 1) * keys : (2 * i + 2) * keys, :],
            preferred_element_type=f32,
        )
        for i, weight in enumerate(weights)
    ]
    return list(zip(tops, totals, accums))


def combined(states):
    top = functools.reduce(jnp.maximum, [s[0] for s in states])
    total = accum = None
    for t, s, a in states:
        factor = jnp.exp(t - top)
        total = s * factor if total is None else total + s * factor
        accum = a * factor if accum is None else accum + a * factor
    return top, total, accum


def early_kernel(outer, wide, q_ref, cache_ref, line_ref, other_ref, top_ref, total_ref, accum_ref):
    core = lax.axis_index("seq") % 2
    masks = [
        line_mask(wide, ref, z_distance(slot, core))
        for slot in range(outer)
        for ref in (line_ref, other_ref)
    ]
    top, total, accum_ref[...] = combined(span_states(q_ref, cache_ref, masks))
    top_ref[...] = jnp.broadcast_to(top, top_ref.shape)
    total_ref[...] = jnp.broadcast_to(total, total_ref.shape)


def attend_kernel(
    outer, wide, q_ref, top_ref, total_ref, accum_ref, cache_ref, core_ref, far_ref, w_ref, left_ref, send_ref
):
    rows = q_ref.shape[0]
    heads = q_ref.shape[1] // HEAD_DIM
    core = 1 - lax.axis_index("seq") % 2
    masks = [
        line_mask(wide, ref, z_distance(slot, core))
        for slot in range(outer)
        for ref in (core_ref, far_ref)
    ]
    states = span_states(q_ref, cache_ref, masks)
    states.append((top_ref[:, 0:1], total_ref[:, 0:1], accum_ref[...]))
    _, total, accum = combined(states)
    attended = (accum / total).astype(bf16)
    attended = jnp.concatenate([attended[h * rows : (h + 1) * rows] for h in range(heads)], axis=1)
    left_ref[...] = attended
    line_dot(wide, (3,), attended, w_ref, send_ref)


def hidden_kernel(wide, *refs):
    gain_ref, gate_ref, up_ref, down_ref, left_ref, send_ref = refs[QUAD:]
    gate = up = None
    for at, chunk in normed_chunks(wide, z_line_chunks(wide, refs[:QUAD]), gain_ref):
        g = jnp.dot(chunk, gate_ref[at, :], preferred_element_type=f32)
        u = jnp.dot(chunk, up_ref[at, :], preferred_element_type=f32)
        gate = g if gate is None else gate + g
        up = u if up is None else up + u
    hidden = (gate / (1.0 + jnp.exp(-gate)) * up).astype(bf16)
    left_ref[...] = hidden
    scatter_dot(wide, True, hidden, down_ref, send_ref)


def add_kernel(own_ref, recv_ref, out_ref):
    out_ref[...] = (own_ref[...] + recv_ref[...]).astype(out_ref.dtype)


def coded(out_ref, sums):
    rows, wide = sums.shape
    largest = jnp.max(jnp.abs(sums), axis=1, keepdims=True)
    level = jnp.ceil(jnp.log(jnp.maximum(largest, 1e-30)) * STEPS)
    scale = jnp.exp(level * (-1.0 / STEPS)) * RANGE
    out_ref[:, 0:wide] = jnp.round(sums * scale).astype(jnp.int32).astype(jnp.int16)
    level = jnp.broadcast_to(level, (rows, HEAD_DIM)).astype(jnp.int32)
    out_ref[:, wide:] = level.astype(jnp.int16)


def decoded(ref):
    wide = ref.shape[1] - HEAD_DIM
    level = ref[:, wide:].astype(jnp.int32).astype(f32)[:, 0:1]
    scale = jnp.exp(level * (1.0 / STEPS)) * (1.0 / RANGE)
    return ref[:, 0:wide].astype(jnp.int32).astype(f32) * scale


def chip_kernel(own_ref, core_ref, out_ref):
    coded(out_ref, own_ref[...] + core_ref[...])


def pair_kernel(own_ref, core_ref, y_ref, out_ref):
    coded(out_ref, own_ref[...] + core_ref[...] + decoded(y_ref))


def stream_kernel(wide, x_ref, *refs):
    parts, (line_ref, own_ref) = refs[:-2], refs[-2:]
    z = lax.axis_index("seq") // QUAD
    sums = [decoded(part) for part in parts]
    while len(sums) > 1:
        sums = [first + second for first, second in zip(sums[0::2], sums[1::2])]
    for to in range(len(parts)):
        at = pl.multiple_of(jnp.bitwise_xor(z, to) * (wide + HEAD_DIM), HEAD_DIM)
        cols = slice(to * wide, (to + 1) * wide)
        line_ref[:, cols] = (x_ref[:, pl.ds(at, wide)].astype(f32) + sums[0][:, cols]).astype(bf16)
    own_ref[...] = line_ref[:, pl.ds(pl.multiple_of(z * wide, wide), wide)]


def final_kernel(base_ref, parts_ref, out_ref):
    total = parts_ref[0].astype(f32)
    for i in range(1, parts_ref.shape[0]):
        total = total + parts_ref[i].astype(f32)
    out_ref[...] = (base_ref[...].astype(f32) + total).astype(bf16)


def z_swapped(parts):
    arrived = [swap(part, QUAD * k) for k, part in reversed(list(enumerate(parts))) if k > 0]
    return [parts[0], *reversed(arrived)]


def z_routed(parts):
    size = lax.axis_size("seq")
    return [parts[0]] + [
        lax.ppermute(part, "seq", [(i, i ^ QUAD * Z_ORDER[i % 2][slot]) for i in range(size)])
        for slot, part in list(enumerate(parts))[1:]
    ]


def near_gathered(line):
    y = swap(line, 2)
    core, far = swap(line, 1), swap(y, 1)
    return [line, core, y, far]


def far_gathered(line):
    far = swap(line, 3)
    core, y = swap(line, 1), swap(far, 1)
    return [line, core, y, far]


def updated(x_line, send, left, weight, wide, beside):
    rows, half = send.shape
    line = like((rows, half), f32)
    code = like((rows, half + HEAD_DIM), jnp.int16)
    far = swap(send, 1)
    second = call(functools.partial(line_kernel, wide, 2), line, [left, weight])
    second = call(chip_kernel, code, [second, far])
    arrived = swap(second, 2)
    core = swap(call(functools.partial(line_kernel, wide, 1), line, [left, weight]), 1)
    own = call(functools.partial(line_kernel, wide, 0), line, [left, weight], [second])
    sums = call(pair_kernel, code, [own, core, arrived], beside * 2)
    return call(
        functools.partial(stream_kernel, wide),
        [like((rows, half), bf16), like((rows, wide), bf16)],
        [x_line, *z_routed([sums] * (half // wide))],
    )


def scattered(base, send, left, weight, wide):
    far = swap(send, 1)
    own = call(functools.partial(keep_kernel, wide), like(send.shape, f32), [left, weight])
    sums = call(add_kernel, like(send.shape, bf16), [own, far])
    return call(final_kernel, like(base.shape, bf16), [base, to_members(sums)])


def local_pairs(
    x_rows, attn_gain, q_weight, o_weight, mlp_gain, gate_weight, up_weight, down_weight, kv_cache, block_mask
):
    rows, wide = x_rows.shape
    outer = lax.axis_size("seq") // QUAD
    columns = q_weight.shape[1]
    beside = [room(18432)]
    attn_gain = attn_gain.reshape(1, -1)
    mlp_gain = mlp_gain.reshape(1, -1)
    members = lax.axis_size("seq") // 2
    partial_sums = like((members, rows, wide), f32)

    keys = kv_cache.shape[1]
    step = wide + HEAD_DIM
    send, *firsts = call(
        functools.partial(pack_kernel, outer),
        [like((2 * keys, outer * HEAD_DIM), bf16)]
        + [like((keys + step // HEAD_DIM * rows, HEAD_DIM), bf16)] * outer,
        [kv_cache, block_mask[:, :, 0], x_rows],
        beside,
    )
    other = swap(send, 2)
    firsts = z_swapped(firsts)
    line = call(functools.partial(unpack_kernel, keys), like((rows, outer * step), bf16), firsts)
    routed = call(
        functools.partial(route_kernel, outer),
        [like((3 * keys, HEAD_DIM), bf16)] * outer,
        [kv_cache, other],
        [line, *beside],
    )
    routed = z_routed(routed)
    x_parts = near_gathered(line)
    queries = call(
        functools.partial(query_kernel, outer, wide),
        like((rows, columns), bf16),
        [*x_parts, attn_gain, q_weight],
    )
    cache = call(
        functools.partial(cache_kernel, outer, keys),
        like((4 * outer * keys, HEAD_DIM), bf16),
        [*firsts, *routed],
        [queries],
    )
    far_cache = swap(cache, 1)
    tall = like((columns // HEAD_DIM * rows, HEAD_DIM), f32)
    early = call(
        functools.partial(early_kernel, outer, wide), [tall] * 3, [queries, cache, *x_parts[0::2]]
    )
    left, send = call(
        functools.partial(attend_kernel, outer, wide),
        [like((rows, columns), bf16), like((rows, outer * wide), f32)],
        [queries, *early, far_cache, *x_parts[1::2], o_weight],
    )
    line, stream = updated(x_parts[0], send, left, o_weight, wide, beside)
    left, send = call(
        functools.partial(hidden_kernel, wide),
        [like((rows, gate_weight.shape[1]), bf16), partial_sums],
        [*far_gathered(line), mlp_gain, gate_weight, up_weight, down_weight],
    )
    return scattered(stream, send, left, down_weight, wide)


def rms_norm(values, gain):
    wide = values.astype(f32)
    inverse = lax.rsqrt(jnp.mean(wide * wide, axis=-1, keepdims=True) + eps)
    return (wide * inverse * gain.astype(f32)).astype(bf16)


def combine_states(first, second):
    top_a, total_a, accum_a = first
    top_b, total_b, accum_b = second
    top = jnp.maximum(top_a, top_b)
    factor_a = jnp.exp(top_a - top)
    factor_b = jnp.exp(top_b - top)
    return (
        top,
        total_a * factor_a + total_b * factor_b,
        accum_a * factor_a[..., None] + accum_b * factor_b[..., None],
    )


def combined_all(x, axis, combine):
    everything = jax.tree.map(lambda part: lax.all_gather(part, axis), x)
    initial = jax.tree.map(lambda part: part[0], everything)

    def turn(k, so_far):
        return combine(so_far, jax.tree.map(lambda part: part[k], everything))

    return lax.fori_loop(1, lax.axis_size(axis), turn, initial)


def summed(weight, left):
    product = lax.dot_general(weight, left, (((0,), (1,)), ((), ())), preferred_element_type=f32)
    return lax.psum_scatter(product, "seq", scatter_dimension=0, tiled=True).T


def local_tokens(
    x_rows, attn_gain, q_weight, o_weight, mlp_gain, gate_weight, up_weight, down_weight, kv_cache, block_mask
):
    rows = x_rows.shape[0]
    group = HEADS // KV_HEADS
    key_len = kv_cache.shape[1]
    spans = key_len // BLOCK
    scale = 1.0 / HEAD_DIM**0.5
    normed = rms_norm(lax.all_gather(x_rows, "seq", axis=1, tiled=True), attn_gain)
    query_part = jnp.dot(normed, q_weight, preferred_element_type=f32).astype(bf16)
    queries = lax.all_gather(query_part, "seq", axis=1, tiled=True)

    def one_group(index):
        def cut(array, width):
            return lax.dynamic_slice_in_dim(array, index * width, width, 1)

        query_group = cut(queries, group * HEAD_DIM).reshape(rows, group, HEAD_DIM)
        scores = (
            jnp.einsum("rhd,kd->rhk", query_group, cut(kv_cache[0], HEAD_DIM), preferred_element_type=f32)
            * scale
        )
        scores = scores.reshape(rows, group, spans, BLOCK)
        live = (cut(block_mask, 1)[:, 0, :] == 1)[:, None, :, None]
        masked = jnp.where(live, scores, floor_score)
        top = jnp.max(masked, axis=(2, 3))
        weights = jnp.where(live, jnp.exp(masked - top[..., None, None]), 0.0)
        rounded = weights.astype(bf16).reshape(rows, group, key_len)
        accum = jnp.einsum("rhk,kd->rhd", rounded, cut(kv_cache[1], HEAD_DIM), preferred_element_type=f32)
        return (top, jnp.sum(weights, axis=(2, 3)), accum)

    states = lax.map(one_group, jnp.arange(KV_HEADS, dtype=jnp.int32))
    states = jax.tree.map(lambda part: jnp.moveaxis(part, 0, 1), states)
    columns = q_weight.shape[1]
    top, total, accum = combined_all(states, "seq", combine_states)
    attended = (accum / total[..., None]).reshape(rows, HEADS * HEAD_DIM).astype(bf16)
    attn_cols = lax.dynamic_slice_in_dim(attended, lax.axis_index("seq") * columns, columns, 1)
    stream = (x_rows.astype(f32) + summed(o_weight, attn_cols)).astype(bf16)
    normed_two = rms_norm(lax.all_gather(stream, "seq", axis=1, tiled=True), mlp_gain)
    gate = jnp.dot(normed_two, gate_weight, preferred_element_type=f32)
    upward = jnp.dot(normed_two, up_weight, preferred_element_type=f32)
    hidden = (jax.nn.silu(gate) * upward).astype(bf16)
    return (stream.astype(f32) + summed(down_weight, hidden)).astype(bf16)


def solution(mesh):
    pairs = mesh.shape["seq"] == 2 * KV_HEADS
    return jax.shard_map(
        local_pairs if pairs else local_tokens,
        mesh=mesh,
        in_specs=(
            P("group", "seq"),
            P(),
            P(None, "seq"),
            P("seq", None),
            P(),
            P(None, "seq"),
            P(None, "seq"),
            P("seq", None),
            P(None, ("group", "seq"), None),
            P("group", None, "seq"),
        ),
        out_specs=P("group", "seq"),
        check_vma=False,
    )
```
